128 devices in a mesh: dp: 16 (over x_lo, z, core), seq: 8 (over x_hi, y).
Axes of the slice: x: 4 (x_hi: 2, x_lo: 2; x = x_hi * 2 + x_lo), y: 4, z: 4, core: 2. Of those that a mesh axis runs over, the one named last changes fastest.
Arguments:
- hidden_acts: bfloat16 [65536, 14336], P(('dp', 'seq')), may hold values from -8 to 8
- out_grads: bfloat16 [65536, 8192], P(('dp', 'seq')), may hold values from -8 to 8
- val_acts: bfloat16 [512, 14336], P(('dp', 'seq')), may hold values from -6 to 6
- val_grads: bfloat16 [512, 8192], P(('dp', 'seq')), may hold values from -6 to 6
- val_ids: int32 [512], P(('dp', 'seq')), may hold values from 0 to 3, never falling along the last dimension, each value on 1 to 256 neighbouring positions
Outputs:
- token_scores: float32 [4, 65536], P(None, ('dp', 'seq'))
- block_gram: float32 [512, 4], P(('dp', 'seq'))
The draws below stay inside these ranges and needn't reach their ends.
Inputs may be any that keep to these rules, and one draw needn't show every extreme that they name: val_ids never fall along the array; each of the 4 validation sequences has 1 to 256 tokens, and one has exactly 256.
All inputs are finite; a program needn't handle non-finite values.
Results may differ from the reference program's by a relative error of at most 0.0003.
Values may be sent and summed in bfloat16 or wider, within the bound.
No kernel may reach another device: no remote copies, remote signals or barrier semaphores. Data moves between devices by JAX's collectives and lax.ppermute only.
A program may use at most 128 MiB of HBM per device.

```python
import math
import jax
import jax.numpy as jnp
import numpy as np
from jax import lax

D = 8192
FF = 14336
TOK_DEV = 512
BLK = 128
NVAL = 4
TOKENS = 65536
VAL_TOKENS = 512


def token_rows(key, width):
    key_jitter = jax.random.fold_in(key, 0)
    jitter = jnp.clip(jax.random.normal(key_jitter, (TOKENS, width), jnp.float32), -4.0, 4.0)
    return jitter.astype(jnp.bfloat16)


def draw_hidden_acts(key, part):
    key = jax.random.fold_in(key, 11)
    return token_rows(key, FF)


def draw_out_grads(key, part):
    key = jax.random.fold_in(key, 12)
    return token_rows(key, D)


def block_scale(rng, extent, shards, low, high):
    factor_of = 1.0
    for dim, parts in shards:
        draws = jax.random.uniform(jax.random.fold_in(jax.random.fold_in(rng, 6), dim), (parts,), jnp.float32, low / len(shards), high / len(shards))
        factor_of = factor_of * jnp.repeat(jnp.exp(draws), extent[dim] // parts).reshape((-1,) + (1,) * (len(extent) - 1 - dim))
    return factor_of


def profile(number_of, total, reach, slope):
    weights = [(1 << 20) // math.isqrt(grade ** slope) + 1 for grade in range(2, number_of + 1)]
    surplus, holding = total - reach - (number_of - 1), [1] * (number_of - 1)
    while surplus > 0:
        movable = [i for i in range(number_of - 1) if holding[i] < reach]
        pool, left = sum([weights[i] for i in movable]), surplus
        for i in movable:
            addition = min(reach - holding[i], max(1, left * weights[i] // pool), surplus)
            holding[i] = holding[i] + addition
            surplus = surplus - addition
    return np.array([reach] + holding)


def uneven(key, number_of, total, limit, slope):
    if number_of == 2:
        one = jax.random.randint(key, (), max(1, total - limit), min(limit, total - 1) + 1)
        return jnp.stack([one, total - one])
    lengths = jnp.asarray(profile(number_of, total, limit, slope), jnp.int32)
    twos = (number_of - 1) // 2
    giver, taker = lengths[1:1 + 2 * twos:2], lengths[2:2 + 2 * twos:2]
    slack = jnp.minimum(giver - 1, limit - taker)
    moved = jax.random.randint(jax.random.fold_in(key, 1), (twos,), 0, 1 << 20) % (slack + 1)
    lengths = lengths.at[1:1 + 2 * twos:2].set(giver - moved).at[2:2 + 2 * twos:2].set(taker + moved)
    return lengths[jax.random.permutation(jax.random.fold_in(key, 2), number_of)]


def centred(stream_key, dims, scale, bound, pieces=(), kind=jnp.bfloat16):
    entries = scale * jax.random.normal(stream_key, dims, jnp.float32)
    if pieces:
        entries = entries * block_scale(stream_key, dims, pieces, -0.22, 0.18)
    return jnp.clip(entries, -bound, bound).astype(kind)


def setup_inputs(seed: int = 0) -> dict:
    streams_of = jax.random.split(jax.random.key(seed), 6)
    hidden_acts = draw_hidden_acts(jax.random.fold_in(streams_of[5], 71), 0)
    out_grads = draw_out_grads(jax.random.fold_in(streams_of[5], 71), 0)
    val_acts = centred(streams_of[2], (VAL_TOKENS, FF), 1.0, 6.0, ((0, 128),))
    val_grads = centred(streams_of[3], (VAL_TOKENS, D), 1.0, 6.0, ((0, 128),))
    val_ids = jnp.searchsorted(jnp.cumsum(uneven(streams_of[4], NVAL, VAL_TOKENS, VAL_TOKENS // 2, 2)), jnp.arange(VAL_TOKENS), side="right").astype(jnp.int32)
    return dict(hidden_acts=hidden_acts, out_grads=out_grads, val_acts=val_acts, val_grads=val_grads, val_ids=val_ids)


def reference(hidden_acts, out_grads, val_acts, val_grads, val_ids):
    labels = jnp.arange(NVAL, dtype=jnp.int32)
    onehot = (val_ids[:, None] == labels[None, :]).astype(jnp.float32)
    val_kernel = jnp.dot(val_acts, val_acts.T, preferred_element_type=jnp.float32) * jnp.dot(val_grads, val_grads.T, preferred_element_type=jnp.float32)
    val_norm = jnp.einsum('sv,sp,pv->v', onehot, val_kernel, onehot, precision=lax.Precision.HIGHEST)
    inv_norm = lax.rsqrt(val_norm + 1e-06)
    pack_count = TOKENS // TOK_DEV
    block_count = TOK_DEV // BLK
    divisor = float(BLK) * math.sqrt(float(FF) * float(D))
    packed_acts = hidden_acts.reshape(pack_count, TOK_DEV, FF)
    packed_grads = out_grads.reshape(pack_count, TOK_DEV, D)

    def per_pack(pair):
        pack_acts, pack_grads = pair
        cross = jnp.dot(pack_acts, val_acts.T, preferred_element_type=jnp.float32) * jnp.dot(pack_grads, val_grads.T, preferred_element_type=jnp.float32)
        scores_raw = jnp.einsum('tp,pv->vt', cross, onehot, precision=lax.Precision.HIGHEST)
        self_kernel = jnp.dot(pack_acts, pack_acts.T, preferred_element_type=jnp.float32) * jnp.dot(pack_grads, pack_grads.T, preferred_element_type=jnp.float32)
        blocks = self_kernel.reshape(block_count, BLK, block_count, BLK).sum(axis=(1, 3)) / divisor
        return (scores_raw * inv_norm[:, None], jnp.tril(blocks, -1))
    scores, gram_tiles = lax.map(per_pack, (packed_acts, packed_grads))
    token_scores = jnp.transpose(scores, (1, 0, 2)).reshape(NVAL, TOKENS)
    block_gram = gram_tiles.reshape(pack_count * block_count, block_count)
    return (token_scores, block_gram)
```

```python
import functools
import math

import jax
import jax.numpy as jnp
from jax import lax
from jax.experimental import pallas as pl
from jax.experimental.pallas import tpu as pltpu
from jax.sharding import PartitionSpec as P

D = 8192
FF = 14336
BLK = 128
NVAL = 4
TOK = 512
VAL = 512
AXES = ("dp", "seq")
HA = FF // 2
HG = D // 2
C1 = 3840
C2A = HA - C1
C2G = 512
C2 = C2A + C2G
C3G = HG - C2G
IDW = 128
C3 = C3G + IDW
MASKS = ((1, 3), (3, 1))


def coords(i):
    dp, seq = divmod(i, 8)
    c = dp % 2
    z = (dp // 2) % 4
    x = (seq // 4) * 2 + dp // 8
    return {"x": x, "y": seq % 4, "z": z, "c": c}


def index(p):
    dp = ((p["x"] % 2) * 4 + p["z"]) * 2 + p["c"]
    return dp * 8 + (p["x"] // 2) * 4 + p["y"]


def ring_pairs(axis, step):
    pairs = []
    for i in range(128):
        p = coords(i)
        p[axis] ^= MASKS[p["c"]][step]
        pairs.append((i, index(p)))
    return pairs


def core_pairs():
    pairs = []
    for i in range(128):
        p = coords(i)
        p["c"] ^= 1
        pairs.append((i, index(p)))
    return pairs


def swap(x):
    return lax.ppermute(x, AXES, core_pairs())


def hop(x, axis, step):
    return lax.ppermute(x, AXES, ring_pairs(axis, step))


def grow(x, axis, dim, first):
    a1 = hop(x, axis, 0)
    b = hop(jnp.stack([x, a1]), axis, 1)
    return jnp.stack(
        [x, jnp.where(first, a1, b[0]), jnp.where(first, b[0], a1), b[1]], axis=dim
    )


def nt(a, b):
    return lax.dot_general(a, b, (((1,), (1,)), ((), ())), preferred_element_type=jnp.float32)


def self_body(acts_ref, grads_ref, out_ref, sa, sg, *, na, ng):
    i = pl.program_id(0)

    @pl.when(i == 0)
    def _():
        sa[...] = jnp.zeros_like(sa)
        sg[...] = jnp.zeros_like(sg)

    def add(acc, ref):
        acc[0:256, :] += nt(ref[256:512, :], ref[0:256, :])
        acc[256:384, 0:128] += nt(ref[128:256, :], ref[0:128, :])
        acc[384:512, 0:128] += nt(ref[384:512, :], ref[256:384, :])

    @pl.when(i < na)
    def _():
        add(sa, acts_ref)

    @pl.when(i >= na)
    def _():
        add(sg, grads_ref)

    @pl.when(i == na + ng - 1)
    def _():
        k = sa[...] * sg[...]
        rows = lax.broadcasted_iota(jnp.int32, (4, 4), 0)
        cols = lax.broadcasted_iota(jnp.int32, (4, 4), 1)
        out = jnp.zeros((4, 4), jnp.float32)
        spots = (
            (2, 0, 0, 0), (2, 1, 0, 128), (3, 0, 128, 0), (3, 1, 128, 128),
            (1, 0, 256, 0), (3, 2, 384, 0),
        )
        for b, c, r0, c0 in spots:
            s = jnp.sum(k[r0:r0 + 128, c0:c0 + 128])
            out = jnp.where((rows == b) & (cols == c), s, out)
        out_ref[...] = out / (float(BLK) * math.sqrt(float(FF) * float(D)))


def self_gram(acts, grads):
    kc = 2048
    na, ng = FF // kc, D // kc
    return pl.pallas_call(
        functools.partial(self_body, na=na, ng=ng),
        grid=(na + ng,),
        in_specs=[
            pl.BlockSpec((TOK, kc), lambda i: (0, jnp.minimum(i, na - 1))),
            pl.BlockSpec((TOK, kc), lambda i: (0, jnp.maximum(i - na, 0))),
        ],
        out_specs=pl.BlockSpec((4, 4), lambda i: (0, 0)),
        out_shape=jax.ShapeDtypeStruct((4, 4), jnp.float32),
        scratch_shapes=[pltpu.VMEM((512, 256), jnp.float32)] * 2,
        compiler_params=pltpu.CompilerParams(vmem_limit_bytes=24 << 20),
        cost_estimate=pl.CostEstimate(
            flops=2 * 512 * 256 * (FF + D), bytes_accessed=2 * TOK * (FF + D), transcendentals=0
        ),
    )(acts, grads)


def cross_body(core_ref, acts, grads, *refs):
    pieces = refs[:24]
    raw_ref, norm_ref = refs[24:26]
    v1, v2, v3, h1, h2, h3, ca, cg, ka, kg, ids, sems = refs[26:]
    c = core_ref[0]
    vbufs = (v1, v2, v3)
    hbufs = (h1, h2, h3)

    def slots(half):
        o = c if half == 0 else 1 - c
        return (0, 1 + o, 2 - o, 3)

    def copies(half, part):
        out = []
        ss = slots(half)
        for k in range(4):
            src = pieces[half * 12 + part * 4 + k]
            if part == 0:
                dst = vbufs[0].at[half, ss[k]]
            elif part == 1:
                dst = vbufs[1].at[half, :, ss[k]]
            else:
                dst = vbufs[2].at[half, :, :, ss[k]]
            out.append((src, dst))
        o = c if half == 0 else 1 - c
        a0 = pl.multiple_of(o * HA, 128)
        g0 = pl.multiple_of(o * HG, 128)
        if part == 0:
            out.append((acts.at[:, pl.ds(a0, C1)], hbufs[0].at[half]))
        elif part == 1:
            out.append((acts.at[:, pl.ds(a0 + C1, C2A)], hbufs[1].at[half, :, pl.ds(0, C2A)]))
            out.append((grads.at[:, pl.ds(g0, C2G)], hbufs[1].at[half, :, pl.ds(C2A, C2G)]))
        else:
            out.append((grads.at[:, pl.ds(g0 + C2G, C3G)], hbufs[2].at[half]))
        return [
            pltpu.make_async_copy(s, d, sems.at[half, part, n]) for n, (s, d) in enumerate(out)
        ]

    order = [(half, part) for half in range(2) for part in range(3)]
    for half, part in order:
        for cp in copies(half, part):
            cp.start()
    seen = set()
    for half, part in order:
        for cp in copies(half, part):
            cp.wait()
        v = vbufs[part]
        width = (C1, C2, C3)[part]
        rows = v[half].reshape(VAL, width)
        mine = v[half, pl.ds(2 * c, 2)].reshape(VAL // 2, width)
        if part == 0:
            segments = ((ca, ka, 0, C1),)
        elif part == 1:
            segments = ((ca, ka, 0, C2A), (cg, kg, C2A, C2G))
        else:
            segments = ((cg, kg, 0, C3G),)
        for cross, kern, at, n in segments:
            r = rows[:, at:at + n]
            x = nt(r, hbufs[part][half, :, at:at + n])
            y = nt(mine[:, at:at + n], r)
            name = "a" if cross is ca else "g"
            if name in seen:
                cross[...] += x
                kern[...] += y
            else:
                cross[...] = x
                kern[...] = y
                seen.add(name)
        if half == 0 and part == 2:
            ids[...] = rows[:, C3G:].astype(jnp.float32)

    cross = ca[...] * cg[...]
    kern = ka[...] * kg[...]
    row_ids = jnp.transpose(ids[...])[0:1, :]
    half_ids = ids[pl.ds(pl.multiple_of(c * 256, 256), 256), :]
    for v in range(NVAL):
        keep = jnp.where(ids[...] == float(v), 1.0, 0.0)
        keep = jnp.concatenate([keep] * 4, axis=1)
        raw_ref[v:v + 1, :] = jnp.sum(cross * keep, axis=0, keepdims=True)
        keep = jnp.where(half_ids == float(v), 1.0, 0.0)
        keep = jnp.concatenate([keep] * 4, axis=1)
        part = jnp.sum(kern * keep, axis=0, keepdims=True)
        part = jnp.sum(jnp.where(row_ids == float(v), part, 0.0))
        norm_ref[v:v + 1, :] = jnp.full((1, 128), part, jnp.float32)


def cross_scores(core, acts, grads, pieces):
    anyspec = pl.BlockSpec(memory_space=pl.ANY)
    return pl.pallas_call(
        cross_body,
        in_specs=[pl.BlockSpec(memory_space=pltpu.SMEM)] + [anyspec] * (2 + len(pieces)),
        out_specs=[pl.BlockSpec(memory_space=pltpu.VMEM)] * 2,
        out_shape=[
            jax.ShapeDtypeStruct((NVAL, TOK), jnp.float32),
            jax.ShapeDtypeStruct((NVAL, 128), jnp.float32),
        ],
        scratch_shapes=[
            pltpu.VMEM((2, 4, 4, 4, 8, C1), jnp.bfloat16),
            pltpu.VMEM((2, 4, 4, 4, 8, C2), jnp.bfloat16),
            pltpu.VMEM((2, 4, 4, 4, 8, C3), jnp.bfloat16),
            pltpu.VMEM((2, TOK, C1), jnp.bfloat16),
            pltpu.VMEM((2, TOK, C2), jnp.bfloat16),
            pltpu.VMEM((2, TOK, C3G), jnp.bfloat16),
            pltpu.VMEM((VAL, TOK), jnp.float32),
            pltpu.VMEM((VAL, TOK), jnp.float32),
            pltpu.VMEM((VAL // 2, VAL), jnp.float32),
            pltpu.VMEM((VAL // 2, VAL), jnp.float32),
            pltpu.VMEM((VAL, IDW), jnp.float32),
            pltpu.SemaphoreType.DMA((2, 3, 6)),
        ],
        compiler_params=pltpu.CompilerParams(vmem_limit_bytes=58 << 20),
        cost_estimate=pl.CostEstimate(
            flops=2 * 512 * 768 * (FF + D), bytes_accessed=4 * TOK * (FF + D), transcendentals=0
        ),
    )(core, acts, grads, *pieces)


def shards(hidden_acts, out_grads, val_acts, val_grads, val_ids):
    core = lax.axis_index("dp") % 2
    first = core == 0
    idcol = jnp.broadcast_to(val_ids[:, None].astype(jnp.bfloat16), (4, IDW))
    halves = [
        jnp.concatenate(
            [val_acts[:, h * HA:(h + 1) * HA], val_grads[:, h * HG:(h + 1) * HG], idcol], axis=1
        )
        for h in range(2)
    ]
    keep = jnp.where(first, halves[0], halves[1])
    got = swap(jnp.where(first, halves[1], halves[0]))
    rows = jnp.concatenate([jnp.where(first, keep, got), jnp.where(first, got, keep)], axis=0)
    parts = (rows[:, :C1], rows[:, C1:C1 + C2], rows[:, C1 + C2:])

    plans = (
        (("z", 0), ("y", 0), "x"),
        (("x", 0), ("z", 1), "y"),
        (("y", 0), ("x", 0), "z"),
    )
    grown = list(parts)
    for stage in range(2):
        for j, plan in enumerate(plans):
            axis, dim = plan[stage]
            grown[j] = grow(grown[j], axis, dim, first)
    own, other = [], []
    for j, plan in enumerate(plans):
        x = grown[j]
        a1 = hop(x, plan[2], 0)
        b0 = hop(x, plan[2], 1)
        b1 = hop(a1, plan[2], 1)
        own += [x, a1, b0, b1]
        other += [swap(x), swap(a1), swap(b0), swap(b1)]

    block_gram = self_gram(hidden_acts, out_grads)
    raw, norm = cross_scores(core.reshape(1).astype(jnp.int32), hidden_acts, out_grads, own + other)
    norm = norm + swap(norm)
    token_scores = raw * lax.rsqrt(norm[:, :1] + 1e-06)
    return (token_scores, block_gram)


def solution(mesh):
    return jax.shard_map(
        shards,
        mesh=mesh,
        in_specs=(
            P(AXES, None),
            P(AXES, None),
            P(AXES, None),
            P(AXES, None),
            P(AXES),
        ),
        out_specs=(P(None, AXES), P(AXES, None)),
        check_vma=False,
    )
```

```python
import functools
import math

import jax
import jax.numpy as jnp
from jax import lax
from jax.experimental import pallas as pl
from jax.experimental.pallas import tpu as pltpu
from jax.sharding import PartitionSpec as P

D = 8192
FF = 14336
BLK = 128
NVAL = 4
TOK = 512
VAL = 512
AXES = ("dp", "seq")
HA = FF // 2
HG = D // 2
C1 = 3840
C2A = HA - C1
C2G = 512
C2 = C2A + C2G
C3G = HG - C2G
IDW = 128
C3 = C3G + IDW
MASKS = ((1, 3), (3, 1))


def coords(i):
    dp, seq = divmod(i, 8)
    c = dp % 2
    z = (dp // 2) % 4
    x = (seq // 4) * 2 + dp // 8
    return {"x": x, "y": seq % 4, "z": z, "c": c}


def index(p):
    dp = ((p["x"] % 2) * 4 + p["z"]) * 2 + p["c"]
    return dp * 8 + (p["x"] // 2) * 4 + p["y"]


def ring_pairs(axis, step):
    pairs = []
    for i in range(128):
        p = coords(i)
        p[axis] ^= MASKS[p["c"]][step]
        pairs.append((i, index(p)))
    return pairs


def core_pairs():
    pairs = []
    for i in range(128):
        p = coords(i)
        p["c"] ^= 1
        pairs.append((i, index(p)))
    return pairs


def swap(x):
    return lax.ppermute(x, AXES, core_pairs())


def hop(x, axis, step):
    return lax.ppermute(x, AXES, ring_pairs(axis, step))


def double(x, axis, step):
    return jnp.stack([x, hop(x, axis, step)])


def gate(xs, dep):
    n = len(xs)
    anyspec = pl.BlockSpec(memory_space=pl.ANY)
    return pl.pallas_call(
        lambda *refs: None,
        in_specs=[anyspec] * (n + 1),
        out_specs=[anyspec] * n,
        out_shape=[jax.ShapeDtypeStruct(x.shape, x.dtype) for x in xs],
        input_output_aliases={i: i for i in range(n)},
        cost_estimate=pl.CostEstimate(flops=0, bytes_accessed=0, transcendentals=0),
    )(*xs, dep)


def nt(a, b):
    return lax.dot_general(a, b, (((1,), (1,)), ((), ())), preferred_element_type=jnp.float32)


def self_add(acc, ref):
    acc[0:256, :] += nt(ref[256:512, :], ref[0:256, :])
    acc[256:384, 0:128] += nt(ref[128:256, :], ref[0:128, :])
    acc[384:512, 0:128] += nt(ref[384:512, :], ref[256:384, :])


def self_acts_body(acts_ref, dep_ref, out_ref):
    @pl.when(pl.program_id(0) == 0)
    def _():
        out_ref[...] = jnp.zeros_like(out_ref)

    self_add(out_ref, acts_ref)


def self_grads_body(grads_ref, sa_ref, dep_ref, out_ref, sg, *, steps):
    i = pl.program_id(0)

    @pl.when(i == 0)
    def _():
        sg[...] = jnp.zeros_like(sg)

    self_add(sg, grads_ref)

    @pl.when(i == steps - 1)
    def _():
        k = sa_ref[...] * sg[...]
        rows = lax.broadcasted_iota(jnp.int32, (4, 4), 0)
        cols = lax.broadcasted_iota(jnp.int32, (4, 4), 1)
        out = jnp.zeros((4, 4), jnp.float32)
        spots = (
            (2, 0, 0, 0), (2, 1, 0, 128), (3, 0, 128, 0), (3, 1, 128, 128),
            (1, 0, 256, 0), (3, 2, 384, 0),
        )
        for b, c, r0, c0 in spots:
            s = jnp.sum(k[r0:r0 + 128, c0:c0 + 128])
            out = jnp.where((rows == b) & (cols == c), s, out)
        out_ref[...] = out / (float(BLK) * math.sqrt(float(FF) * float(D)))


KC = 2048


def self_acts(acts, dep):
    return pl.pallas_call(
        self_acts_body,
        grid=(FF // KC,),
        in_specs=[
            pl.BlockSpec((TOK, KC), lambda i: (0, i)),
            pl.BlockSpec(memory_space=pl.ANY),
        ],
        out_specs=pl.BlockSpec((512, 256), lambda i: (0, 0)),
        out_shape=jax.ShapeDtypeStruct((512, 256), jnp.float32),
        compiler_params=pltpu.CompilerParams(vmem_limit_bytes=16 << 20),
        cost_estimate=pl.CostEstimate(
            flops=2 * 512 * 256 * FF, bytes_accessed=2 * TOK * FF, transcendentals=0
        ),
    )(acts, dep)


def self_grads(grads, sa, dep):
    return pl.pallas_call(
        functools.partial(self_grads_body, steps=D // KC),
        grid=(D // KC,),
        in_specs=[
            pl.BlockSpec((TOK, KC), lambda i: (0, i)),
            pl.BlockSpec((512, 256), lambda i: (0, 0)),
            pl.BlockSpec(memory_space=pl.ANY),
        ],
        out_specs=pl.BlockSpec((4, 4), lambda i: (0, 0)),
        out_shape=jax.ShapeDtypeStruct((4, 4), jnp.float32),
        scratch_shapes=[pltpu.VMEM((512, 256), jnp.float32)],
        compiler_params=pltpu.CompilerParams(vmem_limit_bytes=16 << 20),
        cost_estimate=pl.CostEstimate(
            flops=2 * 512 * 256 * D, bytes_accessed=2 * TOK * D, transcendentals=0
        ),
    )(grads, sa, dep)


RUNS = ("y", "z", "x")
STEP5 = ("z", "x", "y")
STEP6 = ("x", "y", "z")
WEIGHT = {"x": 4, "y": 2, "z": 1}


def place(part, k, s4):
    n = s4 * WEIGHT[RUNS[part]]
    if k in (1, 3):
        n += WEIGHT[STEP5[part]]
    if k in (2, 3):
        n += WEIGHT[STEP6[part]]
    return n


WIDTHS = (C1, C2, C3)
STARTS = (0, C1, C1 + C2)
ALLW = C1 + C2 + C3
ORDER = tuple((half, part) for half in range(2) for part in range(3))
SEGMENTS = ((("a", 0, C1),), (("a", 0, C2A), ("g", C2A, C2G)), (("g", 0, C3G),))


def train_copies(acts, grads, o, part, dst):
    a0 = pl.multiple_of(o * HA, 128)
    g0 = pl.multiple_of(o * HG, 128)
    if part == 0:
        return [(acts.at[:, pl.ds(a0, C1)], dst.at[:, pl.ds(0, C1)])]
    if part == 1:
        return [
            (acts.at[:, pl.ds(a0 + C1, C2A)], dst.at[:, pl.ds(0, C2A)]),
            (grads.at[:, pl.ds(g0, C2G)], dst.at[:, pl.ds(C2A, C2G)]),
        ]
    return [(grads.at[:, pl.ds(g0 + C2G, C3G)], dst.at[:, pl.ds(0, C3G)])]


def add_rows(acc, half, at, x):
    if half == 0:
        acc[at] += x.reshape(8, 8, TOK)
    else:
        acc[:, at] += x.reshape(8, 8, TOK)


def early_body(core_ref, acts, grads, *refs, half):
    if half == 0:
        pieces = refs[:9]
        ca, cg, pbuf, hbuf, sems = refs[9:]
        ca[...] = jnp.zeros_like(ca)
        cg[...] = jnp.zeros_like(cg)
    else:
        pieces = refs[:3]
        ain, gin, ca, cg, pbuf, hbuf, sems = refs[3:]
    c = core_ref[0]
    o = c if half == 0 else 1 - c
    todo = []
    for part in range(3):
        w, s = WIDTHS[part], STARTS[part]
        out = []
        for k in range(3):
            if half == 0:
                out.append((pieces[part * 3 + k], pbuf.at[k, :, :, :, pl.ds(s, w)]))
            else:
                out.append(
                    (pieces[k].at[:, :, :, pl.ds(s, w)], pbuf.at[k, :, :, :, pl.ds(s, w)])
                )
        out += train_copies(acts, grads, o, part, hbuf.at[part])
        cps = [pltpu.make_async_copy(a, b, sems.at[part, i]) for i, (a, b) in enumerate(out)]
        for cp in cps:
            cp.start()
        todo.append(cps)
    if half == 1:
        moves = [
            pltpu.make_async_copy(ain, ca, sems.at[3, 0]),
            pltpu.make_async_copy(gin, cg, sems.at[3, 1]),
        ]
        for cp in moves:
            cp.start()
        for cp in moves:
            cp.wait()
    for part in range(3):
        for cp in todo[part]:
            cp.wait()
        for name, at, w in SEGMENTS[part]:
            acc = ca if name == "a" else cg
            p0 = STARTS[part] + at
            rows = pbuf[:, :, :, :, p0:p0 + w].reshape(384, w)
            x = nt(rows, hbuf[part, :, at:at + w])
            for k in range(3):
                for s4 in range(2):
                    r = k * 128 + s4 * 64
                    add_rows(acc, half, place(part, k, s4), x[r:r + 64])


def early_cross(core, acts, grads, pieces, accs, half):
    anyspec = pl.BlockSpec(memory_space=pl.ANY)
    vmem = pl.BlockSpec(memory_space=pltpu.VMEM)
    args = list(pieces) + list(accs)
    return pl.pallas_call(
        functools.partial(early_body, half=half),
        in_specs=[pl.BlockSpec(memory_space=pltpu.SMEM)] + [anyspec] * (2 + len(args)),
        out_specs=[vmem] * 2,
        out_shape=[jax.ShapeDtypeStruct((8, 8, 8, TOK), jnp.float32)] * 2,
        scratch_shapes=[
            pltpu.VMEM((3, 2, 8, 8, ALLW), jnp.bfloat16),
            pltpu.VMEM((3, TOK, C1), jnp.bfloat16),
            pltpu.SemaphoreType.DMA((4, 6)),
        ],
        compiler_params=pltpu.CompilerParams(vmem_limit_bytes=28 << 20),
        cost_estimate=pl.CostEstimate(
            flops=2 * 512 * 384 * (HA + HG), bytes_accessed=2 * TOK * (FF + D), transcendentals=0
        ),
    )(core, acts, grads, *args)


def late_body(core_ref, acts, grads, gram_ref, ain, gin, *refs):
    own, other = refs[:12], refs[12:16]
    raw_ref, norm_ref, vbuf, hbuf, ca, cg, ka, kg, ids, sems, asem = refs[16:]
    c = core_ref[0]

    def copies(n):
        half, part = ORDER[n]
        b = n % 2
        w, s = WIDTHS[part], STARTS[part]
        out = []
        for k in range(4):
            for s4 in range(2):
                at = place(part, k, s4)
                if half == 0:
                    out.append((own[part * 4 + k].at[s4], vbuf.at[b, at, :, :, pl.ds(0, w)]))
                else:
                    out.append(
                        (other[k].at[s4, :, :, pl.ds(s, w)], vbuf.at[b, :, at, :, pl.ds(0, w)])
                    )
        o = c if half == 0 else 1 - c
        out += train_copies(acts, grads, o, part, hbuf.at[b])
        return [pltpu.make_async_copy(x, y, sems.at[b, i]) for i, (x, y) in enumerate(out)]

    for cp in copies(0):
        cp.start()
    moves = [
        pltpu.make_async_copy(ain, ca, asem.at[0]),
        pltpu.make_async_copy(gin, cg, asem.at[1]),
    ]
    for cp in moves:
        cp.start()
    for cp in moves:
        cp.wait()
    seen = set()
    for n, (half, part) in enumerate(ORDER):
        b = n % 2
        if n + 1 < len(ORDER):
            for cp in copies(n + 1):
                cp.start()
        for cp in copies(n):
            cp.wait()
        for name, at, w in SEGMENTS[part]:
            cross, kern = (ca, ka) if name == "a" else (cg, kg)
            cols = slice(at, at + w)
            rows = vbuf[b, :, :, :, cols].reshape(VAL, w)
            even = vbuf[b, :, 0:4, :, cols].reshape(VAL // 2, w)
            late = vbuf[b, 4:8, :, :, cols].reshape(VAL // 2, w)
            mine = jnp.where(c == 0, even, late)
            y = nt(mine, rows)
            if name in seen:
                kern[...] += y
            else:
                kern[...] = y
                seen.add(name)
            spots = [place(part, 3, s4) for s4 in range(2)]
            if half == 0:
                last = [vbuf[b, at4, :, :, cols].reshape(64, w) for at4 in spots]
            else:
                last = [vbuf[b, :, at4, :, cols].reshape(64, w) for at4 in spots]
            x = nt(jnp.concatenate(last, axis=0), hbuf[b, :, cols])
            for s4 in range(2):
                add_rows(cross, half, spots[s4], x[s4 * 64:s4 * 64 + 64])
        if n == 2:
            ids[...] = vbuf[b, :, :, :, C3G:C3].astype(jnp.float32)

    cross = ca[...].reshape(VAL, TOK) * cg[...].reshape(VAL, TOK)
    kern = ka[...] * kg[...]
    all_ids = ids[...].reshape(VAL, IDW)
    row_ids = jnp.transpose(all_ids)[0:1, :]
    half_ids = jnp.where(
        c == 0,
        ids[:, 0:4].reshape(VAL // 2, IDW),
        ids[4:8].reshape(VAL // 2, IDW),
    )
    for v in range(NVAL):
        keep = jnp.where(all_ids == float(v), 1.0, 0.0)
        keep = jnp.concatenate([keep] * 4, axis=1)
        raw_ref[v:v + 1, :] = jnp.sum(cross * keep, axis=0, keepdims=True)
        keep = jnp.where(half_ids == float(v), 1.0, 0.0)
        keep = jnp.concatenate([keep] * 4, axis=1)
        part = jnp.sum(kern * keep, axis=0, keepdims=True)
        part = jnp.sum(jnp.where(row_ids == float(v), part, 0.0))
        norm_ref[v:v + 1, :] = jnp.full((1, 128), part, jnp.float32)


def late_cross(core, acts, grads, gram, accs, own, other):
    anyspec = pl.BlockSpec(memory_space=pl.ANY)
    args = list(accs) + list(own) + list(other)
    return pl.pallas_call(
        late_body,
        in_specs=[pl.BlockSpec(memory_space=pltpu.SMEM)] + [anyspec] * (3 + len(args)),
        out_specs=[pl.BlockSpec(memory_space=pltpu.VMEM)] * 2,
        out_shape=[
            jax.ShapeDtypeStruct((NVAL, TOK), jnp.float32),
            jax.ShapeDtypeStruct((NVAL, 128), jnp.float32),
        ],
        scratch_shapes=[
            pltpu.VMEM((2, 8, 8, 8, C1), jnp.bfloat16),
            pltpu.VMEM((2, TOK, C1), jnp.bfloat16),
            pltpu.VMEM((8, 8, 8, TOK), jnp.float32),
            pltpu.VMEM((8, 8, 8, TOK), jnp.float32),
            pltpu.VMEM((VAL // 2, VAL), jnp.float32),
            pltpu.VMEM((VAL // 2, VAL), jnp.float32),
            pltpu.VMEM((8, 8, 8, IDW), jnp.float32),
            pltpu.SemaphoreType.DMA((2, 10)),
            pltpu.SemaphoreType.DMA((2,)),
        ],
        compiler_params=pltpu.CompilerParams(vmem_limit_bytes=28 << 20),
        cost_estimate=pl.CostEstimate(
            flops=2 * 512 * 384 * (FF + D), bytes_accessed=4 * TOK * (FF + D), transcendentals=0
        ),
    )(core, acts, grads, gram, *args)


def shards(hidden_acts, out_grads, val_acts, val_grads, val_ids):
    hidden_acts = pltpu.with_memory_space_constraint(hidden_acts, pltpu.HBM)
    out_grads = pltpu.with_memory_space_constraint(out_grads, pltpu.HBM)
    core = lax.axis_index("dp") % 2
    first = core == 0
    idcol = jnp.broadcast_to(val_ids[:, None].astype(jnp.bfloat16), (4, IDW))
    halves = [
        jnp.concatenate(
            [val_acts[:, h * HA:(h + 1) * HA], val_grads[:, h * HG:(h + 1) * HG], idcol], axis=1
        )
        for h in range(2)
    ]
    keep = jnp.where(first, halves[0], halves[1])
    got = swap(jnp.where(first, halves[1], halves[0]))
    rows = jnp.concatenate([jnp.where(first, keep, got), jnp.where(first, got, keep)], axis=0)

    rows = double(rows, "z", 0)
    rows = double(rows, "y", 0)
    sa = self_acts(hidden_acts, rows)
    (rows,) = gate([double(rows, "x", 0)], sa)
    rows = rows.reshape(8, 8, ALLW)
    block_gram = self_grads(out_grads, sa, rows)
    piece = [[rows[..., s:s + w]] for s, w in zip(STARTS, WIDTHS)]
    grown = [double(piece[j][0], RUNS[j], 1) for j in range(3)]
    piece = [[x] for x in gate(grown, block_gram)]
    for j in range(3):
        piece[j].append(hop(piece[j][0], STEP5[j], 1))
    for j in range(3):
        piece[j].append(hop(piece[j][0], STEP6[j], 1))
    for j in range(3):
        piece[j].append(hop(piece[j][1], STEP6[j], 1))
    joined = [jnp.concatenate([piece[j][k] for j in range(3)], axis=-1) for k in range(4)]
    other = [swap(x) for x in joined[:3]]
    core = core.reshape(1).astype(jnp.int32)
    accs = early_cross(
        core, hidden_acts, out_grads, [piece[j][k] for j in range(3) for k in range(3)], [], 0
    )
    other += [swap(x) for x in gate(joined[3:], accs[0])]
    accs = early_cross(core, hidden_acts, out_grads, other[:3], accs, 1)
    raw, norm = late_cross(
        core, hidden_acts, out_grads, block_gram, accs,
        [piece[j][k] for j in range(3) for k in range(4)], other,
    )
    norm = norm + swap(norm)
    token_scores = raw * lax.rsqrt(norm[:, :1] + 1e-06)
    return (token_scores, block_gram)


def solution(mesh):
    return jax.shard_map(
        shards,
        mesh=mesh,
        in_specs=(
            P(AXES, None),
            P(AXES, None),
            P(AXES, None),
            P(AXES, None),
            P(AXES),
        ),
        out_specs=(P(None, AXES), P(AXES, None)),
        check_vma=False,
    )
```

```python
import functools
import math

import jax
import jax.numpy as jnp
from jax import lax
from jax.experimental import pallas as pl
from jax.experimental.pallas import tpu as pltpu
from jax.sharding import PartitionSpec as P

D = 8192
FF = 14336
BLK = 128
NVAL = 4
TOK = 512
VAL = 512
AXES = ("dp", "seq")
HA = FF // 2
HG = D // 2
C1 = 3840
C2A = HA - C1
C2G = 512
C2 = C2A + C2G
C3G = HG - C2G
IDW = 128
C3 = C3G + IDW
MASKS = ((1, 3), (3, 1))


def coords(i):
    dp, seq = divmod(i, 8)
    c = dp % 2
    z = (dp // 2) % 4
    x = (seq // 4) * 2 + dp // 8
    return {"x": x, "y": seq % 4, "z": z, "c": c}


def index(p):
    dp = ((p["x"] % 2) * 4 + p["z"]) * 2 + p["c"]
    return dp * 8 + (p["x"] // 2) * 4 + p["y"]


def ring_pairs(axis, step):
    pairs = []
    for i in range(128):
        p = coords(i)
        p[axis] ^= MASKS[p["c"]][step]
        pairs.append((i, index(p)))
    return pairs


def core_pairs():
    pairs = []
    for i in range(128):
        p = coords(i)
        p["c"] ^= 1
        pairs.append((i, index(p)))
    return pairs


def swap(x):
    return lax.ppermute(x, AXES, core_pairs())


def hop(x, axis, step):
    return lax.ppermute(x, AXES, ring_pairs(axis, step))


def double(x, axis, step):
    return jnp.stack([x, hop(x, axis, step)])


def pin(x):
    return pltpu.with_memory_space_constraint(x, pltpu.VMEM)


def gate(xs, dep):
    n = len(xs)
    anyspec = pl.BlockSpec(memory_space=pl.ANY)
    return pl.pallas_call(
        lambda *refs: None,
        in_specs=[anyspec] * (n + 1),
        out_specs=[anyspec] * n,
        out_shape=[jax.ShapeDtypeStruct(x.shape, x.dtype) for x in xs],
        input_output_aliases={i: i for i in range(n)},
        cost_estimate=pl.CostEstimate(flops=0, bytes_accessed=0, transcendentals=0),
    )(*[pin(x) for x in xs], dep)


def nt(a, b):
    return lax.dot_general(a, b, (((1,), (1,)), ((), ())), preferred_element_type=jnp.float32)


def self_add(acc, ref):
    acc[0:256, :] += nt(ref[256:512, :], ref[0:256, :])
    acc[256:384, 0:128] += nt(ref[128:256, :], ref[0:128, :])
    acc[384:512, 0:128] += nt(ref[384:512, :], ref[256:384, :])


def self_acts_body(acts_ref, dep_ref, out_ref):
    @pl.when(pl.program_id(0) == 0)
    def _():
        out_ref[...] = jnp.zeros_like(out_ref)

    self_add(out_ref, acts_ref)


def self_grads_body(grads_ref, sa_ref, dep_ref, out_ref, sg, *, steps):
    i = pl.program_id(0)

    @pl.when(i == 0)
    def _():
        sg[...] = jnp.zeros_like(sg)

    self_add(sg, grads_ref)

    @pl.when(i == steps - 1)
    def _():
        k = sa_ref[...] * sg[...]
        rows = lax.broadcasted_iota(jnp.int32, (4, 4), 0)
        cols = lax.broadcasted_iota(jnp.int32, (4, 4), 1)
        out = jnp.zeros((4, 4), jnp.float32)
        spots = (
            (2, 0, 0, 0), (2, 1, 0, 128), (3, 0, 128, 0), (3, 1, 128, 128),
            (1, 0, 256, 0), (3, 2, 384, 0),
        )
        for b, c, r0, c0 in spots:
            s = jnp.sum(k[r0:r0 + 128, c0:c0 + 128])
            out = jnp.where((rows == b) & (cols == c), s, out)
        out_ref[...] = out / (float(BLK) * math.sqrt(float(FF) * float(D)))


KC = 2048


def self_acts(acts, dep):
    return pl.pallas_call(
        self_acts_body,
        grid=(FF // KC,),
        in_specs=[
            pl.BlockSpec((TOK, KC), lambda i: (0, i)),
            pl.BlockSpec(memory_space=pl.ANY),
        ],
        out_specs=pl.BlockSpec((512, 256), lambda i: (0, 0)),
        out_shape=jax.ShapeDtypeStruct((512, 256), jnp.float32),
        compiler_params=pltpu.CompilerParams(vmem_limit_bytes=16 << 20),
        cost_estimate=pl.CostEstimate(
            flops=2 * 512 * 256 * FF, bytes_accessed=2 * TOK * FF, transcendentals=0
        ),
    )(acts, dep)


def self_grads(grads, sa, dep):
    return pl.pallas_call(
        functools.partial(self_grads_body, steps=D // KC),
        grid=(D // KC,),
        in_specs=[
            pl.BlockSpec((TOK, KC), lambda i: (0, i)),
            pl.BlockSpec((512, 256), lambda i: (0, 0)),
            pl.BlockSpec(memory_space=pl.ANY),
        ],
        out_specs=pl.BlockSpec((4, 4), lambda i: (0, 0)),
        out_shape=jax.ShapeDtypeStruct((4, 4), jnp.float32),
        scratch_shapes=[pltpu.VMEM((512, 256), jnp.float32)],
        compiler_params=pltpu.CompilerParams(vmem_limit_bytes=16 << 20),
        cost_estimate=pl.CostEstimate(
            flops=2 * 512 * 256 * D, bytes_accessed=2 * TOK * D, transcendentals=0
        ),
    )(grads, sa, dep)


RUNS = ("y", "z", "x")
STEP5 = ("z", "x", "y")
STEP6 = ("x", "y", "z")
WEIGHT = {"x": 4, "y": 2, "z": 1}


def place(part, k, s4):
    n = s4 * WEIGHT[RUNS[part]]
    if k in (1, 3):
        n += WEIGHT[STEP5[part]]
    if k in (2, 3):
        n += WEIGHT[STEP6[part]]
    return n


WIDTHS = (C1, C2, C3)
STARTS = (0, C1, C1 + C2)
ALLW = C1 + C2 + C3
SEGMENTS = ((("a", 0, C1),), (("a", 0, C2A), ("g", C2A, C2G)), (("g", 0, C3G),))


def train_copies(acts, grads, o, part, dst):
    a0 = pl.multiple_of(o * HA, 128)
    g0 = pl.multiple_of(o * HG, 128)
    if part == 0:
        return [(acts.at[:, pl.ds(a0, C1)], dst.at[:, pl.ds(0, C1)])]
    if part == 1:
        return [
            (acts.at[:, pl.ds(a0 + C1, C2A)], dst.at[:, pl.ds(0, C2A)]),
            (grads.at[:, pl.ds(g0, C2G)], dst.at[:, pl.ds(C2A, C2G)]),
        ]
    return [(grads.at[:, pl.ds(g0 + C2G, C3G)], dst.at[:, pl.ds(0, C3G)])]


def add_rows(acc, half, at, x):
    if half == 0:
        acc[at] += x.reshape(8, 8, TOK)
    else:
        acc[:, at] += x.reshape(8, 8, TOK)


def start_train(core_ref, acts, grads, half, hbuf, sems):
    c = core_ref[0]
    o = c if half == 0 else 1 - c
    todo = []
    for part in range(3):
        moves = train_copies(acts, grads, o, part, hbuf.at[part])
        cps = [pltpu.make_async_copy(a, b, sems.at[part, i]) for i, (a, b) in enumerate(moves)]
        for cp in cps:
            cp.start()
        todo.append(cps)
    return todo


def cols_of(half, part, at, w):
    base = at if half == 0 else STARTS[part] + at
    return slice(base, base + w)


def cross_rows(half, ks, pieces, todo, hbuf, ca, cg):
    for part in range(3):
        for cp in todo[part]:
            cp.wait()
        for name, at, w in SEGMENTS[part]:
            acc = ca if name == "a" else cg
            cols = cols_of(half, part, at, w)
            rows = [pieces[part][i][:, :, :, cols].reshape(128, w) for i in range(len(ks))]
            rows = rows[0] if len(rows) == 1 else jnp.concatenate(rows, axis=0)
            x = nt(rows, hbuf[part, :, at:at + w])
            for i, k in enumerate(ks):
                for s4 in range(2):
                    r = i * 128 + s4 * 64
                    add_rows(acc, half, place(part, k, s4), x[r:r + 64])


def val_rows(core_ref, blocks, name, seen, ka, kg):
    even = jnp.concatenate([x[:32] for x in blocks], axis=0)
    late = jnp.concatenate(blocks[4:], axis=0)
    y = nt(jnp.where(core_ref[0] == 0, even, late), jnp.concatenate(blocks, axis=0))
    acc = ka if name == "a" else kg
    if name in seen:
        acc[...] += y
    else:
        acc[...] = y
        seen.add(name)


def early_own_body(core_ref, acts, grads, dep_ref, *refs):
    pieces = [refs[p * 3:p * 3 + 3] for p in range(3)]
    ca, cg, tok, hbuf, sems = refs[9:]
    tok[...] = jnp.zeros_like(tok)
    todo = start_train(core_ref, acts, grads, 0, hbuf, sems)
    ca[...] = jnp.zeros_like(ca)
    cg[...] = jnp.zeros_like(cg)
    cross_rows(0, (0, 1, 2), pieces, todo, hbuf, ca, cg)


def early_other_body(core_ref, acts, grads, o0, o1, o2, ain, gin, ca, cg, hbuf, sems):
    todo = start_train(core_ref, acts, grads, 1, hbuf, sems)
    cross_rows(1, (0, 1, 2), [(o0, o1, o2)] * 3, todo, hbuf, ca, cg)


def late_own_body(core_ref, acts, grads, *refs):
    pieces = [refs[p * 4:p * 4 + 4] for p in range(3)]
    ca, cg, ka, kg, ids, hbuf, sems = refs[14:]
    todo = start_train(core_ref, acts, grads, 0, hbuf, sems)

    def blocks(part, cols, w):
        out = [None] * 8
        for k in range(4):
            for s4 in range(2):
                out[place(part, k, s4)] = pieces[part][k][s4, :, :, cols].reshape(64, w)
        return out

    for at, x in enumerate(blocks(2, slice(C3G, C3), IDW)):
        ids[at * 64:at * 64 + 64, :] = x.astype(jnp.float32)
    seen = set()
    for part in range(3):
        for name, at, w in SEGMENTS[part]:
            val_rows(core_ref, blocks(part, slice(at, at + w), w), name, seen, ka, kg)
    cross_rows(0, (3,), [p[3:] for p in pieces], todo, hbuf, ca, cg)


def late_other_body(core_ref, acts, grads, o0, o1, o2, o3, ain, gin, kain, kgin, ids,
                    raw_ref, norm_ref, ca, cg, ka, kg, hbuf, sems, vbuf, vsems):
    c = core_ref[0]
    todo = start_train(core_ref, acts, grads, 1, hbuf, sems)

    def moves(part):
        b = part % 2
        cols = pl.ds(STARTS[part], WIDTHS[part])
        return [
            pltpu.make_async_copy(
                o.at[s4, :, :, cols],
                vbuf.at[b, :, place(part, k, s4), :, pl.ds(0, WIDTHS[part])],
                vsems.at[b, k, s4],
            )
            for k, o in enumerate((o0, o1, o2, o3)) for s4 in range(2)
        ]

    for part in range(2):
        for cp in moves(part):
            cp.start()
    cross_rows(1, (3,), [(o3,)] * 3, todo, hbuf, ca, cg)
    seen = {"a", "g"}
    for part in range(3):
        for cp in moves(part):
            cp.wait()
        for name, at, w in SEGMENTS[part]:
            blocks = [vbuf[part % 2, b, :, :, at:at + w].reshape(64, w) for b in range(8)]
            val_rows(core_ref, blocks, name, seen, ka, kg)
        if part == 0:
            for cp in moves(2):
                cp.start()

    cross = ca[...].reshape(VAL, TOK) * cg[...].reshape(VAL, TOK)
    kern = ka[...] * kg[...]
    all_ids = ids[...]
    row_ids = jnp.transpose(all_ids)[0:1, :]
    even = jnp.concatenate([all_ids[b * 64:b * 64 + 32] for b in range(8)], axis=0)
    half_ids = jnp.where(c == 0, even, all_ids[256:512])
    for v in range(NVAL):
        keep = jnp.where(all_ids == float(v), 1.0, 0.0)
        keep = jnp.concatenate([keep] * 4, axis=1)
        raw_ref[v:v + 1, :] = jnp.sum(cross * keep, axis=0, keepdims=True)
        keep = jnp.where(half_ids == float(v), 1.0, 0.0)
        keep = jnp.concatenate([keep] * 4, axis=1)
        part = jnp.sum(kern * keep, axis=0, keepdims=True)
        part = jnp.sum(jnp.where(row_ids == float(v), part, 0.0))
        norm_ref[v:v + 1, :] = jnp.full((1, 128), part, jnp.float32)


ACC = jax.ShapeDtypeStruct((8, 8, 8, TOK), jnp.float32)
KERN = jax.ShapeDtypeStruct((VAL // 2, VAL), jnp.float32)


def local_call(body, core, acts, grads, args, outs, flops, scratch=(), anys=(), aliases=None, mib=21):
    vmem = pl.BlockSpec(memory_space=pltpu.VMEM)
    anyspec = pl.BlockSpec(memory_space=pl.ANY)
    return pl.pallas_call(
        body,
        in_specs=[pl.BlockSpec(memory_space=pltpu.SMEM)] + [anyspec] * 2
        + [anyspec if i in anys else vmem for i in range(len(args))],
        out_specs=[vmem] * len(outs),
        out_shape=outs,
        scratch_shapes=[
            pltpu.VMEM((3, TOK, C1), jnp.bfloat16),
            pltpu.SemaphoreType.DMA((3, 2)),
        ] + list(scratch),
        input_output_aliases={3 + k: v for k, v in (aliases or {}).items()},
        compiler_params=pltpu.CompilerParams(vmem_limit_bytes=mib << 20),
        cost_estimate=pl.CostEstimate(
            flops=flops, bytes_accessed=TOK * (FF + D), transcendentals=0
        ),
    )(core, acts, grads, *[x if i in anys else pin(x) for i, x in enumerate(args)])


def shards(hidden_acts, out_grads, val_acts, val_grads, val_ids):
    hidden_acts = pltpu.with_memory_space_constraint(hidden_acts, pltpu.HBM)
    out_grads = pltpu.with_memory_space_constraint(out_grads, pltpu.HBM)
    core = lax.axis_index("dp") % 2
    first = core == 0
    idcol = jnp.broadcast_to(val_ids[:, None].astype(jnp.bfloat16), (4, IDW))
    halves = [
        jnp.concatenate(
            [val_acts[:, h * HA:(h + 1) * HA], val_grads[:, h * HG:(h + 1) * HG], idcol], axis=1
        )
        for h in range(2)
    ]
    keep = jnp.where(first, halves[0], halves[1])
    got = swap(jnp.where(first, halves[1], halves[0]))
    rows = jnp.concatenate([jnp.where(first, keep, got), jnp.where(first, got, keep)], axis=0)

    rows = double(rows, "z", 0)
    rows = double(rows, "y", 0)
    sa = self_acts(hidden_acts, rows)
    (rows,) = gate([double(rows, "x", 0)], sa)
    rows = rows.reshape(8, 8, ALLW)
    block_gram = self_grads(out_grads, sa, rows)
    piece = [[rows[..., s:s + w]] for s, w in zip(STARTS, WIDTHS)]
    piece = [[double(piece[j][0], RUNS[j], 1)] for j in range(3)]
    for j in range(3):
        piece[j].append(hop(piece[j][0], STEP5[j], 1))
    for j in range(3):
        piece[j].append(hop(piece[j][0], STEP6[j], 1))
    for j in range(3):
        piece[j].append(hop(piece[j][1], STEP6[j], 1))
    joined = [jnp.concatenate([piece[j][k] for j in range(3)], axis=-1) for k in range(4)]
    o0, o1, o2 = [swap(x) for x in joined[:3]]
    call = functools.partial(
        local_call, core=core.reshape(1).astype(jnp.int32), acts=hidden_acts, grads=out_grads
    )
    unit = 2 * 512 * (HA + HG)
    ca, cg, tok = call(
        early_own_body, args=[block_gram] + [piece[j][k] for j in range(3) for k in range(3)],
        outs=[ACC, ACC, jax.ShapeDtypeStruct((8, 128), jnp.float32)],
        flops=384 * unit, anys=(0,),
    )
    (joined3,) = gate(joined[3:], tok)
    o3 = swap(joined3)
    ca, cg = call(
        early_other_body, args=[o0, o1, o2, ca, cg], outs=[ACC, ACC],
        flops=384 * unit, aliases={3: 0, 4: 1},
    )
    ids = jax.ShapeDtypeStruct((VAL, IDW), jnp.float32)
    ca, cg, ka, kg, ids = call(
        late_own_body, args=[piece[j][k] for j in range(3) for k in range(4)] + [ca, cg],
        outs=[ACC, ACC, KERN, KERN, ids], flops=384 * unit, aliases={12: 0, 13: 1},
    )
    raw, norm, *_ = call(
        late_other_body, args=[o0, o1, o2, o3, ca, cg, ka, kg, ids],
        outs=[
            jax.ShapeDtypeStruct((NVAL, TOK), jnp.float32),
            jax.ShapeDtypeStruct((NVAL, 128), jnp.float32),
            ACC, ACC, KERN, KERN,
        ],
        scratch=[
            pltpu.VMEM((2, 8, 8, 8, C1), jnp.bfloat16),
            pltpu.SemaphoreType.DMA((2, 4, 2)),
        ],
        flops=384 * unit, aliases={4: 2, 5: 3, 6: 4, 7: 5}, mib=32,
    )
    norm = norm + swap(norm)
    token_scores = raw * lax.rsqrt(norm[:, :1] + 1e-06)
    return (token_scores, block_gram)


def solution(mesh):
    return jax.shard_map(
        shards,
        mesh=mesh,
        in_specs=(
            P(AXES, None),
            P(AXES, None),
            P(AXES, None),
            P(AXES, None),
            P(AXES),
        ),
        out_specs=(P(None, AXES), P(AXES, None)),
        check_vma=False,
    )
```

```python
import functools
import math

import jax
import jax.numpy as jnp
from jax import lax
from jax.experimental import pallas as pl
from jax.experimental.pallas import tpu as pltpu
from jax.sharding import PartitionSpec as P

D = 8192
FF = 14336
BLK = 128
NVAL = 4
TOK = 512
VAL = 512
AXES = ("dp", "seq")
HA = FF // 2
HG = D // 2
C1 = 3840
C2A = HA - C1
C2G = 512
C2 = C2A + C2G
C3G = HG - C2G
IDW = 128
C3 = C3G + IDW
MASKS = ((1, 3), (3, 1))


def coords(i):
    dp, seq = divmod(i, 8)
    c = dp % 2
    z = (dp // 2) % 4
    x = (seq // 4) * 2 + dp // 8
    return {"x": x, "y": seq % 4, "z": z, "c": c}


def index(p):
    dp = ((p["x"] % 2) * 4 + p["z"]) * 2 + p["c"]
    return dp * 8 + (p["x"] // 2) * 4 + p["y"]


def ring_pairs(axis, step):
    pairs = []
    for i in range(128):
        p = coords(i)
        p[axis] ^= MASKS[p["c"]][step]
        pairs.append((i, index(p)))
    return pairs


def core_pairs():
    pairs = []
    for i in range(128):
        p = coords(i)
        p["c"] ^= 1
        pairs.append((i, index(p)))
    return pairs


def swap(x):
    return lax.ppermute(x, AXES, core_pairs())


def hop(x, axis, step):
    return lax.ppermute(x, AXES, ring_pairs(axis, step))


def double(x, axis, step):
    return jnp.stack([x, hop(x, axis, step)])


def pin(x):
    return pltpu.with_memory_space_constraint(x, pltpu.VMEM)


def gate(xs, dep):
    n = len(xs)
    anyspec = pl.BlockSpec(memory_space=pl.ANY)
    return pl.pallas_call(
        lambda *refs: None,
        in_specs=[anyspec] * (n + 1),
        out_specs=[anyspec] * n,
        out_shape=[jax.ShapeDtypeStruct(x.shape, x.dtype) for x in xs],
        input_output_aliases={i: i for i in range(n)},
        cost_estimate=pl.CostEstimate(flops=0, bytes_accessed=0, transcendentals=0),
    )(*[pin(x) for x in xs], dep)


def nt(a, b):
    return lax.dot_general(a, b, (((1,), (1,)), ((), ())), preferred_element_type=jnp.float32)


def self_add(acc, ref):
    acc[0:256, :] += nt(ref[256:512, :], ref[0:256, :])
    acc[256:384, 0:128] += nt(ref[128:256, :], ref[0:128, :])
    acc[384:512, 0:128] += nt(ref[384:512, :], ref[256:384, :])


def self_first_body(x_ref, dep_ref, out_ref):
    @pl.when(pl.program_id(0) == 0)
    def _():
        out_ref[...] = jnp.zeros_like(out_ref)

    self_add(out_ref, x_ref)


def self_last_body(x_ref, first_ref, dep_ref, out_ref, acc, *, steps):
    i = pl.program_id(0)

    @pl.when(i == 0)
    def _():
        acc[...] = jnp.zeros_like(acc)

    self_add(acc, x_ref)

    @pl.when(i == steps - 1)
    def _():
        k = first_ref[...] * acc[...]
        rows = lax.broadcasted_iota(jnp.int32, (4, 4), 0)
        cols = lax.broadcasted_iota(jnp.int32, (4, 4), 1)
        out = jnp.zeros((4, 4), jnp.float32)
        spots = (
            (2, 0, 0, 0), (2, 1, 0, 128), (3, 0, 128, 0), (3, 1, 128, 128),
            (1, 0, 256, 0), (3, 2, 384, 0),
        )
        for b, c, r0, c0 in spots:
            s = jnp.sum(k[r0:r0 + 128, c0:c0 + 128])
            out = jnp.where((rows == b) & (cols == c), s, out)
        out_ref[...] = out / (float(BLK) * math.sqrt(float(FF) * float(D)))


KC = 2048


def self_call(x, dep, first=None):
    width = x.shape[1]
    half = pl.BlockSpec((512, 256), lambda i: (0, 0))
    anyspec = pl.BlockSpec(memory_space=pl.ANY)
    args = [x] + ([] if first is None else [first]) + [dep]
    body = self_first_body
    if first is not None:
        body = functools.partial(self_last_body, steps=width // KC)
    return pl.pallas_call(
        body,
        grid=(width // KC,),
        in_specs=[pl.BlockSpec((TOK, KC), lambda i: (0, i))]
        + ([] if first is None else [half]) + [anyspec],
        out_specs=half if first is None else pl.BlockSpec((4, 4), lambda i: (0, 0)),
        out_shape=jax.ShapeDtypeStruct((512, 256) if first is None else (4, 4), jnp.float32),
        scratch_shapes=[] if first is None else [pltpu.VMEM((512, 256), jnp.float32)],
        compiler_params=pltpu.CompilerParams(vmem_limit_bytes=16 << 20),
        cost_estimate=pl.CostEstimate(
            flops=2 * 512 * 256 * width, bytes_accessed=2 * TOK * width, transcendentals=0
        ),
    )(*args)


RUNS = ("y", "z", "x")
STEP5 = ("z", "x", "y")
STEP6 = ("x", "y", "z")
WEIGHT = {"x": 4, "y": 2, "z": 1}


def place(part, k, s4):
    n = s4 * WEIGHT[RUNS[part]]
    if k in (1, 3):
        n += WEIGHT[STEP5[part]]
    if k in (2, 3):
        n += WEIGHT[STEP6[part]]
    return n


WIDTHS = (C1, C2, C3)
STARTS = (0, C1, C1 + C2)
ALLW = C1 + C2 + C3
ORDER = tuple((half, part) for half in range(2) for part in range(3))
SEGMENTS = ((("a", 0, C1),), (("a", 0, C2A), ("g", C2A, C2G)), (("g", 0, C3G),))


def train_copies(acts, grads, o, part, dst):
    a0 = pl.multiple_of(o * HA, 128)
    g0 = pl.multiple_of(o * HG, 128)
    if part == 0:
        return [(acts.at[:, pl.ds(a0, C1)], dst.at[:, pl.ds(0, C1)])]
    if part == 1:
        return [
            (acts.at[:, pl.ds(a0 + C1, C2A)], dst.at[:, pl.ds(0, C2A)]),
            (grads.at[:, pl.ds(g0, C2G)], dst.at[:, pl.ds(C2A, C2G)]),
        ]
    return [(grads.at[:, pl.ds(g0 + C2G, C3G)], dst.at[:, pl.ds(0, C3G)])]


SLOTS = 3


class Train:
    def __init__(self, core_ref, acts, grads, order, hbuf, sems):
        c = core_ref[0]
        self.hbuf, self.todo = hbuf, []
        for n, (half, part) in enumerate(order):
            slot = n % SLOTS
            moves = train_copies(acts, grads, c if half == 0 else 1 - c, part, hbuf.at[slot])
            self.todo.append(
                [pltpu.make_async_copy(a, b, sems.at[slot, i]) for i, (a, b) in enumerate(moves)]
            )
        for n in range(min(SLOTS, len(order))):
            self.start(n)

    def start(self, n):
        if n < len(self.todo):
            for cp in self.todo[n]:
                cp.start()

    def wait(self, n):
        for cp in self.todo[n]:
            cp.wait()

    def get(self, n, at, w):
        return self.hbuf[n % SLOTS, :, at:at + w]


def cross_rows(part, ks, pieces, train, n, ca, cg):
    train.wait(n)
    for name, at, w in SEGMENTS[part]:
        acc = ca if name == "a" else cg
        rows = [p[:, :, :, at:at + w].reshape(128, w) for p in pieces]
        rows = rows[0] if len(rows) == 1 else jnp.concatenate(rows, axis=0)
        x = nt(rows, train.get(n, at, w))
        for i, k in enumerate(ks):
            for s4 in range(2):
                r = i * 128 + s4 * 64
                acc[place(part, k, s4)] += x[r:r + 64].reshape(8, 8, TOK)
    train.start(n + SLOTS)


def val_rows(core_ref, blocks, name, seen, ka, kg):
    even = jnp.concatenate([x[:32] for x in blocks], axis=0)
    late = jnp.concatenate(blocks[4:], axis=0)
    y = nt(jnp.where(core_ref[0] == 0, even, late), jnp.concatenate(blocks, axis=0))
    acc = ka if name == "a" else kg
    if name in seen:
        acc[...] += y
    else:
        acc[...] = y
        seen.add(name)


def early_body(core_ref, acts, grads, dep_ref, *refs):
    own = [refs[p * 3:p * 3 + 3] for p in range(3)]
    ca, cg, tok, hbuf, sems = refs[9:]
    train = Train(core_ref, acts, grads, ORDER[:3], hbuf, sems)
    tok[...] = jnp.zeros_like(tok)
    ca[...] = jnp.zeros_like(ca)
    cg[...] = jnp.zeros_like(cg)
    for part in range(3):
        cross_rows(part, (0, 1, 2), own[part], train, part, ca, cg)


def late_own_body(core_ref, acts, grads, *refs):
    pieces = [refs[p * 4:p * 4 + 4] for p in range(3)]
    ca, cg, ka, kg, ids, hbuf, sems, pbuf, psems = refs[12:]

    def moves(part):
        b = part % 2
        return [
            pltpu.make_async_copy(
                pieces[part][k], pbuf.at[b, k, :, :, :, pl.ds(0, WIDTHS[part])], psems.at[b, k]
            )
            for k in range(4)
        ]

    for part in range(2):
        for cp in moves(part):
            cp.start()
    train = Train(core_ref, acts, grads, ORDER[:3], hbuf, sems)
    ca[...] = jnp.zeros_like(ca)
    cg[...] = jnp.zeros_like(cg)
    seen = set()
    for part in range(3):
        b = part % 2
        for cp in moves(part):
            cp.wait()

        def blocks(at, w):
            out = [None] * 8
            for k in range(4):
                for s4 in range(2):
                    out[place(part, k, s4)] = pbuf[b, k, s4, :, :, at:at + w].reshape(64, w)
            return out

        for name, at, w in SEGMENTS[part]:
            val_rows(core_ref, blocks(at, w), name, seen, ka, kg)
        if part == 2:
            for at, x in enumerate(blocks(C3G, IDW)):
                ids[at * 64:at * 64 + 64, :] = x.astype(jnp.float32)
        cross_rows(part, (3,), [pbuf.at[b, 3]], train, part, ca, cg)
        if part == 0:
            for cp in moves(2):
                cp.start()


def late_other_body(core_ref, acts, grads, o0, o1, o2, o3, a1, g1, a3, g3, k1, k2, ids,
                    raw_ref, norm_ref, hbuf, sems, vbuf, ca, cg, ka, kg, vsems):
    c = core_ref[0]

    def moves(part):
        b = part % 2
        cols = pl.ds(STARTS[part], WIDTHS[part])
        return [
            pltpu.make_async_copy(
                o.at[s4, :, :, cols],
                vbuf.at[b, :, place(part, k, s4), :, pl.ds(0, WIDTHS[part])],
                vsems.at[b, k, s4],
            )
            for k, o in enumerate((o0, o1, o2, o3)) for s4 in range(2)
        ]

    for part in range(2):
        for cp in moves(part):
            cp.start()
    train = Train(core_ref, acts, grads, ORDER[3:], hbuf, sems)
    ca[...] = (a1[...] + a3[...]).reshape(VAL, TOK)
    cg[...] = (g1[...] + g3[...]).reshape(VAL, TOK)
    ka[...] = k1[...]
    kg[...] = k2[...]
    seen = {"a", "g"}
    for part in range(3):
        for cp in moves(part):
            cp.wait()
        for name, at, w in SEGMENTS[part]:
            blocks = [vbuf[part % 2, b, :, :, at:at + w].reshape(64, w) for b in range(8)]
            val_rows(core_ref, blocks, name, seen, ka, kg)
        train.wait(part)
        for name, at, w in SEGMENTS[part]:
            acc = ca if name == "a" else cg
            rows = vbuf[part % 2, :, :, :, at:at + w].reshape(VAL, w)
            acc[...] += nt(rows, train.get(part, at, w))
        if part == 0:
            for cp in moves(2):
                cp.start()

    cross = ca[...] * cg[...]
    kern = ka[...] * kg[...]
    all_ids = ids[...]
    row_ids = jnp.transpose(all_ids)[0:1, :]
    even = jnp.concatenate([all_ids[b * 64:b * 64 + 32] for b in range(8)], axis=0)
    half_ids = jnp.where(c == 0, even, all_ids[256:512])
    for v in range(NVAL):
        keep = jnp.where(all_ids == float(v), 1.0, 0.0)
        keep = jnp.concatenate([keep] * 4, axis=1)
        raw_ref[v:v + 1, :] = jnp.sum(cross * keep, axis=0, keepdims=True)
        keep = jnp.where(half_ids == float(v), 1.0, 0.0)
        keep = jnp.concatenate([keep] * 4, axis=1)
        part = jnp.sum(kern * keep, axis=0, keepdims=True)
        part = jnp.sum(jnp.where(row_ids == float(v), part, 0.0))
        norm_ref[v:v + 1, :] = jnp.full((1, 128), part, jnp.float32)


ACC = jax.ShapeDtypeStruct((8, 8, 8, TOK), jnp.float32)
KERN = jax.ShapeDtypeStruct((VAL // 2, VAL), jnp.float32)


def local_call(body, core, acts, grads, args, outs, flops, scratch=(), anys=(), mib=28):
    vmem = pl.BlockSpec(memory_space=pltpu.VMEM)
    anyspec = pl.BlockSpec(memory_space=pl.ANY)
    return pl.pallas_call(
        body,
        in_specs=[pl.BlockSpec(memory_space=pltpu.SMEM)] + [anyspec] * 2
        + [anyspec if i in anys else vmem for i in range(len(args))],
        out_specs=[vmem] * len(outs),
        out_shape=outs,
        scratch_shapes=[
            pltpu.VMEM((SLOTS, TOK, C1), jnp.bfloat16),
            pltpu.SemaphoreType.DMA((SLOTS, 2)),
        ] + list(scratch),
        compiler_params=pltpu.CompilerParams(vmem_limit_bytes=mib << 20),
        cost_estimate=pl.CostEstimate(
            flops=flops, bytes_accessed=TOK * (FF + D), transcendentals=0
        ),
    )(core, acts, grads, *[x if i in anys else pin(x) for i, x in enumerate(args)])


def shards(hidden_acts, out_grads, val_acts, val_grads, val_ids):
    hidden_acts = pltpu.with_memory_space_constraint(hidden_acts, pltpu.HBM)
    out_grads = pltpu.with_memory_space_constraint(out_grads, pltpu.HBM)
    core = lax.axis_index("dp") % 2
    first = core == 0
    idcol = jnp.broadcast_to(val_ids[:, None].astype(jnp.bfloat16), (4, IDW))
    halves = [
        jnp.concatenate(
            [val_acts[:, h * HA:(h + 1) * HA], val_grads[:, h * HG:(h + 1) * HG], idcol], axis=1
        )
        for h in range(2)
    ]
    keep = jnp.where(first, halves[0], halves[1])
    got = swap(jnp.where(first, halves[1], halves[0]))
    rows = jnp.concatenate([jnp.where(first, keep, got), jnp.where(first, got, keep)], axis=0)

    rows = double(rows, "z", 0)
    sg = self_call(out_grads, rows)
    (rows,) = gate([double(rows, "y", 0)], sg)
    block_gram = self_call(hidden_acts, rows, sg)
    (rows,) = gate([double(rows, "x", 0)], block_gram)
    rows = rows.reshape(8, 8, ALLW)
    piece = [[rows[..., s:s + w]] for s, w in zip(STARTS, WIDTHS)]
    piece = [[double(piece[j][0], RUNS[j], 1)] for j in range(3)]
    for j in range(3):
        piece[j].append(hop(piece[j][0], STEP5[j], 1))
    for j in range(3):
        piece[j].append(hop(piece[j][0], STEP6[j], 1))
    for j in range(3):
        piece[j].append(hop(piece[j][1], STEP6[j], 1))
    joined = [jnp.concatenate([piece[j][k] for j in range(3)], axis=-1) for k in range(4)]
    o0, o1 = [swap(gate([x], block_gram)[0]) for x in joined[:2]]
    call = functools.partial(
        local_call, core=core.reshape(1).astype(jnp.int32), acts=hidden_acts, grads=out_grads
    )
    unit = 2 * 512 * (HA + HG)
    a1, g1, tok = call(
        early_body,
        args=[block_gram] + [piece[j][k] for j in range(3) for k in range(3)],
        outs=[ACC, ACC, jax.ShapeDtypeStruct((8, 128), jnp.float32)],
        flops=384 * unit, anys=(0,),
    )
    o2, o3 = [swap(gate([x], tok)[0]) for x in joined[2:]]
    ids = jax.ShapeDtypeStruct((VAL, IDW), jnp.float32)
    a3, g3, k1, k2, ids = call(
        late_own_body, args=[piece[j][k] for j in range(3) for k in range(4)],
        outs=[ACC, ACC, KERN, KERN, ids], flops=384 * unit, anys=range(12),
        scratch=[
            pltpu.VMEM((2, 4, 2, 8, 8, C1), jnp.bfloat16),
            pltpu.SemaphoreType.DMA((2, 4)),
        ],
        mib=30,
    )
    raw, norm = call(
        late_other_body, args=[o0, o1, o2, o3, a1, g1, a3, g3, k1, k2, ids],
        outs=[
            jax.ShapeDtypeStruct((NVAL, TOK), jnp.float32),
            jax.ShapeDtypeStruct((NVAL, 128), jnp.float32),
        ],
        scratch=[
            pltpu.VMEM((2, 8, 8, 8, C1), jnp.bfloat16),
            pltpu.VMEM((VAL, TOK), jnp.float32),
            pltpu.VMEM((VAL, TOK), jnp.float32),
            pltpu.VMEM((VAL // 2, VAL), jnp.float32),
            pltpu.VMEM((VAL // 2, VAL), jnp.float32),
            pltpu.SemaphoreType.DMA((2, 4, 2)),
        ],
        flops=768 * unit, mib=34,
    )
    norm = norm + swap(norm)
    token_scores = raw * lax.rsqrt(norm[:, :1] + 1e-06)
    return (token_scores, block_gram)


def solution(mesh):
    return jax.shard_map(
        shards,
        mesh=mesh,
        in_specs=(
            P(AXES, None),
            P(AXES, None),
            P(AXES, None),
            P(AXES, None),
            P(AXES),
        ),
        out_specs=(P(None, AXES), P(AXES, None)),
        check_vma=False,
    )
```

```python
import functools
import math

import jax
import jax.numpy as jnp
from jax import lax
from jax.experimental import pallas as pl
from jax.experimental.pallas import tpu as pltpu
from jax.sharding import PartitionSpec as P

D = 8192
FF = 14336
BLK = 128
NVAL = 4
TOK = 512
VAL = 512
AXES = ("dp", "seq")
HA = FF // 2
HG = D // 2
C1 = 3840
C2A = HA - C1
C2G = 512
C2 = C2A + C2G
C3G = HG - C2G
IDW = 128
C3 = C3G + IDW
MASKS = ((1, 3), (3, 1))


def coords(i):
    dp, seq = divmod(i, 8)
    c = dp % 2
    z = (dp // 2) % 4
    x = (seq // 4) * 2 + dp // 8
    return {"x": x, "y": seq % 4, "z": z, "c": c}


def index(p):
    dp = ((p["x"] % 2) * 4 + p["z"]) * 2 + p["c"]
    return dp * 8 + (p["x"] // 2) * 4 + p["y"]


def ring_pairs(axes, step):
    pairs = []
    for i in range(128):
        p = coords(i)
        for axis in axes:
            p[axis] ^= MASKS[p["c"]][step]
        pairs.append((i, index(p)))
    return pairs


def core_pairs():
    pairs = []
    for i in range(128):
        p = coords(i)
        p["c"] ^= 1
        pairs.append((i, index(p)))
    return pairs


def swap(x):
    return lax.ppermute(x, AXES, core_pairs())


def hop(x, axes, step):
    return lax.ppermute(x, AXES, ring_pairs(axes, step))


def double(x, axis, step):
    return jnp.stack([x, hop(x, axis, step)])


def pin(x):
    return pltpu.with_memory_space_constraint(x, pltpu.VMEM)


def gate(xs, *deps):
    n = len(xs)
    anyspec = pl.BlockSpec(memory_space=pl.ANY)
    return pl.pallas_call(
        lambda *refs: None,
        in_specs=[anyspec] * (n + len(deps)),
        out_specs=[anyspec] * n,
        out_shape=[jax.ShapeDtypeStruct(x.shape, x.dtype) for x in xs],
        input_output_aliases={i: i for i in range(n)},
        compiler_params=pltpu.CompilerParams(vmem_limit_bytes=1 << 20),
        cost_estimate=pl.CostEstimate(flops=0, bytes_accessed=0, transcendentals=0),
    )(*[pin(x) for x in xs], *deps)


def nt(a, b):
    return lax.dot_general(a, b, (((1,), (1,)), ((), ())), preferred_element_type=jnp.float32)


def self_add(acc, ref):
    acc[0:256, :] += nt(ref[256:512, :], ref[0:256, :])
    acc[256:384, 0:128] += nt(ref[128:256, :], ref[0:128, :])
    acc[384:512, 0:128] += nt(ref[384:512, :], ref[256:384, :])


def self_first_body(x_ref, dep_ref, out_ref):
    @pl.when(pl.program_id(0) == 0)
    def _():
        out_ref[...] = jnp.zeros_like(out_ref)

    self_add(out_ref, x_ref)


def self_last_body(x_ref, first_ref, dep_ref, out_ref, acc, *, steps):
    i = pl.program_id(0)

    @pl.when(i == 0)
    def _():
        acc[...] = jnp.zeros_like(acc)

    self_add(acc, x_ref)

    @pl.when(i == steps - 1)
    def _():
        k = first_ref[...] * acc[...]
        rows = lax.broadcasted_iota(jnp.int32, (4, 4), 0)
        cols = lax.broadcasted_iota(jnp.int32, (4, 4), 1)
        out = jnp.zeros((4, 4), jnp.float32)
        spots = (
            (2, 0, 0, 0), (2, 1, 0, 128), (3, 0, 128, 0), (3, 1, 128, 128),
            (1, 0, 256, 0), (3, 2, 384, 0),
        )
        for b, c, r0, c0 in spots:
            s = jnp.sum(k[r0:r0 + 128, c0:c0 + 128])
            out = jnp.where((rows == b) & (cols == c), s, out)
        out_ref[...] = out / (float(BLK) * math.sqrt(float(FF) * float(D)))


KC = 2048


def self_call(x, dep, first=None):
    width = x.shape[1]
    half = pl.BlockSpec((512, 256), lambda i: (0, 0))
    anyspec = pl.BlockSpec(memory_space=pl.ANY)
    args = [x] + ([] if first is None else [first]) + [dep]
    body = self_first_body
    if first is not None:
        body = functools.partial(self_last_body, steps=width // KC)
    return pl.pallas_call(
        body,
        grid=(width // KC,),
        in_specs=[pl.BlockSpec((TOK, KC), lambda i: (0, i))]
        + ([] if first is None else [half]) + [anyspec],
        out_specs=half if first is None else pl.BlockSpec((4, 4), lambda i: (0, 0)),
        out_shape=jax.ShapeDtypeStruct((512, 256) if first is None else (4, 4), jnp.float32),
        scratch_shapes=[] if first is None else [pltpu.VMEM((512, 256), jnp.float32)],
        compiler_params=pltpu.CompilerParams(vmem_limit_bytes=16 << 20),
        cost_estimate=pl.CostEstimate(
            flops=2 * 512 * 256 * width, bytes_accessed=2 * TOK * width, transcendentals=0
        ),
    )(*args)


RUNS = ("y", "z", "x")
STEP5 = ("z", "x", "y")
STEP6 = ("x", "y", "z")
WEIGHT = {"x": 4, "y": 2, "z": 1}


def place(part, k, s4):
    n = s4 * WEIGHT[RUNS[part]]
    if k in (1, 3):
        n += WEIGHT[STEP5[part]]
    if k in (2, 3):
        n += WEIGHT[STEP6[part]]
    return n


WIDTHS = (C1, C2, C3)
STARTS = (0, C1, C1 + C2)
ALLW = C1 + C2 + C3
ORDER = tuple((half, part) for half in range(2) for part in range(3))
SEGMENTS = ((("a", 0, C1),), (("a", 0, C2A), ("g", C2A, C2G)), (("g", 0, C3G),))


def train_copies(acts, grads, o, part, dst):
    a0 = pl.multiple_of(o * HA, 128)
    g0 = pl.multiple_of(o * HG, 128)
    if part == 0:
        return [(acts.at[:, pl.ds(a0, C1)], dst.at[:, pl.ds(0, C1)])]
    if part == 1:
        return [
            (acts.at[:, pl.ds(a0 + C1, C2A)], dst.at[:, pl.ds(0, C2A)]),
            (grads.at[:, pl.ds(g0, C2G)], dst.at[:, pl.ds(C2A, C2G)]),
        ]
    return [(grads.at[:, pl.ds(g0 + C2G, C3G)], dst.at[:, pl.ds(0, C3G)])]


SLOTS = 3


class Train:
    def __init__(self, core_ref, acts, grads, order, hbuf, sems):
        c = core_ref[0]
        self.hbuf, self.todo = hbuf, []
        for n, (half, part) in enumerate(order):
            slot = n % SLOTS
            moves = train_copies(acts, grads, c if half == 0 else 1 - c, part, hbuf.at[slot])
            self.todo.append(
                [pltpu.make_async_copy(a, b, sems.at[slot, i]) for i, (a, b) in enumerate(moves)]
            )
        for n in range(min(SLOTS, len(order))):
            self.start(n)

    def start(self, n):
        if n < len(self.todo):
            for cp in self.todo[n]:
                cp.start()

    def wait(self, n):
        for cp in self.todo[n]:
            cp.wait()

    def get(self, n, at, w):
        return self.hbuf[n % SLOTS, :, at:at + w]


def cross_rows(part, ks, pieces, train, n, ca, cg):
    train.wait(n)
    for name, at, w in SEGMENTS[part]:
        acc = ca if name == "a" else cg
        rows = [p[:, :, :, at:at + w].reshape(128, w) for p in pieces]
        rows = rows[0] if len(rows) == 1 else jnp.concatenate(rows, axis=0)
        x = nt(rows, train.get(n, at, w))
        for i, k in enumerate(ks):
            for s4 in range(2):
                r = i * 128 + s4 * 64
                acc[place(part, k, s4)] += x[r:r + 64].reshape(8, 8, TOK)
    train.start(n + SLOTS)


def val_rows(core_ref, blocks, name, seen, ka, kg):
    even = jnp.concatenate([x[:32] for x in blocks], axis=0)
    late = jnp.concatenate(blocks[4:], axis=0)
    y = nt(jnp.where(core_ref[0] == 0, even, late), jnp.concatenate(blocks, axis=0))
    acc = ka if name == "a" else kg
    if name in seen:
        acc[...] += y
    else:
        acc[...] = y
        seen.add(name)


def early_body(core_ref, acts, grads, dep_ref, *refs):
    own = [refs[p * 2:p * 2 + 2] for p in range(3)]
    ca, cg, tok, hbuf, sems = refs[6:]
    train = Train(core_ref, acts, grads, ORDER[:3], hbuf, sems)
    tok[...] = jnp.zeros_like(tok)
    ca[...] = jnp.zeros_like(ca)
    cg[...] = jnp.zeros_like(cg)
    for part in range(3):
        cross_rows(part, (0, 1), own[part], train, part, ca, cg)


def late_own_body(core_ref, acts, grads, *refs):
    pieces = [refs[p * 3:p * 3 + 3] for p in range(3)]
    ain, gin, ca, cg, ka, kg, ids, hbuf, sems, pbuf, psems, asems = refs[9:]
    sums = [
        pltpu.make_async_copy(ain, ca, asems.at[0]),
        pltpu.make_async_copy(gin, cg, asems.at[1]),
    ]

    def moves(part):
        b = part % 2
        x, a1, last = pieces[part]
        return [
            pltpu.make_async_copy(
                src, pbuf.at[b, k, :, :, :, pl.ds(0, WIDTHS[part])], psems.at[b, k]
            )
            for k, src in enumerate((x, a1, last.at[0], last.at[1]))
        ]

    for part in range(2):
        for cp in moves(part):
            cp.start()
    train = Train(core_ref, acts, grads, ORDER[:3], hbuf, sems)
    for cp in sums:
        cp.start()
    seen = set()
    for part in range(3):
        b = part % 2
        for cp in moves(part):
            cp.wait()

        def blocks(at, w):
            out = [None] * 8
            for k in range(4):
                for s4 in range(2):
                    out[place(part, k, s4)] = pbuf[b, k, s4, :, :, at:at + w].reshape(64, w)
            return out

        for name, at, w in SEGMENTS[part]:
            val_rows(core_ref, blocks(at, w), name, seen, ka, kg)
        if part == 2:
            for at, x in enumerate(blocks(C3G, IDW)):
                ids[at * 64:at * 64 + 64, :] = x.astype(jnp.float32)
        if part == 0:
            for cp in sums:
                cp.wait()
        cross_rows(part, (2, 3), [pbuf.at[b, 2], pbuf.at[b, 3]], train, part, ca, cg)
        if part == 0:
            for cp in moves(2):
                cp.start()


def late_other_body(core_ref, acts, grads, o0, o1, o2, ain, gin, k1, k2, idin,
                    raw_ref, norm_ref, hbuf, sems, vbuf, acc_a, acc_g, ka, kg, ids, vsems, asems):
    c = core_ref[0]
    sums = [
        pltpu.make_async_copy(x, y, asems.at[i])
        for i, (x, y) in enumerate(
            ((ain, acc_a), (gin, acc_g), (k1, ka), (k2, kg), (idin, ids))
        )
    ]

    def moves(part):
        b = part % 2
        cols = pl.ds(STARTS[part], WIDTHS[part])
        return [
            pltpu.make_async_copy(
                o.at[s4, :, :, cols],
                vbuf.at[b, :, place(part, k, s4), :, pl.ds(0, WIDTHS[part])],
                vsems.at[b, k, s4],
            )
            for k, o in enumerate((o0, o1, o2.at[0], o2.at[1])) for s4 in range(2)
        ]

    for part in range(2):
        for cp in moves(part):
            cp.start()
    train = Train(core_ref, acts, grads, ORDER[3:], hbuf, sems)
    for cp in sums:
        cp.start()
    seen = {"a", "g"}
    for part in range(3):
        for cp in moves(part):
            cp.wait()
        if part == 0:
            for cp in sums:
                cp.wait()
        for name, at, w in SEGMENTS[part]:
            blocks = [vbuf[part % 2, b, :, :, at:at + w].reshape(64, w) for b in range(8)]
            val_rows(core_ref, blocks, name, seen, ka, kg)
        train.wait(part)
        for name, at, w in SEGMENTS[part]:
            acc = acc_a if name == "a" else acc_g
            rows = vbuf[part % 2, :, :, :, at:at + w].reshape(VAL, w)
            acc[...] += nt(rows, train.get(part, at, w)).reshape(8, 8, 8, TOK)
        if part == 0:
            for cp in moves(2):
                cp.start()

    cross = acc_a[...].reshape(VAL, TOK) * acc_g[...].reshape(VAL, TOK)
    kern = ka[...] * kg[...]
    all_ids = ids[...]
    row_ids = jnp.transpose(all_ids)[0:1, :]
    even = jnp.concatenate([all_ids[b * 64:b * 64 + 32] for b in range(8)], axis=0)
    half_ids = jnp.where(c == 0, even, all_ids[256:512])
    for v in range(NVAL):
        keep = jnp.where(all_ids == float(v), 1.0, 0.0)
        keep = jnp.concatenate([keep] * 4, axis=1)
        raw_ref[v:v + 1, :] = jnp.sum(cross * keep, axis=0, keepdims=True)
        keep = jnp.where(half_ids == float(v), 1.0, 0.0)
        keep = jnp.concatenate([keep] * 4, axis=1)
        part = jnp.sum(kern * keep, axis=0, keepdims=True)
        part = jnp.sum(jnp.where(row_ids == float(v), part, 0.0))
        norm_ref[v:v + 1, :] = jnp.full((1, 128), part, jnp.float32)


ACC = jax.ShapeDtypeStruct((8, 8, 8, TOK), jnp.float32)
KERN = jax.ShapeDtypeStruct((VAL // 2, VAL), jnp.float32)


def local_call(body, core, acts, grads, args, outs, flops, scratch=(), anys=(), mib=28):
    vmem = pl.BlockSpec(memory_space=pltpu.VMEM)
    anyspec = pl.BlockSpec(memory_space=pl.ANY)
    return pl.pallas_call(
        body,
        in_specs=[pl.BlockSpec(memory_space=pltpu.SMEM)] + [anyspec] * 2
        + [anyspec if i in anys else vmem for i in range(len(args))],
        out_specs=[vmem] * len(outs),
        out_shape=outs,
        scratch_shapes=[
            pltpu.VMEM((SLOTS, TOK, C1), jnp.bfloat16),
            pltpu.SemaphoreType.DMA((SLOTS, 2)),
        ] + list(scratch),
        compiler_params=pltpu.CompilerParams(vmem_limit_bytes=mib << 20),
        cost_estimate=pl.CostEstimate(
            flops=flops, bytes_accessed=TOK * (FF + D), transcendentals=0
        ),
    )(core, acts, grads, *[x if i in anys else pin(x) for i, x in enumerate(args)])


def shards(hidden_acts, out_grads, val_acts, val_grads, val_ids):
    hidden_acts = pltpu.with_memory_space_constraint(hidden_acts, pltpu.HBM)
    out_grads = pltpu.with_memory_space_constraint(out_grads, pltpu.HBM)
    core = lax.axis_index("dp") % 2
    first = core == 0
    idcol = jnp.broadcast_to(val_ids[:, None].astype(jnp.bfloat16), (4, IDW))
    halves = [
        jnp.concatenate(
            [val_acts[:, h * HA:(h + 1) * HA], val_grads[:, h * HG:(h + 1) * HG], idcol], axis=1
        )
        for h in range(2)
    ]
    keep = jnp.where(first, halves[0], halves[1])
    got = swap(jnp.where(first, halves[1], halves[0]))
    rows = jnp.concatenate([jnp.where(first, keep, got), jnp.where(first, got, keep)], axis=0)

    near = [
        hop(rows, [a for a in "xyz" if n & WEIGHT[a]], 0) for n in (1, 2, 4, 3, 5, 6, 7)
    ]
    rows = jnp.stack([rows, near[0], near[1], near[3], near[2], near[4], near[5], near[6]])
    sg = self_call(out_grads, rows)
    x = [double(rows[..., s:s + w], RUNS[j], 1) for j, (s, w) in enumerate(zip(STARTS, WIDTHS))]
    x = gate(x, sg)
    block_gram = self_call(hidden_acts, x[1], sg)
    a1 = [hop(x[j], STEP5[j], 1) for j in range(3)]
    o0 = swap(gate([jnp.concatenate(x, axis=-1)], sg)[0])
    pair = gate([jnp.stack([x[j], a1[j]]) for j in range(3)], block_gram, o0)
    last = [hop(pair[j], STEP6[j], 1) for j in range(3)]
    o1 = swap(gate([jnp.concatenate(a1, axis=-1)], sg)[0])
    call = functools.partial(
        local_call, core=core.reshape(1).astype(jnp.int32), acts=hidden_acts, grads=out_grads
    )
    unit = 2 * 512 * (HA + HG)
    ca1, cg1, tok = call(
        early_body, args=[block_gram] + [y for j in range(3) for y in (x[j], a1[j])],
        outs=[ACC, ACC, jax.ShapeDtypeStruct((8, 128), jnp.float32)],
        flops=256 * unit, anys=(0,),
    )
    o2 = swap(gate([jnp.concatenate(last, axis=-1)], tok, o1)[0])
    ids = jax.ShapeDtypeStruct((VAL, IDW), jnp.float32)
    ca2, cg2, k1, k2, ids = call(
        late_own_body,
        args=[y for j in range(3) for y in (x[j], a1[j], last[j])] + [ca1, cg1],
        outs=[ACC, ACC, KERN, KERN, ids], flops=512 * unit, anys=range(11),
        scratch=[
            pltpu.VMEM((2, 4, 2, 8, 8, C1), jnp.bfloat16),
            pltpu.SemaphoreType.DMA((2, 4)),
            pltpu.SemaphoreType.DMA((2,)),
        ],
        mib=30,
    )
    raw, norm = call(
        late_other_body, args=[o0, o1, o2, ca2, cg2, k1, k2, ids], anys=range(8),
        outs=[
            jax.ShapeDtypeStruct((NVAL, TOK), jnp.float32),
            jax.ShapeDtypeStruct((NVAL, 128), jnp.float32),
        ],
        scratch=[
            pltpu.VMEM((2, 8, 8, 8, C1), jnp.bfloat16),
            pltpu.VMEM((8, 8, 8, TOK), jnp.float32),
            pltpu.VMEM((8, 8, 8, TOK), jnp.float32),
            pltpu.VMEM((VAL // 2, VAL), jnp.float32),
            pltpu.VMEM((VAL // 2, VAL), jnp.float32),
            pltpu.VMEM((VAL, IDW), jnp.float32),
            pltpu.SemaphoreType.DMA((2, 4, 2)),
            pltpu.SemaphoreType.DMA((5,)),
        ],
        flops=768 * unit, mib=34,
    )
    norm = norm + swap(norm)
    token_scores = raw * lax.rsqrt(norm[:, :1] + 1e-06)
    return (token_scores, block_gram)


def solution(mesh):
    return jax.shard_map(
        shards,
        mesh=mesh,
        in_specs=(
            P(AXES, None),
            P(AXES, None),
            P(AXES, None),
            P(AXES, None),
            P(AXES),
        ),
        out_specs=(P(None, AXES), P(AXES, None)),
        check_vma=False,
    )
```

```python
import functools
import math

import jax
import jax.numpy as jnp
from jax import lax
from jax.experimental import pallas as pl
from jax.experimental.pallas import tpu as pltpu
from jax.sharding import PartitionSpec as P

D = 8192
FF = 14336
BLK = 128
NVAL = 4
TOK = 512
VAL = 512
AXES = ("dp", "seq")
HA = FF // 2
HG = D // 2
C1 = 3840
C2A = HA - C1
C2G = 512
C2 = C2A + C2G
C3G = HG - C2G
IDW = 128
C3 = C3G + IDW
MASKS = ((1, 3), (3, 1))


def coords(i):
    dp, seq = divmod(i, 8)
    c = dp % 2
    z = (dp // 2) % 4
    x = (seq // 4) * 2 + dp // 8
    return {"x": x, "y": seq % 4, "z": z, "c": c}


def index(p):
    dp = ((p["x"] % 2) * 4 + p["z"]) * 2 + p["c"]
    return dp * 8 + (p["x"] // 2) * 4 + p["y"]


def ring_pairs(axes, step):
    pairs = []
    for i in range(128):
        p = coords(i)
        for axis in axes:
            p[axis] ^= MASKS[p["c"]][step]
        pairs.append((i, index(p)))
    return pairs


def core_pairs():
    pairs = []
    for i in range(128):
        p = coords(i)
        p["c"] ^= 1
        pairs.append((i, index(p)))
    return pairs


def swap(x):
    return lax.ppermute(x, AXES, core_pairs())


def hop(x, axes, step):
    return lax.ppermute(x, AXES, ring_pairs(axes, step))


def double(x, axis, step):
    return jnp.stack([x, hop(x, axis, step)])


def pin(x):
    return pltpu.with_memory_space_constraint(x, pltpu.VMEM)


def gate(xs, *deps, space=pltpu.VMEM):
    n = len(xs)
    anyspec = pl.BlockSpec(memory_space=pl.ANY)
    return pl.pallas_call(
        lambda *refs: None,
        in_specs=[anyspec] * (n + len(deps)),
        out_specs=[anyspec] * n,
        out_shape=[jax.ShapeDtypeStruct(x.shape, x.dtype) for x in xs],
        input_output_aliases={i: i for i in range(n)},
        compiler_params=pltpu.CompilerParams(vmem_limit_bytes=1 << 20),
        cost_estimate=pl.CostEstimate(flops=0, bytes_accessed=0, transcendentals=0),
    )(*[pltpu.with_memory_space_constraint(x, space) for x in xs], *deps)


def nt(a, b):
    return lax.dot_general(a, b, (((1,), (1,)), ((), ())), preferred_element_type=jnp.float32)


def self_add(acc, ref):
    acc[0:256, :] += nt(ref[256:512, :], ref[0:256, :])
    acc[256:384, 0:128] += nt(ref[128:256, :], ref[0:128, :])
    acc[384:512, 0:128] += nt(ref[384:512, :], ref[256:384, :])


def self_first_body(x_ref, dep_ref, out_ref):
    @pl.when(pl.program_id(0) == 0)
    def _():
        out_ref[...] = jnp.zeros_like(out_ref)

    self_add(out_ref, x_ref)


def self_last_body(x_ref, first_ref, dep_ref, out_ref, acc, *, steps):
    i = pl.program_id(0)

    @pl.when(i == 0)
    def _():
        acc[...] = jnp.zeros_like(acc)

    self_add(acc, x_ref)

    @pl.when(i == steps - 1)
    def _():
        k = first_ref[...] * acc[...]
        rows = lax.broadcasted_iota(jnp.int32, (4, 4), 0)
        cols = lax.broadcasted_iota(jnp.int32, (4, 4), 1)
        out = jnp.zeros((4, 4), jnp.float32)
        spots = (
            (2, 0, 0, 0), (2, 1, 0, 128), (3, 0, 128, 0), (3, 1, 128, 128),
            (1, 0, 256, 0), (3, 2, 384, 0),
        )
        for b, c, r0, c0 in spots:
            s = jnp.sum(k[r0:r0 + 128, c0:c0 + 128])
            out = jnp.where((rows == b) & (cols == c), s, out)
        out_ref[...] = out / (float(BLK) * math.sqrt(float(FF) * float(D)))


KC = 2048


def self_call(x, dep, first=None):
    width = x.shape[1]
    half = pl.BlockSpec((512, 256), lambda i: (0, 0))
    anyspec = pl.BlockSpec(memory_space=pl.ANY)
    args = [x] + ([] if first is None else [first]) + [dep]
    body = self_first_body
    if first is not None:
        body = functools.partial(self_last_body, steps=width // KC)
    return pl.pallas_call(
        body,
        grid=(width // KC,),
        in_specs=[pl.BlockSpec((TOK, KC), lambda i: (0, i))]
        + ([] if first is None else [half]) + [anyspec],
        out_specs=half if first is None else pl.BlockSpec((4, 4), lambda i: (0, 0)),
        out_shape=jax.ShapeDtypeStruct((512, 256) if first is None else (4, 4), jnp.float32),
        scratch_shapes=[] if first is None else [pltpu.VMEM((512, 256), jnp.float32)],
        compiler_params=pltpu.CompilerParams(vmem_limit_bytes=16 << 20),
        cost_estimate=pl.CostEstimate(
            flops=2 * 512 * 256 * width, bytes_accessed=2 * TOK * width, transcendentals=0
        ),
    )(*args)


RUNS = ("y", "z", "x")
STEP5 = ("z", "x", "y")
STEP6 = ("x", "y", "z")
WEIGHT = {"x": 4, "y": 2, "z": 1}


def place(part, k, s4):
    n = s4 * WEIGHT[RUNS[part]]
    if k in (1, 3):
        n += WEIGHT[STEP5[part]]
    if k in (2, 3):
        n += WEIGHT[STEP6[part]]
    return n


WIDTHS = (C1, C2, C3)
STARTS = (0, C1, C1 + C2)
ALLW = C1 + C2 + C3
FULL = (
    (("a", 0, 0, C1),),
    (("a", C1, 0, C2A), ("g", 0, C2A, C2G)),
    (("g", C2G, 0, C3G),),
)
SETAT = ((0, 0, 0), (2048, 1792, 1792))
SETW = ((2048, 1792, 1792), (C1 - 2048, C2 - 1792, C3 - 1792))
SETS = (
    ((("a", 0, 0, 2048),), (("a", C1, 0, 1792),), (("g", C2G, 0, 1792),)),
    (
        (("a", 2048, 0, C1 - 2048),),
        (("a", C1 + 1792, 0, C2A - 1792), ("g", 0, C2A - 1792, C2G)),
        (("g", C2G + 1792, 0, C3G - 1792),),
    ),
)
SETMAX = 2048


class Train:
    def __init__(self, core_ref, acts, grads, half, parts, hbuf, sems):
        c = core_ref[0]
        o = c if half == 0 else 1 - c
        self.hbuf, self.todo = hbuf, []
        for part, segments in enumerate(parts):
            cps = []
            for i, (name, col, at, w) in enumerate(segments):
                src, step = (acts, HA) if name == "a" else (grads, HG)
                first = pl.multiple_of(o * step + col, 128)
                cps.append(pltpu.make_async_copy(
                    src.at[:, pl.ds(first, w)], hbuf.at[part, :, pl.ds(at, w)], sems.at[part, i]
                ))
            for cp in cps:
                cp.start()
            self.todo.append(cps)

    def wait(self, part):
        for cp in self.todo[part]:
            cp.wait()

    def get(self, part, at, w):
        return self.hbuf[part, :, at:at + w]


def cross_rows(part, segments, ks, pieces, train, ca, cg):
    train.wait(part)
    for name, _, at, w in segments:
        acc = ca if name == "a" else cg
        rows = [p[:, :, :, at:at + w].reshape(128, w) for p in pieces]
        x = nt(jnp.concatenate(rows, axis=0), train.get(part, at, w))
        for i, k in enumerate(ks):
            for s4 in range(2):
                r = i * 128 + s4 * 64
                acc[place(part, k, s4)] += x[r:r + 64].reshape(8, 8, TOK)


def val_rows(core_ref, blocks, ka, kg, name, seen):
    even = jnp.concatenate([x[:32] for x in blocks], axis=0)
    late = jnp.concatenate(blocks[4:], axis=0)
    y = nt(jnp.where(core_ref[0] == 0, even, late), jnp.concatenate(blocks, axis=0))
    acc = ka if name == "a" else kg
    if name in seen:
        acc[...] += y
    else:
        acc[...] = y
        seen.add(name)


def early_body(core_ref, acts, grads, dep_ref, *refs):
    own = [refs[p * 2:p * 2 + 2] for p in range(3)]
    ca, cg, tok, hbuf, sems = refs[6:]
    train = Train(core_ref, acts, grads, 0, FULL, hbuf, sems)
    tok[...] = jnp.zeros_like(tok)
    ca[...] = jnp.zeros_like(ca)
    cg[...] = jnp.zeros_like(cg)
    for part in range(3):
        cross_rows(part, FULL[part], (0, 1), own[part], train, ca, cg)


def bring(moves, sems):
    cps = [pltpu.make_async_copy(x, y, sems.at[i]) for i, (x, y) in enumerate(moves)]
    for cp in cps:
        cp.start()
    return cps


def late_own_body(core_ref, acts, grads, *refs, which):
    pieces = [refs[p * 3:p * 3 + 3] for p in range(3)]
    n = 2 + 2 * which
    ins, refs = refs[9:9 + n], refs[9 + n:]
    ca, cg, ka, kg = refs[:4]
    if which:
        ids = refs[4]
    hbuf, sems, pbuf, psems, asems = refs[4 + which:]
    sums = bring(list(zip(ins, (ca, cg, ka, kg))), asems)
    todo = []
    for part in range(3):
        x, a1, last = pieces[part]
        w = SETW[which][part]
        cols = pl.ds(SETAT[which][part], w)
        srcs = (x.at[:, :, :, cols], a1.at[:, :, :, cols], last.at[0], last.at[1])
        todo.append(bring(
            [(src, pbuf.at[part, k, :, :, :, pl.ds(0, w)]) for k, src in enumerate(srcs)],
            psems.at[part],
        ))
    train = Train(core_ref, acts, grads, 0, SETS[which], hbuf, sems)
    seen = {"a", "g"} if which else set()
    for part in range(3):
        for cp in todo[part]:
            cp.wait()
        if part == 0:
            for cp in sums:
                cp.wait()

        def blocks(at, w):
            out = [None] * 8
            for k in range(4):
                for s4 in range(2):
                    out[place(part, k, s4)] = pbuf[part, k, s4, :, :, at:at + w].reshape(64, w)
            return out

        for name, _, at, w in SETS[which][part]:
            val_rows(core_ref, blocks(at, w), ka, kg, name, seen)
        if which and part == 2:
            for b, x in enumerate(blocks(SETW[1][2] - IDW, IDW)):
                ids[b * 64:b * 64 + 64, :] = x.astype(jnp.float32)
        cross_rows(
            part, SETS[which][part], (2, 3), [pbuf.at[part, 2], pbuf.at[part, 3]], train, ca, cg
        )


def late_other_body(core_ref, acts, grads, o0, o1, o2, o3, o4, ain, gin, k1, k2, *refs, which):
    c = core_ref[0]
    lasts = (o2, o3, o4)
    if which:
        idin, raw_ref, norm_ref, hbuf, sems, vbuf, acc_a, acc_g, ka, kg, ids, vsems, asems = refs
        extra = [(idin, ids)]
    else:
        acc_a, acc_g, ka, kg, tok, hbuf, sems, vbuf, vsems, asems = refs
        tok[...] = jnp.zeros_like(tok)
        extra = []
    sums = bring([(ain, acc_a), (gin, acc_g), (k1, ka), (k2, kg)] + extra, asems)
    todo = []
    for part in range(3):
        w = SETW[which][part]
        cols = pl.ds(STARTS[part] + SETAT[which][part], w)
        todo.append(bring(
            [
                (
                    o.at[s4, :, :, cols] if k < 2 else o.at[s4],
                    vbuf.at[part, :, place(part, k, s4), :, pl.ds(0, w)],
                )
                for k, o in enumerate((o0, o1, lasts[part].at[0], lasts[part].at[1]))
                for s4 in range(2)
            ],
            vsems.at[part],
        ))
    train = Train(core_ref, acts, grads, 1, SETS[which], hbuf, sems)
    seen = {"a", "g"}
    for part in range(3):
        for cp in todo[part]:
            cp.wait()
        if part == 0:
            for cp in sums:
                cp.wait()
        for name, _, at, w in SETS[which][part]:
            blocks = [vbuf[part, b, :, :, at:at + w].reshape(64, w) for b in range(8)]
            val_rows(core_ref, blocks, ka, kg, name, seen)
        train.wait(part)
        for name, _, at, w in SETS[which][part]:
            acc = acc_a if name == "a" else acc_g
            rows = vbuf[part, :, :, :, at:at + w].reshape(VAL, w)
            acc[...] += nt(rows, train.get(part, at, w)).reshape(8, 8, 8, TOK)
    if not which:
        return

    cross = acc_a[...].reshape(VAL, TOK) * acc_g[...].reshape(VAL, TOK)
    kern = ka[...] * kg[...]
    all_ids = ids[...]
    row_ids = jnp.transpose(all_ids)[0:1, :]
    even = jnp.concatenate([all_ids[b * 64:b * 64 + 32] for b in range(8)], axis=0)
    half_ids = jnp.where(c == 0, even, all_ids[256:512])
    for v in range(NVAL):
        keep = jnp.where(all_ids == float(v), 1.0, 0.0)
        keep = jnp.concatenate([keep] * 4, axis=1)
        raw_ref[v:v + 1, :] = jnp.sum(cross * keep, axis=0, keepdims=True)
        keep = jnp.where(half_ids == float(v), 1.0, 0.0)
        keep = jnp.concatenate([keep] * 4, axis=1)
        part = jnp.sum(kern * keep, axis=0, keepdims=True)
        part = jnp.sum(jnp.where(row_ids == float(v), part, 0.0))
        norm_ref[v:v + 1, :] = jnp.full((1, 128), part, jnp.float32)


ACC = jax.ShapeDtypeStruct((8, 8, 8, TOK), jnp.float32)
KERN = jax.ShapeDtypeStruct((VAL // 2, VAL), jnp.float32)


TOKEN = jax.ShapeDtypeStruct((8, 128), jnp.float32)
IDS = jax.ShapeDtypeStruct((VAL, IDW), jnp.float32)


def local_call(body, core, acts, grads, args, outs, flops, width, scratch=(), pinned=(), mib=26):
    vmem = pl.BlockSpec(memory_space=pltpu.VMEM)
    anyspec = pl.BlockSpec(memory_space=pl.ANY)
    return pl.pallas_call(
        body,
        in_specs=[pl.BlockSpec(memory_space=pltpu.SMEM)] + [anyspec] * 2
        + [vmem if i in pinned else anyspec for i in range(len(args))],
        out_specs=[vmem] * len(outs),
        out_shape=outs,
        scratch_shapes=[
            pltpu.VMEM((3, TOK, width), jnp.bfloat16),
            pltpu.SemaphoreType.DMA((3, 2)),
        ] + list(scratch),
        compiler_params=pltpu.CompilerParams(vmem_limit_bytes=mib << 20),
        cost_estimate=pl.CostEstimate(
            flops=flops, bytes_accessed=TOK * (FF + D), transcendentals=0
        ),
    )(core, acts, grads, *[pin(x) if i in pinned else x for i, x in enumerate(args)])


def shards(hidden_acts, out_grads, val_acts, val_grads, val_ids):
    hidden_acts = pltpu.with_memory_space_constraint(hidden_acts, pltpu.HBM)
    out_grads = pltpu.with_memory_space_constraint(out_grads, pltpu.HBM)
    core = lax.axis_index("dp") % 2
    first = core == 0
    idcol = jnp.broadcast_to(val_ids[:, None].astype(jnp.bfloat16), (4, IDW))
    halves = [
        jnp.concatenate(
            [val_acts[:, h * HA:(h + 1) * HA], val_grads[:, h * HG:(h + 1) * HG], idcol], axis=1
        )
        for h in range(2)
    ]
    keep = jnp.where(first, halves[0], halves[1])
    got = swap(jnp.where(first, halves[1], halves[0]))
    rows = jnp.concatenate([jnp.where(first, keep, got), jnp.where(first, got, keep)], axis=0)

    near = [
        hop(rows, [a for a in "xyz" if n & WEIGHT[a]], 0) for n in (1, 2, 4, 3, 5, 6, 7)
    ]
    rows = jnp.stack([rows, near[0], near[1], near[3], near[2], near[4], near[5], near[6]])
    sg = self_call(out_grads, rows)
    x = [double(rows[..., s:s + w], RUNS[j], 1) for j, (s, w) in enumerate(zip(STARTS, WIDTHS))]
    x = gate(x, sg)
    block_gram = self_call(hidden_acts, x[1], sg)
    a1 = [hop(x[j], STEP5[j], 1) for j in range(3)]
    o0 = swap(gate([jnp.concatenate(x, axis=-1)], sg)[0])
    pair = gate([jnp.stack([x[j], a1[j]]) for j in range(3)], block_gram, o0)
    last = [
        [hop(pair[j][..., a:a + w], STEP6[j], 1) for j, (a, w) in enumerate(zip(at, width))]
        for at, width in zip(SETAT, SETW)
    ]
    o1 = swap(gate([jnp.concatenate(a1, axis=-1)], sg)[0])
    call = functools.partial(
        local_call, core=core.reshape(1).astype(jnp.int32), acts=hidden_acts, grads=out_grads
    )
    unit = 512 * (HA + HG)
    ca, cg, tok = call(
        early_body, args=[block_gram] + [y for j in range(3) for y in (x[j], a1[j])],
        outs=[ACC, ACC, TOKEN], flops=512 * unit, width=C1, pinned=range(1, 7), mib=28,
    )
    sums = [ca, cg]
    for which in range(2):
        got = [gate([y], tok, *([] if which else [o1]))[0] for y in last[which]]
        swapped = [swap(y) for y in got]
        sums = call(
            functools.partial(late_own_body, which=which),
            args=[y for j in range(3) for y in (x[j], a1[j], got[j])] + list(sums),
            outs=[ACC, ACC, KERN, KERN] + [IDS] * which, flops=512 * unit, width=SETMAX,
            scratch=[
                pltpu.VMEM((3, 4, 2, 8, 8, SETMAX), jnp.bfloat16),
                pltpu.SemaphoreType.DMA((3, 4)),
                pltpu.SemaphoreType.DMA((4,)),
            ],
        )
        outs = [ACC, ACC, KERN, KERN, TOKEN]
        scratch = [pltpu.VMEM((3, 8, 8, 8, SETMAX), jnp.bfloat16)]
        if which:
            outs = [
                jax.ShapeDtypeStruct((NVAL, TOK), jnp.float32),
                jax.ShapeDtypeStruct((NVAL, 128), jnp.float32),
            ]
            scratch += [pltpu.VMEM(a.shape, a.dtype) for a in (ACC, ACC, KERN, KERN, IDS)]
        outs = call(
            functools.partial(late_other_body, which=which),
            args=[o0, o1] + swapped + list(sums), outs=outs, flops=768 * unit, width=SETMAX,
            scratch=scratch + [
                pltpu.SemaphoreType.DMA((3, 8)),
                pltpu.SemaphoreType.DMA((5,)),
            ],
        )
        sums, tok = outs[:4], outs[-1]
    raw, norm = outs
    norm = norm + swap(norm)
    token_scores = raw * lax.rsqrt(norm[:, :1] + 1e-06)
    return (token_scores, block_gram)


def solution(mesh):
    return jax.shard_map(
        shards,
        mesh=mesh,
        in_specs=(
            P(AXES, None),
            P(AXES, None),
            P(AXES, None),
            P(AXES, None),
            P(AXES),
        ),
        out_specs=(P(None, AXES), P(AXES, None)),
        check_vma=False,
    )
```

```python
import functools
import math

import jax
import jax.numpy as jnp
from jax import lax
from jax.experimental import pallas as pl
from jax.experimental.pallas import tpu as pltpu
from jax.sharding import PartitionSpec as P

D = 8192
FF = 14336
BLK = 128
NVAL = 4
TOK = 512
VAL = 512
AXES = ("dp", "seq")
HA = FF // 2
HG = D // 2
C1 = 3840
C2A = HA - C1
C2G = 512
C2 = C2A + C2G
C3G = HG - C2G
IDW = 128
C3 = C3G + IDW
MASKS = ((1, 3), (3, 1))


def coords(i):
    dp, seq = divmod(i, 8)
    c = dp % 2
    z = (dp // 2) % 4
    x = (seq // 4) * 2 + dp // 8
    return {"x": x, "y": seq % 4, "z": z, "c": c}


def index(p):
    dp = ((p["x"] % 2) * 4 + p["z"]) * 2 + p["c"]
    return dp * 8 + (p["x"] // 2) * 4 + p["y"]


def ring_pairs(axes, step):
    pairs = []
    for i in range(128):
        p = coords(i)
        for axis in axes:
            p[axis] ^= MASKS[p["c"]][step]
        pairs.append((i, index(p)))
    return pairs


def core_pairs():
    pairs = []
    for i in range(128):
        p = coords(i)
        p["c"] ^= 1
        pairs.append((i, index(p)))
    return pairs


def swap(x):
    return lax.ppermute(x, AXES, core_pairs())


def hop(x, axes, step):
    return lax.ppermute(x, AXES, ring_pairs(axes, step))


def double(x, axis, step):
    return jnp.stack([x, hop(x, axis, step)])


def pin(x):
    return pltpu.with_memory_space_constraint(x, pltpu.VMEM)


def gate(xs, *deps, space=pltpu.VMEM):
    n = len(xs)
    anyspec = pl.BlockSpec(memory_space=pl.ANY)
    return pl.pallas_call(
        lambda *refs: None,
        in_specs=[anyspec] * (n + len(deps)),
        out_specs=[anyspec] * n,
        out_shape=[jax.ShapeDtypeStruct(x.shape, x.dtype) for x in xs],
        input_output_aliases={i: i for i in range(n)},
        compiler_params=pltpu.CompilerParams(vmem_limit_bytes=1 << 20),
        cost_estimate=pl.CostEstimate(flops=0, bytes_accessed=0, transcendentals=0),
    )(*[pltpu.with_memory_space_constraint(x, space) for x in xs], *deps)


def nt(a, b):
    return lax.dot_general(a, b, (((1,), (1,)), ((), ())), preferred_element_type=jnp.float32)


def self_add(acc, ref):
    acc[0:256, :] += nt(ref[256:512, :], ref[0:256, :])
    acc[256:384, 0:128] += nt(ref[128:256, :], ref[0:128, :])
    acc[384:512, 0:128] += nt(ref[384:512, :], ref[256:384, :])


def self_first_body(x_ref, dep_ref, out_ref):
    @pl.when(pl.program_id(0) == 0)
    def _():
        out_ref[...] = jnp.zeros_like(out_ref)

    self_add(out_ref, x_ref)


def self_last_body(x_ref, first_ref, dep_ref, out_ref, acc, *, steps):
    i = pl.program_id(0)

    @pl.when(i == 0)
    def _():
        acc[...] = jnp.zeros_like(acc)

    self_add(acc, x_ref)

    @pl.when(i == steps - 1)
    def _():
        k = first_ref[...] * acc[...]
        rows = lax.broadcasted_iota(jnp.int32, (4, 4), 0)
        cols = lax.broadcasted_iota(jnp.int32, (4, 4), 1)
        out = jnp.zeros((4, 4), jnp.float32)
        spots = (
            (2, 0, 0, 0), (2, 1, 0, 128), (3, 0, 128, 0), (3, 1, 128, 128),
            (1, 0, 256, 0), (3, 2, 384, 0),
        )
        for b, c, r0, c0 in spots:
            s = jnp.sum(k[r0:r0 + 128, c0:c0 + 128])
            out = jnp.where((rows == b) & (cols == c), s, out)
        out_ref[...] = out / (float(BLK) * math.sqrt(float(FF) * float(D)))


KC = 2048


def self_call(x, dep, first=None):
    width = x.shape[1]
    half = pl.BlockSpec((512, 256), lambda i: (0, 0))
    anyspec = pl.BlockSpec(memory_space=pl.ANY)
    args = [x] + ([] if first is None else [first]) + [dep]
    body = self_first_body
    if first is not None:
        body = functools.partial(self_last_body, steps=width // KC)
    return pl.pallas_call(
        body,
        grid=(width // KC,),
        in_specs=[pl.BlockSpec((TOK, KC), lambda i: (0, i))]
        + ([] if first is None else [half]) + [anyspec],
        out_specs=half if first is None else pl.BlockSpec((4, 4), lambda i: (0, 0)),
        out_shape=jax.ShapeDtypeStruct((512, 256) if first is None else (4, 4), jnp.float32),
        scratch_shapes=[] if first is None else [pltpu.VMEM((512, 256), jnp.float32)],
        compiler_params=pltpu.CompilerParams(vmem_limit_bytes=16 << 20),
        cost_estimate=pl.CostEstimate(
            flops=2 * 512 * 256 * width, bytes_accessed=2 * TOK * width, transcendentals=0
        ),
    )(*args)


RUNS = ("y", "z", "x")
STEP5 = ("z", "x", "y")
STEP6 = ("x", "y", "z")
WEIGHT = {"x": 4, "y": 2, "z": 1}


def place(part, k, s4):
    n = s4 * WEIGHT[RUNS[part]]
    if k in (1, 3):
        n += WEIGHT[STEP5[part]]
    if k in (2, 3):
        n += WEIGHT[STEP6[part]]
    return n


WIDTHS = (C1, C2, C3)
STARTS = (0, C1, C1 + C2)
ALLW = C1 + C2 + C3
FULL = (
    (("a", 0, 0, C1),),
    (("a", C1, 0, C2A), ("g", 0, C2A, C2G)),
    (("g", C2G, 0, C3G),),
)
SETAT = ((0, 0, 0), (2048, 1792, 1792))
SETW = ((2048, 1792, 1792), (C1 - 2048, C2 - 1792, C3 - 1792))
SETS = (
    ((("a", 0, 0, 2048),), (("a", C1, 0, 1792),), (("g", C2G, 0, 1792),)),
    (
        (("a", 2048, 0, C1 - 2048),),
        (("a", C1 + 1792, 0, C2A - 1792), ("g", 0, C2A - 1792, C2G)),
        (("g", C2G + 1792, 0, C3G - 1792),),
    ),
)
SETMAX = 2048


class Train:
    def __init__(self, core_ref, acts, grads, half, parts, hbuf, sems):
        c = core_ref[0]
        o = c if half == 0 else 1 - c
        self.hbuf, self.todo = hbuf, []
        for part, segments in enumerate(parts):
            cps = []
            for i, (name, col, at, w) in enumerate(segments):
                src, step = (acts, HA) if name == "a" else (grads, HG)
                first = pl.multiple_of(o * step + col, 128)
                cps.append(pltpu.make_async_copy(
                    src.at[:, pl.ds(first, w)], hbuf.at[part, :, pl.ds(at, w)], sems.at[part, i]
                ))
            for cp in cps:
                cp.start()
            self.todo.append(cps)

    def wait(self, part):
        for cp in self.todo[part]:
            cp.wait()

    def get(self, part, at, w):
        return self.hbuf[part, :, at:at + w]


def cross_rows(part, segments, ks, pieces, train, ca, cg):
    train.wait(part)
    for name, _, at, w in segments:
        acc = ca if name == "a" else cg
        rows = [p[:, :, :, at:at + w].reshape(128, w) for p in pieces]
        x = nt(jnp.concatenate(rows, axis=0), train.get(part, at, w))
        for i, k in enumerate(ks):
            for s4 in range(2):
                r = i * 128 + s4 * 64
                acc[place(part, k, s4)] += x[r:r + 64].reshape(8, 8, TOK)


def val_rows(core_ref, blocks, ka, kg, name, seen):
    even = jnp.concatenate([x[:32] for x in blocks], axis=0)
    late = jnp.concatenate(blocks[4:], axis=0)
    y = nt(jnp.where(core_ref[0] == 0, even, late), jnp.concatenate(blocks, axis=0))
    acc = ka if name == "a" else kg
    if name in seen:
        acc[...] += y
    else:
        acc[...] = y
        seen.add(name)


def early_body(core_ref, acts, grads, dep_ref, *refs):
    own = [refs[p * 2:p * 2 + 2] for p in range(3)]
    ca, cg, tok, hbuf, sems = refs[6:]
    train = Train(core_ref, acts, grads, 0, FULL, hbuf, sems)
    tok[...] = jnp.zeros_like(tok)
    ca[...] = jnp.zeros_like(ca)
    cg[...] = jnp.zeros_like(cg)
    for part in range(3):
        cross_rows(part, FULL[part], (0, 1), own[part], train, ca, cg)


def bring(moves, sems):
    cps = [pltpu.make_async_copy(x, y, sems.at[i]) for i, (x, y) in enumerate(moves)]
    for cp in cps:
        cp.start()
    return cps


def late_own_body(core_ref, acts, grads, *refs, which):
    pieces = [refs[p * 3:p * 3 + 3] for p in range(3)]
    n = 2 + 2 * which
    ins, refs = refs[9:9 + n], refs[9 + n:]
    ca, cg, ka, kg = refs[:4]
    if which:
        ids = refs[4]
    hbuf, sems, pbuf, psems, asems = refs[4 + which:]
    sums = bring(list(zip(ins, (ca, cg, ka, kg))), asems)
    todo = []
    for part in range(3):
        x, a1, last = pieces[part]
        w = SETW[which][part]
        cols = pl.ds(SETAT[which][part], w)
        srcs = (x.at[:, :, :, cols], a1.at[:, :, :, cols], last.at[0], last.at[1])
        todo.append(bring(
            [(src, pbuf.at[part, k, :, :, :, pl.ds(0, w)]) for k, src in enumerate(srcs)],
            psems.at[part],
        ))
    train = Train(core_ref, acts, grads, 0, SETS[which], hbuf, sems)
    seen = {"a", "g"} if which else set()
    for part in range(3):
        for cp in todo[part]:
            cp.wait()
        if part == 0:
            for cp in sums:
                cp.wait()

        def blocks(at, w):
            out = [None] * 8
            for k in range(4):
                for s4 in range(2):
                    out[place(part, k, s4)] = pbuf[part, k, s4, :, :, at:at + w].reshape(64, w)
            return out

        for name, _, at, w in SETS[which][part]:
            val_rows(core_ref, blocks(at, w), ka, kg, name, seen)
        if which and part == 2:
            for b, x in enumerate(blocks(SETW[1][2] - IDW, IDW)):
                ids[b * 64:b * 64 + 64, :] = x.astype(jnp.float32)
        cross_rows(
            part, SETS[which][part], (2, 3), [pbuf.at[part, 2], pbuf.at[part, 3]], train, ca, cg
        )


def late_other_body(core_ref, acts, grads, o0, o1, o2, o3, o4, ain, gin, k1, k2, *refs, which):
    c = core_ref[0]
    lasts = (o2, o3, o4)
    if which:
        idin, raw_ref, norm_ref, hbuf, sems, vbuf, acc_a, acc_g, ka, kg, ids, vsems, asems = refs
        extra = [(idin, ids)]
    else:
        acc_a, acc_g, ka, kg, tok, hbuf, sems, vbuf, vsems, asems = refs
        tok[...] = jnp.zeros_like(tok)
        extra = []
    sums = bring([(ain, acc_a), (gin, acc_g), (k1, ka), (k2, kg)] + extra, asems)
    todo = []
    for part in range(3):
        w = SETW[which][part]
        cols = pl.ds(STARTS[part] + SETAT[which][part], w)
        todo.append(bring(
            [
                (
                    o.at[s4, :, :, cols] if k < 2 else o.at[s4],
                    vbuf.at[part, :, place(part, k, s4), :, pl.ds(0, w)],
                )
                for k, o in enumerate((o0, o1, lasts[part].at[0], lasts[part].at[1]))
                for s4 in range(2)
            ],
            vsems.at[part],
        ))
    train = Train(core_ref, acts, grads, 1, SETS[which], hbuf, sems)
    seen = {"a", "g"}
    for part in range(3):
        for cp in todo[part]:
            cp.wait()
        if part == 0:
            for cp in sums:
                cp.wait()
        for name, _, at, w in SETS[which][part]:
            blocks = [vbuf[part, b, :, :, at:at + w].reshape(64, w) for b in range(8)]
            val_rows(core_ref, blocks, ka, kg, name, seen)
        train.wait(part)
        for name, _, at, w in SETS[which][part]:
            acc = acc_a if name == "a" else acc_g
            rows = vbuf[part, :, :, :, at:at + w].reshape(VAL, w)
            acc[...] += nt(rows, train.get(part, at, w)).reshape(8, 8, 8, TOK)
    if not which:
        return

    cross = acc_a[...].reshape(VAL, TOK) * acc_g[...].reshape(VAL, TOK)
    kern = ka[...] * kg[...]
    all_ids = ids[...]
    row_ids = jnp.transpose(all_ids)[0:1, :]
    even = jnp.concatenate([all_ids[b * 64:b * 64 + 32] for b in range(8)], axis=0)
    half_ids = jnp.where(c == 0, even, all_ids[256:512])
    for v in range(NVAL):
        keep = jnp.where(all_ids == float(v), 1.0, 0.0)
        keep = jnp.concatenate([keep] * 4, axis=1)
        raw_ref[v:v + 1, :] = jnp.sum(cross * keep, axis=0, keepdims=True)
        keep = jnp.where(half_ids == float(v), 1.0, 0.0)
        keep = jnp.concatenate([keep] * 4, axis=1)
        part = jnp.sum(kern * keep, axis=0, keepdims=True)
        part = jnp.sum(jnp.where(row_ids == float(v), part, 0.0))
        norm_ref[v:v + 1, :] = jnp.full((1, 128), part, jnp.float32)


ACC = jax.ShapeDtypeStruct((8, 8, 8, TOK), jnp.float32)
KERN = jax.ShapeDtypeStruct((VAL // 2, VAL), jnp.float32)


TOKEN = jax.ShapeDtypeStruct((8, 128), jnp.float32)
IDS = jax.ShapeDtypeStruct((VAL, IDW), jnp.float32)


def local_call(body, core, acts, grads, args, outs, flops, width, scratch=(), pinned=(), mib=26):
    vmem = pl.BlockSpec(memory_space=pltpu.VMEM)
    anyspec = pl.BlockSpec(memory_space=pl.ANY)
    return pl.pallas_call(
        body,
        in_specs=[pl.BlockSpec(memory_space=pltpu.SMEM)] + [anyspec] * 2
        + [vmem if i in pinned else anyspec for i in range(len(args))],
        out_specs=[vmem] * len(outs),
        out_shape=outs,
        scratch_shapes=[
            pltpu.VMEM((3, TOK, width), jnp.bfloat16),
            pltpu.SemaphoreType.DMA((3, 2)),
        ] + list(scratch),
        compiler_params=pltpu.CompilerParams(vmem_limit_bytes=mib << 20),
        cost_estimate=pl.CostEstimate(
            flops=flops, bytes_accessed=TOK * (FF + D), transcendentals=0
        ),
    )(core, acts, grads, *[pin(x) if i in pinned else x for i, x in enumerate(args)])


def shards(hidden_acts, out_grads, val_acts, val_grads, val_ids):
    hidden_acts = pltpu.with_memory_space_constraint(hidden_acts, pltpu.HBM)
    out_grads = pltpu.with_memory_space_constraint(out_grads, pltpu.HBM)
    core = lax.axis_index("dp") % 2
    first = core == 0
    idcol = jnp.broadcast_to(val_ids[:, None].astype(jnp.bfloat16), (4, IDW))
    halves = [
        jnp.concatenate(
            [val_acts[:, h * HA:(h + 1) * HA], val_grads[:, h * HG:(h + 1) * HG], idcol], axis=1
        )
        for h in range(2)
    ]
    keep = jnp.where(first, halves[0], halves[1])
    got = swap(jnp.where(first, halves[1], halves[0]))
    rows = jnp.concatenate([jnp.where(first, keep, got), jnp.where(first, got, keep)], axis=0)

    def send(block, n):
        return hop(block, [a for a in "xyz" if n & WEIGHT[a]], 0)

    near = {n: send(rows, n) for n in (1, 2, 4, 3)}
    (again,) = gate([rows], near[1])
    near.update({n: send(again, n) for n in (5, 6, 7)})
    rows = jnp.stack([rows] + [near[n] for n in range(1, 8)])
    x = [double(rows[..., s:s + w], RUNS[j], 1) for j, (s, w) in enumerate(zip(STARTS, WIDTHS))]
    sa = self_call(hidden_acts, x[1])
    a1 = [hop(x[j], STEP5[j], 1) for j in range(3)]
    o0 = swap(jnp.concatenate(x, axis=-1))
    pair = gate([jnp.stack([x[j], a1[j]]) for j in range(3)], sa, o0)
    last = [
        [hop(pair[j][..., a:a + w], STEP6[j], 1) for j, (a, w) in enumerate(zip(at, width))]
        for at, width in zip(SETAT, SETW)
    ]
    o1 = swap(gate([jnp.concatenate(a1, axis=-1)], pair[0])[0])
    call = functools.partial(
        local_call, core=core.reshape(1).astype(jnp.int32), acts=hidden_acts, grads=out_grads
    )
    unit = 512 * (HA + HG)
    ca, cg, tok = call(
        early_body, args=[sa] + [y for j in range(3) for y in (x[j], a1[j])],
        outs=[ACC, ACC, TOKEN], flops=512 * unit, width=C1, pinned=range(1, 7), mib=28,
    )
    block_gram = self_call(out_grads, tok, sa)
    tok = block_gram
    sums = [ca, cg]
    for which in range(2):
        got = [gate([y], tok, *([] if which else [o1]))[0] for y in last[which]]
        swapped = [swap(y) for y in got]
        sums = call(
            functools.partial(late_own_body, which=which),
            args=[y for j in range(3) for y in (x[j], a1[j], got[j])] + list(sums),
            outs=[ACC, ACC, KERN, KERN] + [IDS] * which, flops=512 * unit, width=SETMAX,
            scratch=[
                pltpu.VMEM((3, 4, 2, 8, 8, SETMAX), jnp.bfloat16),
                pltpu.SemaphoreType.DMA((3, 4)),
                pltpu.SemaphoreType.DMA((4,)),
            ],
        )
        outs = [ACC, ACC, KERN, KERN, TOKEN]
        scratch = [pltpu.VMEM((3, 8, 8, 8, SETMAX), jnp.bfloat16)]
        if which:
            outs = [
                jax.ShapeDtypeStruct((NVAL, TOK), jnp.float32),
                jax.ShapeDtypeStruct((NVAL, 128), jnp.float32),
            ]
            scratch += [pltpu.VMEM(a.shape, a.dtype) for a in (ACC, ACC, KERN, KERN, IDS)]
        outs = call(
            functools.partial(late_other_body, which=which),
            args=[o0, o1] + swapped + list(sums), outs=outs, flops=768 * unit, width=SETMAX,
            scratch=scratch + [
                pltpu.SemaphoreType.DMA((3, 8)),
                pltpu.SemaphoreType.DMA((5,)),
            ],
        )
        sums, tok = outs[:4], outs[-1]
    raw, norm = outs
    norm = norm + swap(norm)
    token_scores = raw * lax.rsqrt(norm[:, :1] + 1e-06)
    return (token_scores, block_gram)


def solution(mesh):
    return jax.shard_map(
        shards,
        mesh=mesh,
        in_specs=(
            P(AXES, None),
            P(AXES, None),
            P(AXES, None),
            P(AXES, None),
            P(AXES),
        ),
        out_specs=(P(None, AXES), P(AXES, None)),
        check_vma=False,
    )
```

```python
import functools
import math

import jax
import jax.numpy as jnp
from jax import lax
from jax.experimental import pallas as pl
from jax.experimental.pallas import tpu as pltpu
from jax.sharding import PartitionSpec as P

D = 8192
FF = 14336
BLK = 128
NVAL = 4
TOK = 512
VAL = 512
AXES = ("dp", "seq")
HA = FF // 2
HG = D // 2
C1 = 3840
C2A = HA - C1
C2G = 512
C2 = C2A + C2G
C3G = HG - C2G
IDW = 128
C3 = C3G + IDW
MASKS = ((1, 3), (3, 1))


def coords(i):
    dp, seq = divmod(i, 8)
    c = dp % 2
    z = (dp // 2) % 4
    x = (seq // 4) * 2 + dp // 8
    return {"x": x, "y": seq % 4, "z": z, "c": c}


def index(p):
    dp = ((p["x"] % 2) * 4 + p["z"]) * 2 + p["c"]
    return dp * 8 + (p["x"] // 2) * 4 + p["y"]


def ring_pairs(axes, step):
    pairs = []
    for i in range(128):
        p = coords(i)
        for axis in axes:
            p[axis] ^= MASKS[p["c"]][step]
        pairs.append((i, index(p)))
    return pairs


def core_pairs():
    pairs = []
    for i in range(128):
        p = coords(i)
        p["c"] ^= 1
        pairs.append((i, index(p)))
    return pairs


def swap(x):
    return lax.ppermute(x, AXES, core_pairs())


def hop(x, axes, step):
    return lax.ppermute(x, AXES, ring_pairs(axes, step))


def double(x, axis, step):
    return jnp.stack([x, hop(x, axis, step)])


def pin(x):
    return pltpu.with_memory_space_constraint(x, pltpu.VMEM)


def gate(xs, *deps, space=pltpu.VMEM):
    n = len(xs)
    anyspec = pl.BlockSpec(memory_space=pl.ANY)
    return pl.pallas_call(
        lambda *refs: None,
        in_specs=[anyspec] * (n + len(deps)),
        out_specs=[anyspec] * n,
        out_shape=[jax.ShapeDtypeStruct(x.shape, x.dtype) for x in xs],
        input_output_aliases={i: i for i in range(n)},
        compiler_params=pltpu.CompilerParams(vmem_limit_bytes=1 << 20),
        cost_estimate=pl.CostEstimate(flops=0, bytes_accessed=0, transcendentals=0),
    )(*[pltpu.with_memory_space_constraint(x, space) for x in xs], *deps)


def nt(a, b):
    return lax.dot_general(a, b, (((1,), (1,)), ((), ())), preferred_element_type=jnp.float32)


def self_add(acc, ref):
    acc[0:256, :] += nt(ref[256:512, :], ref[0:256, :])
    acc[256:384, 0:128] += nt(ref[128:256, :], ref[0:128, :])
    acc[384:512, 0:128] += nt(ref[384:512, :], ref[256:384, :])


def self_first_body(x_ref, dep_ref, out_ref):
    @pl.when(pl.program_id(0) == 0)
    def _():
        out_ref[...] = jnp.zeros_like(out_ref)

    self_add(out_ref, x_ref)


def self_last_body(x_ref, first_ref, dep_ref, out_ref, acc, *, steps):
    i = pl.program_id(0)

    @pl.when(i == 0)
    def _():
        acc[...] = jnp.zeros_like(acc)

    self_add(acc, x_ref)

    @pl.when(i == steps - 1)
    def _():
        k = first_ref[...] * acc[...]
        rows = lax.broadcasted_iota(jnp.int32, (4, 4), 0)
        cols = lax.broadcasted_iota(jnp.int32, (4, 4), 1)
        out = jnp.zeros((4, 4), jnp.float32)
        spots = (
            (2, 0, 0, 0), (2, 1, 0, 128), (3, 0, 128, 0), (3, 1, 128, 128),
            (1, 0, 256, 0), (3, 2, 384, 0),
        )
        for b, c, r0, c0 in spots:
            s = jnp.sum(k[r0:r0 + 128, c0:c0 + 128])
            out = jnp.where((rows == b) & (cols == c), s, out)
        out_ref[...] = out / (float(BLK) * math.sqrt(float(FF) * float(D)))


KC = 2048


def self_call(x, dep, first=None):
    width = x.shape[1]
    half = pl.BlockSpec((512, 256), lambda i: (0, 0))
    anyspec = pl.BlockSpec(memory_space=pl.ANY)
    args = [x] + ([] if first is None else [first]) + [dep]
    body = self_first_body
    if first is not None:
        body = functools.partial(self_last_body, steps=width // KC)
    return pl.pallas_call(
        body,
        grid=(width // KC,),
        in_specs=[pl.BlockSpec((TOK, KC), lambda i: (0, i))]
        + ([] if first is None else [half]) + [anyspec],
        out_specs=half if first is None else pl.BlockSpec((4, 4), lambda i: (0, 0)),
        out_shape=jax.ShapeDtypeStruct((512, 256) if first is None else (4, 4), jnp.float32),
        scratch_shapes=[] if first is None else [pltpu.VMEM((512, 256), jnp.float32)],
        compiler_params=pltpu.CompilerParams(vmem_limit_bytes=16 << 20),
        cost_estimate=pl.CostEstimate(
            flops=2 * 512 * 256 * width, bytes_accessed=2 * TOK * width, transcendentals=0
        ),
    )(*args)


RUNS = ("y", "z", "x")
STEP5 = ("z", "x", "y")
STEP6 = ("x", "y", "z")
WEIGHT = {"x": 4, "y": 2, "z": 1}


def place(part, k, s4):
    n = s4 * WEIGHT[RUNS[part]]
    if k in (1, 3):
        n += WEIGHT[STEP5[part]]
    if k in (2, 3):
        n += WEIGHT[STEP6[part]]
    return n


WIDTHS = (C1, C2, C3)
STARTS = (0, C1, C1 + C2)
ALLW = C1 + C2 + C3
FULL = (
    (("a", 0, 0, C1),),
    (("a", C1, 0, C2A), ("g", 0, C2A, C2G)),
    (("g", C2G, 0, C3G),),
)
SETAT = ((0, 0, 0), (2048, 1792, 1792))
SETW = ((2048, 1792, 1792), (C1 - 2048, C2 - 1792, C3 - 1792))
SETS = (
    ((("a", 0, 0, 2048),), (("a", C1, 0, 1792),), (("g", C2G, 0, 1792),)),
    (
        (("a", 2048, 0, C1 - 2048),),
        (("a", C1 + 1792, 0, C2A - 1792), ("g", 0, C2A - 1792, C2G)),
        (("g", C2G + 1792, 0, C3G - 1792),),
    ),
)
SETMAX = 2048


class Train:
    def __init__(self, core_ref, acts, grads, half, parts, hbuf, sems):
        c = core_ref[0]
        o = c if half == 0 else 1 - c
        self.hbuf, self.todo = hbuf, []
        for part, segments in enumerate(parts):
            cps = []
            for i, (name, col, at, w) in enumerate(segments):
                src, step = (acts, HA) if name == "a" else (grads, HG)
                first = pl.multiple_of(o * step + col, 128)
                cps.append(pltpu.make_async_copy(
                    src.at[:, pl.ds(first, w)], hbuf.at[part, :, pl.ds(at, w)], sems.at[part, i]
                ))
            for cp in cps:
                cp.start()
            self.todo.append(cps)

    def wait(self, part):
        for cp in self.todo[part]:
            cp.wait()

    def get(self, part, at, w):
        return self.hbuf[part, :, at:at + w]


def cross_rows(part, segments, ks, pieces, train, ca, cg):
    train.wait(part)
    for name, _, at, w in segments:
        acc = ca if name == "a" else cg
        rows = [p[:, :, :, at:at + w].reshape(128, w) for p in pieces]
        x = nt(jnp.concatenate(rows, axis=0), train.get(part, at, w))
        for i, k in enumerate(ks):
            for s4 in range(2):
                r = i * 128 + s4 * 64
                acc[place(part, k, s4)] += x[r:r + 64].reshape(8, 8, TOK)


def val_rows(core_ref, blocks, ka, kg, name, seen):
    even = jnp.concatenate([x[:32] for x in blocks], axis=0)
    late = jnp.concatenate(blocks[4:], axis=0)
    y = nt(jnp.where(core_ref[0] == 0, even, late), jnp.concatenate(blocks, axis=0))
    acc = ka if name == "a" else kg
    if name in seen:
        acc[...] += y
    else:
        acc[...] = y
        seen.add(name)


def early_body(core_ref, acts, grads, dep_ref, *refs):
    own = [refs[p * 2:p * 2 + 2] for p in range(3)]
    ca, cg, tok, hbuf, sems = refs[6:]
    train = Train(core_ref, acts, grads, 0, FULL, hbuf, sems)
    tok[...] = jnp.zeros_like(tok)
    ca[...] = jnp.zeros_like(ca)
    cg[...] = jnp.zeros_like(cg)
    for part in range(3):
        cross_rows(part, FULL[part], (0, 1), own[part], train, ca, cg)


def bring(moves, sems):
    cps = [pltpu.make_async_copy(x, y, sems.at[i]) for i, (x, y) in enumerate(moves)]
    for cp in cps:
        cp.start()
    return cps


def late_own_body(core_ref, acts, grads, *refs, which):
    pieces = [refs[p * 3:p * 3 + 3] for p in range(3)]
    n = 2 + 2 * which
    ins, refs = refs[9:9 + n], refs[9 + n:]
    ca, cg, ka, kg = refs[:4]
    if which:
        ids = refs[4]
    hbuf, sems, pbuf, psems, asems = refs[4 + which:]
    sums = bring(list(zip(ins, (ca, cg, ka, kg))), asems)
    todo = []
    for part in range(3):
        x, a1, last = pieces[part]
        w = SETW[which][part]
        cols = pl.ds(SETAT[which][part], w)
        srcs = (x.at[:, :, :, cols], a1.at[:, :, :, cols], last.at[0], last.at[1])
        todo.append(bring(
            [(src, pbuf.at[part, k, :, :, :, pl.ds(0, w)]) for k, src in enumerate(srcs)],
            psems.at[part],
        ))
    train = Train(core_ref, acts, grads, 0, SETS[which], hbuf, sems)
    seen = {"a", "g"} if which else set()
    for part in range(3):
        for cp in todo[part]:
            cp.wait()
        if part == 0:
            for cp in sums:
                cp.wait()

        def blocks(at, w):
            out = [None] * 8
            for k in range(4):
                for s4 in range(2):
                    out[place(part, k, s4)] = pbuf[part, k, s4, :, :, at:at + w].reshape(64, w)
            return out

        for name, _, at, w in SETS[which][part]:
            val_rows(core_ref, blocks(at, w), ka, kg, name, seen)
        if which and part == 2:
            for b, x in enumerate(blocks(SETW[1][2] - IDW, IDW)):
                ids[b * 64:b * 64 + 64, :] = x.astype(jnp.float32)
        cross_rows(
            part, SETS[which][part], (2, 3), [pbuf.at[part, 2], pbuf.at[part, 3]], train, ca, cg
        )


def late_other_body(core_ref, acts, grads, o0, o1, o2, o3, o4, ain, gin, k1, k2, *refs, which):
    c = core_ref[0]
    lasts = (o2, o3, o4)
    if which:
        idin, raw_ref, norm_ref, hbuf, sems, vbuf, acc_a, acc_g, ka, kg, ids, vsems, asems = refs
        extra = [(idin, ids)]
    else:
        acc_a, acc_g, ka, kg, tok, hbuf, sems, vbuf, vsems, asems = refs
        tok[...] = jnp.zeros_like(tok)
        extra = []
    sums = bring([(ain, acc_a), (gin, acc_g), (k1, ka), (k2, kg)] + extra, asems)
    todo = []
    for part in range(3):
        w = SETW[which][part]
        cols = pl.ds(STARTS[part] + SETAT[which][part], w)
        todo.append(bring(
            [
                (
                    o.at[s4, :, :, cols] if k < 2 else o.at[s4],
                    vbuf.at[part, :, place(part, k, s4), :, pl.ds(0, w)],
                )
                for k, o in enumerate((o0, o1, lasts[part].at[0], lasts[part].at[1]))
                for s4 in range(2)
            ],
            vsems.at[part],
        ))
    train = Train(core_ref, acts, grads, 1, SETS[which], hbuf, sems)
    seen = {"a", "g"}
    for part in range(3):
        for cp in todo[part]:
            cp.wait()
        if part == 0:
            for cp in sums:
                cp.wait()
        for name, _, at, w in SETS[which][part]:
            blocks = [vbuf[part, b, :, :, at:at + w].reshape(64, w) for b in range(8)]
            val_rows(core_ref, blocks, ka, kg, name, seen)
        train.wait(part)
        for name, _, at, w in SETS[which][part]:
            acc = acc_a if name == "a" else acc_g
            rows = vbuf[part, :, :, :, at:at + w].reshape(VAL, w)
            acc[...] += nt(rows, train.get(part, at, w)).reshape(8, 8, 8, TOK)
    if not which:
        return

    cross = acc_a[...].reshape(VAL, TOK) * acc_g[...].reshape(VAL, TOK)
    kern = ka[...] * kg[...]
    all_ids = ids[...]
    even = jnp.concatenate([all_ids[b * 64:b * 64 + 32] for b in range(8)], axis=0)
    half_ids = jnp.where(c == 0, even, all_ids[256:512])

    def onehot(x):
        n = x.shape[0]
        want = lax.broadcasted_iota(jnp.int32, (8, n), 0).astype(jnp.float32)
        return jnp.where(jnp.transpose(x)[0:8, :] == want, 1.0, 0.0)

    def total(a, b):
        return jnp.dot(a, b, precision=lax.Precision.HIGHEST, preferred_element_type=jnp.float32)

    each = onehot(all_ids)
    raw_ref[...] = total(each, cross)[0:NVAL]
    norm = jnp.sum(total(onehot(half_ids), kern) * each, axis=1, keepdims=True)
    norm_ref[...] = jnp.broadcast_to(norm, (8, 128))[0:NVAL]


ACC = jax.ShapeDtypeStruct((8, 8, 8, TOK), jnp.float32)
KERN = jax.ShapeDtypeStruct((VAL // 2, VAL), jnp.float32)


TOKEN = jax.ShapeDtypeStruct((8, 128), jnp.float32)
IDS = jax.ShapeDtypeStruct((VAL, IDW), jnp.float32)


def local_call(body, core, acts, grads, args, outs, flops, width, scratch=(), pinned=(), mib=26):
    vmem = pl.BlockSpec(memory_space=pltpu.VMEM)
    anyspec = pl.BlockSpec(memory_space=pl.ANY)
    return pl.pallas_call(
        body,
        in_specs=[pl.BlockSpec(memory_space=pltpu.SMEM)] + [anyspec] * 2
        + [vmem if i in pinned else anyspec for i in range(len(args))],
        out_specs=[vmem] * len(outs),
        out_shape=outs,
        scratch_shapes=[
            pltpu.VMEM((3, TOK, width), jnp.bfloat16),
            pltpu.SemaphoreType.DMA((3, 2)),
        ] + list(scratch),
        compiler_params=pltpu.CompilerParams(vmem_limit_bytes=mib << 20),
        cost_estimate=pl.CostEstimate(
            flops=flops, bytes_accessed=TOK * (FF + D), transcendentals=0
        ),
    )(core, acts, grads, *[pin(x) if i in pinned else x for i, x in enumerate(args)])


def shards(hidden_acts, out_grads, val_acts, val_grads, val_ids):
    hidden_acts = pltpu.with_memory_space_constraint(hidden_acts, pltpu.HBM)
    out_grads = pltpu.with_memory_space_constraint(out_grads, pltpu.HBM)
    core = lax.axis_index("dp") % 2
    first = core == 0
    idcol = jnp.broadcast_to(val_ids[:, None].astype(jnp.bfloat16), (4, IDW))
    halves = [
        jnp.concatenate(
            [val_acts[:, h * HA:(h + 1) * HA], val_grads[:, h * HG:(h + 1) * HG], idcol], axis=1
        )
        for h in range(2)
    ]
    keep = jnp.where(first, halves[0], halves[1])
    got = swap(jnp.where(first, halves[1], halves[0]))
    rows = jnp.concatenate([jnp.where(first, keep, got), jnp.where(first, got, keep)], axis=0)

    def send(block, n):
        return hop(block, [a for a in "xyz" if n & WEIGHT[a]], 0)

    near = {n: send(rows, n) for n in (1, 2, 4, 3)}
    (again,) = gate([rows], near[3])
    near.update({n: send(again, n) for n in (5, 6, 7)})
    sg = self_call(out_grads, near[3])
    (rows,) = gate([jnp.stack([rows] + [near[n] for n in range(1, 8)])], sg)
    x = [double(rows[..., s:s + w], RUNS[j], 1) for j, (s, w) in enumerate(zip(STARTS, WIDTHS))]
    block_gram = self_call(hidden_acts, x[1], sg)
    a1 = [hop(x[j], STEP5[j], 1) for j in range(3)]
    o0 = swap(jnp.concatenate(x, axis=-1))
    pair = gate([jnp.stack([x[j], a1[j]]) for j in range(3)], block_gram, o0)
    last = [
        [hop(pair[j][..., a:a + w], STEP6[j], 1) for j, (a, w) in enumerate(zip(at, width))]
        for at, width in zip(SETAT, SETW)
    ]
    o1 = swap(gate([jnp.concatenate(a1, axis=-1)], pair[0])[0])
    call = functools.partial(
        local_call, core=core.reshape(1).astype(jnp.int32), acts=hidden_acts, grads=out_grads
    )
    unit = 512 * (HA + HG)
    ca, cg, tok = call(
        early_body, args=[block_gram] + [y for j in range(3) for y in (x[j], a1[j])],
        outs=[ACC, ACC, TOKEN], flops=512 * unit, width=C1, pinned=range(1, 7), mib=28,
    )
    sums = [ca, cg]
    for which in range(2):
        got = [gate([y], tok, *([] if which else [o1]))[0] for y in last[which]]
        swapped = [swap(y) for y in got]
        sums = call(
            functools.partial(late_own_body, which=which),
            args=[y for j in range(3) for y in (x[j], a1[j], got[j])] + list(sums),
            outs=[ACC, ACC, KERN, KERN] + [IDS] * which, flops=512 * unit, width=SETMAX,
            scratch=[
                pltpu.VMEM((3, 4, 2, 8, 8, SETMAX), jnp.bfloat16),
                pltpu.SemaphoreType.DMA((3, 4)),
                pltpu.SemaphoreType.DMA((4,)),
            ],
        )
        outs = [ACC, ACC, KERN, KERN, TOKEN]
        scratch = [pltpu.VMEM((3, 8, 8, 8, SETMAX), jnp.bfloat16)]
        if which:
            outs = [
                jax.ShapeDtypeStruct((NVAL, TOK), jnp.float32),
                jax.ShapeDtypeStruct((NVAL, 128), jnp.float32),
            ]
            scratch += [pltpu.VMEM(a.shape, a.dtype) for a in (ACC, ACC, KERN, KERN, IDS)]
        outs = call(
            functools.partial(late_other_body, which=which),
            args=[o0, o1] + swapped + list(sums), outs=outs, flops=768 * unit, width=SETMAX,
            scratch=scratch + [
                pltpu.SemaphoreType.DMA((3, 8)),
                pltpu.SemaphoreType.DMA((5,)),
            ],
        )
        sums, tok = outs[:4], outs[-1]
    raw, norm = outs
    norm = norm + swap(norm)
    token_scores = raw * lax.rsqrt(norm[:, :1] + 1e-06)
    return (token_scores, block_gram)


def solution(mesh):
    return jax.shard_map(
        shards,
        mesh=mesh,
        in_specs=(
            P(AXES, None),
            P(AXES, None),
            P(AXES, None),
            P(AXES, None),
            P(AXES),
        ),
        out_specs=(P(None, AXES), P(AXES, None)),
        check_vma=False,
    )
```

```python
import functools
import math

import jax
import jax.numpy as jnp
from jax import lax
from jax.experimental import pallas as pl
from jax.experimental.pallas import tpu as pltpu
from jax.sharding import PartitionSpec as P

D = 8192
FF = 14336
BLK = 128
NVAL = 4
TOK = 512
VAL = 512
AXES = ("dp", "seq")
HA = FF // 2
HG = D // 2
C1 = 3840
C2A = HA - C1
C2G = 512
C2 = C2A + C2G
C3G = HG - C2G
IDW = 128
C3 = C3G + IDW
MASKS = ((1, 3), (3, 1))


def coords(i):
    dp, seq = divmod(i, 8)
    c = dp % 2
    z = (dp // 2) % 4
    x = (seq // 4) * 2 + dp // 8
    return {"x": x, "y": seq % 4, "z": z, "c": c}


def index(p):
    dp = ((p["x"] % 2) * 4 + p["z"]) * 2 + p["c"]
    return dp * 8 + (p["x"] // 2) * 4 + p["y"]


def ring_pairs(axes, step):
    pairs = []
    for i in range(128):
        p = coords(i)
        for axis in axes:
            p[axis] ^= MASKS[p["c"]][step]
        pairs.append((i, index(p)))
    return pairs


def core_pairs():
    pairs = []
    for i in range(128):
        p = coords(i)
        p["c"] ^= 1
        pairs.append((i, index(p)))
    return pairs


def swap(x):
    return lax.ppermute(x, AXES, core_pairs())


def hop(x, axes, step):
    return lax.ppermute(x, AXES, ring_pairs(axes, step))


def double(x, axis, step):
    return jnp.stack([x, hop(x, axis, step)])


def pin(x):
    return pltpu.with_memory_space_constraint(x, pltpu.VMEM)


def gate(xs, *deps, space=pltpu.VMEM):
    n = len(xs)
    anyspec = pl.BlockSpec(memory_space=pl.ANY)
    return pl.pallas_call(
        lambda *refs: None,
        in_specs=[anyspec] * (n + len(deps)),
        out_specs=[anyspec] * n,
        out_shape=[jax.ShapeDtypeStruct(x.shape, x.dtype) for x in xs],
        input_output_aliases={i: i for i in range(n)},
        compiler_params=pltpu.CompilerParams(vmem_limit_bytes=1 << 20),
        cost_estimate=pl.CostEstimate(flops=0, bytes_accessed=0, transcendentals=0),
    )(*[pltpu.with_memory_space_constraint(x, space) for x in xs], *deps)


def nt(a, b):
    return lax.dot_general(a, b, (((1,), (1,)), ((), ())), preferred_element_type=jnp.float32)


def self_add(acc, ref):
    acc[0:256, :] += nt(ref[256:512, :], ref[0:256, :])
    acc[256:384, 0:128] += nt(ref[128:256, :], ref[0:128, :])
    acc[384:512, 0:128] += nt(ref[384:512, :], ref[256:384, :])


def self_first_body(x_ref, dep_ref, out_ref):
    @pl.when(pl.program_id(0) == 0)
    def _():
        out_ref[...] = jnp.zeros_like(out_ref)

    self_add(out_ref, x_ref)


def self_last_body(x_ref, first_ref, dep_ref, out_ref, acc, *, steps):
    i = pl.program_id(0)

    @pl.when(i == 0)
    def _():
        acc[...] = jnp.zeros_like(acc)

    self_add(acc, x_ref)

    @pl.when(i == steps - 1)
    def _():
        k = first_ref[...] * acc[...]
        rows = lax.broadcasted_iota(jnp.int32, (4, 4), 0)
        cols = lax.broadcasted_iota(jnp.int32, (4, 4), 1)
        out = jnp.zeros((4, 4), jnp.float32)
        spots = (
            (2, 0, 0, 0), (2, 1, 0, 128), (3, 0, 128, 0), (3, 1, 128, 128),
            (1, 0, 256, 0), (3, 2, 384, 0),
        )
        for b, c, r0, c0 in spots:
            s = jnp.sum(k[r0:r0 + 128, c0:c0 + 128])
            out = jnp.where((rows == b) & (cols == c), s, out)
        out_ref[...] = out / (float(BLK) * math.sqrt(float(FF) * float(D)))


KC = 2048


def self_call(x, dep, first=None):
    width = x.shape[1]
    half = pl.BlockSpec((512, 256), lambda i: (0, 0))
    anyspec = pl.BlockSpec(memory_space=pl.ANY)
    args = [x] + ([] if first is None else [first]) + [dep]
    body = self_first_body
    if first is not None:
        body = functools.partial(self_last_body, steps=width // KC)
    return pl.pallas_call(
        body,
        grid=(width // KC,),
        in_specs=[pl.BlockSpec((TOK, KC), lambda i: (0, i))]
        + ([] if first is None else [half]) + [anyspec],
        out_specs=half if first is None else pl.BlockSpec((4, 4), lambda i: (0, 0)),
        out_shape=jax.ShapeDtypeStruct((512, 256) if first is None else (4, 4), jnp.float32),
        scratch_shapes=[] if first is None else [pltpu.VMEM((512, 256), jnp.float32)],
        compiler_params=pltpu.CompilerParams(vmem_limit_bytes=16 << 20),
        cost_estimate=pl.CostEstimate(
            flops=2 * 512 * 256 * width, bytes_accessed=2 * TOK * width, transcendentals=0
        ),
    )(*args)


RUNS = ("y", "z", "x")
STEP5 = ("z", "x", "y")
STEP6 = ("x", "y", "z")
WEIGHT = {"x": 4, "y": 2, "z": 1}


def place(part, k, s4):
    n = s4 * WEIGHT[RUNS[part]]
    if k in (1, 3):
        n += WEIGHT[STEP5[part]]
    if k in (2, 3):
        n += WEIGHT[STEP6[part]]
    return n


WIDTHS = (C1, C2, C3)
STARTS = (0, C1, C1 + C2)
ALLW = C1 + C2 + C3
FULL = (
    (("a", 0, 0, C1),),
    (("a", C1, 0, C2A), ("g", 0, C2A, C2G)),
    (("g", C2G, 0, C3G),),
)
SETAT = ((0, 0, 0), (2048, 1792, 1792))
SETW = ((2048, 1792, 1792), (C1 - 2048, C2 - 1792, C3 - 1792))
SETS = (
    ((("a", 0, 0, 2048),), (("a", C1, 0, 1792),), (("g", C2G, 0, 1792),)),
    (
        (("a", 2048, 0, C1 - 2048),),
        (("a", C1 + 1792, 0, C2A - 1792), ("g", 0, C2A - 1792, C2G)),
        (("g", C2G + 1792, 0, C3G - 1792),),
    ),
)
SETMAX = 2048


class Train:
    def __init__(self, core_ref, acts, grads, half, parts, hbuf, sems):
        c = core_ref[0]
        o = c if half == 0 else 1 - c
        self.hbuf, self.todo = hbuf, []
        for part, segments in enumerate(parts):
            cps = []
            for i, (name, col, at, w) in enumerate(segments):
                src, step = (acts, HA) if name == "a" else (grads, HG)
                first = pl.multiple_of(o * step + col, 128)
                cps.append(pltpu.make_async_copy(
                    src.at[:, pl.ds(first, w)], hbuf.at[part, :, pl.ds(at, w)], sems.at[part, i]
                ))
            self.todo.append(cps)

    def go(self, part):
        for cp in self.todo[part]:
            cp.start()

    def wait(self, part):
        for cp in self.todo[part]:
            cp.wait()

    def get(self, part, at, w):
        return self.hbuf[part, :, at:at + w]


def cross_rows(part, segments, ks, pieces, train, ca, cg):
    train.wait(part)
    for name, _, at, w in segments:
        acc = ca if name == "a" else cg
        rows = [p[:, :, :, at:at + w].reshape(128, w) for p in pieces]
        x = nt(jnp.concatenate(rows, axis=0), train.get(part, at, w))
        for i, k in enumerate(ks):
            for s4 in range(2):
                r = i * 128 + s4 * 64
                acc[place(part, k, s4)] += x[r:r + 64].reshape(8, 8, TOK)


def once(cps):
    left = list(cps)

    def wait():
        while left:
            left.pop().wait()

    return wait


def val_rows(core_ref, blocks, ka, kg, name, seen, ready):
    even = jnp.concatenate([x[:32] for x in blocks], axis=0)
    late = jnp.concatenate(blocks[4:], axis=0)
    y = nt(jnp.where(core_ref[0] == 0, even, late), jnp.concatenate(blocks, axis=0))
    acc = ka if name == "a" else kg
    ready()
    if name in seen:
        acc[...] += y
    else:
        acc[...] = y
        seen.add(name)


def early_body(core_ref, acts, grads, dep_ref, *refs):
    own = [refs[p * 2:p * 2 + 2] for p in range(3)]
    ca, cg, tok, hbuf, sems = refs[6:]
    train = Train(core_ref, acts, grads, 0, FULL, hbuf, sems)
    for part in range(3):
        train.go(part)
    tok[...] = jnp.zeros_like(tok)
    ca[...] = jnp.zeros_like(ca)
    cg[...] = jnp.zeros_like(cg)
    for part in range(3):
        cross_rows(part, FULL[part], (0, 1), own[part], train, ca, cg)


def bring(moves, sems):
    cps = [pltpu.make_async_copy(x, y, sems.at[i]) for i, (x, y) in enumerate(moves)]
    for cp in cps:
        cp.start()
    return cps


def late_own_body(core_ref, acts, grads, *refs, which):
    pieces = [refs[p * 3:p * 3 + 3] for p in range(3)]
    n = 2 + 2 * which
    ins, refs = refs[9:9 + n], refs[9 + n:]
    ca, cg, ka, kg = refs[:4]
    if which:
        ids = refs[4]
    hbuf, sems, pbuf, psems, asems = refs[4 + which:]
    train = Train(core_ref, acts, grads, 0, SETS[which], hbuf, sems)
    todo = []
    for part in range(3):
        x, a1, last = pieces[part]
        w = SETW[which][part]
        cols = pl.ds(SETAT[which][part], w)
        srcs = (x.at[:, :, :, cols], a1.at[:, :, :, cols], last.at[0], last.at[1])
        todo.append(bring(
            [(src, pbuf.at[part, k, :, :, :, pl.ds(0, w)]) for k, src in enumerate(srcs)],
            psems.at[part],
        ))
        train.go(part)
        if part == 0:
            ready = once(bring(list(zip(ins, (ca, cg, ka, kg))), asems))
    seen = {"a", "g"} if which else set()
    for part in range(3):
        for cp in todo[part]:
            cp.wait()

        def blocks(at, w):
            out = [None] * 8
            for k in range(4):
                for s4 in range(2):
                    out[place(part, k, s4)] = pbuf[part, k, s4, :, :, at:at + w].reshape(64, w)
            return out

        for name, _, at, w in SETS[which][part]:
            val_rows(core_ref, blocks(at, w), ka, kg, name, seen, ready)
        if which and part == 2:
            for b, x in enumerate(blocks(SETW[1][2] - IDW, IDW)):
                ids[b * 64:b * 64 + 64, :] = x.astype(jnp.float32)
        cross_rows(
            part, SETS[which][part], (2, 3), [pbuf.at[part, 2], pbuf.at[part, 3]], train, ca, cg
        )


def late_other_body(core_ref, acts, grads, o0, o1, o2, o3, o4, ain, gin, k1, k2, *refs, which):
    c = core_ref[0]
    lasts = (o2, o3, o4)
    if which:
        idin, raw_ref, norm_ref, hbuf, sems, vbuf, acc_a, acc_g, ka, kg, ids, vsems, asems = refs
        extra = [(idin, ids)]
    else:
        acc_a, acc_g, ka, kg, tok, hbuf, sems, vbuf, vsems, asems = refs
        tok[...] = jnp.zeros_like(tok)
        extra = []
    train = Train(core_ref, acts, grads, 1, SETS[which], hbuf, sems)
    todo = []
    for part in range(3):
        w = SETW[which][part]
        cols = pl.ds(STARTS[part] + SETAT[which][part], w)
        first = 0 if which else sum(SETW[0][:part])
        todo.append(bring(
            [
                (
                    o.at[s4, :, :, cols] if k < 2 else o.at[s4, :, :, pl.ds(first, w)],
                    vbuf.at[part, :, place(part, k, s4), :, pl.ds(0, w)],
                )
                for k, o in enumerate((o0, o1, lasts[part].at[0], lasts[part].at[1]))
                for s4 in range(2)
            ],
            vsems.at[part],
        ))
        train.go(part)
        if part == 0:
            sums = [(ain, acc_a), (gin, acc_g), (k1, ka), (k2, kg)] + extra
            ready = once(bring(sums, asems))
    seen = {"a", "g"}
    for part in range(3):
        for cp in todo[part]:
            cp.wait()
        for name, _, at, w in SETS[which][part]:
            blocks = [vbuf[part, b, :, :, at:at + w].reshape(64, w) for b in range(8)]
            val_rows(core_ref, blocks, ka, kg, name, seen, ready)
        train.wait(part)
        for name, _, at, w in SETS[which][part]:
            acc = acc_a if name == "a" else acc_g
            rows = vbuf[part, :, :, :, at:at + w].reshape(VAL, w)
            acc[...] += nt(rows, train.get(part, at, w)).reshape(8, 8, 8, TOK)
    if not which:
        return

    cross = acc_a[...].reshape(VAL, TOK) * acc_g[...].reshape(VAL, TOK)
    kern = ka[...] * kg[...]
    all_ids = ids[...]
    row_ids = jnp.transpose(all_ids)[0:1, :]
    even = jnp.concatenate([all_ids[b * 64:b * 64 + 32] for b in range(8)], axis=0)
    half_ids = jnp.where(c == 0, even, all_ids[256:512])
    for v in range(NVAL):
        keep = jnp.where(all_ids == float(v), 1.0, 0.0)
        keep = jnp.concatenate([keep] * 4, axis=1)
        raw_ref[v:v + 1, :] = jnp.sum(cross * keep, axis=0, keepdims=True)
        keep = jnp.where(half_ids == float(v), 1.0, 0.0)
        keep = jnp.concatenate([keep] * 4, axis=1)
        part = jnp.sum(kern * keep, axis=0, keepdims=True)
        part = jnp.sum(jnp.where(row_ids == float(v), part, 0.0))
        norm_ref[v:v + 1, :] = jnp.full((1, 128), part, jnp.float32)


ACC = jax.ShapeDtypeStruct((8, 8, 8, TOK), jnp.float32)
KERN = jax.ShapeDtypeStruct((VAL // 2, VAL), jnp.float32)


TOKEN = jax.ShapeDtypeStruct((8, 128), jnp.float32)
IDS = jax.ShapeDtypeStruct((VAL, IDW), jnp.float32)


def local_call(body, core, acts, grads, args, outs, flops, width, scratch=(), pinned=(), mib=26):
    vmem = pl.BlockSpec(memory_space=pltpu.VMEM)
    anyspec = pl.BlockSpec(memory_space=pl.ANY)
    return pl.pallas_call(
        body,
        in_specs=[pl.BlockSpec(memory_space=pltpu.SMEM)] + [anyspec] * 2
        + [vmem if i in pinned else anyspec for i in range(len(args))],
        out_specs=[vmem] * len(outs),
        out_shape=outs,
        scratch_shapes=[
            pltpu.VMEM((3, TOK, width), jnp.bfloat16),
            pltpu.SemaphoreType.DMA((3, 2)),
        ] + list(scratch),
        compiler_params=pltpu.CompilerParams(vmem_limit_bytes=mib << 20),
        cost_estimate=pl.CostEstimate(
            flops=flops, bytes_accessed=TOK * (FF + D) if flops else 0, transcendentals=0
        ),
    )(core, acts, grads, *[pin(x) if i in pinned else x for i, x in enumerate(args)])


def shards(hidden_acts, out_grads, val_acts, val_grads, val_ids):
    hidden_acts = pltpu.with_memory_space_constraint(hidden_acts, pltpu.HBM)
    out_grads = pltpu.with_memory_space_constraint(out_grads, pltpu.HBM)
    core = lax.axis_index("dp") % 2
    first = core == 0
    idcol = jnp.broadcast_to(val_ids[:, None].astype(jnp.bfloat16), (4, IDW))
    halves = [
        jnp.concatenate(
            [val_acts[:, h * HA:(h + 1) * HA], val_grads[:, h * HG:(h + 1) * HG], idcol], axis=1
        )
        for h in range(2)
    ]
    keep = jnp.where(first, halves[0], halves[1])
    got = swap(jnp.where(first, halves[1], halves[0]))
    rows = jnp.concatenate([jnp.where(first, keep, got), jnp.where(first, got, keep)], axis=0)

    def send(block, n):
        return hop(block, [a for a in "xyz" if n & WEIGHT[a]], 0)

    near = {n: send(rows, n) for n in (1, 2, 4, 3)}
    (again,) = gate([rows], near[3])
    near.update({n: send(again, n) for n in (5, 6, 7)})
    sg = self_call(out_grads, near[3])
    (rows,) = gate([jnp.stack([rows] + [near[n] for n in range(1, 8)])], sg)
    x = [double(rows[..., s:s + w], RUNS[j], 1) for j, (s, w) in enumerate(zip(STARTS, WIDTHS))]
    block_gram = self_call(hidden_acts, x[1], sg)
    a1 = [hop(x[j], STEP5[j], 1) for j in range(3)]
    o0 = swap(jnp.concatenate(x, axis=-1))
    pair = gate([jnp.stack([x[j], a1[j]]) for j in range(3)], block_gram, o0)
    cut = [
        [pair[j][..., a:a + w] for j, (a, w) in enumerate(zip(at, width))]
        for at, width in zip(SETAT, SETW)
    ]
    last = [[hop(y, STEP6[j], 1) for j, y in enumerate(cut[0])]]
    o1 = swap(gate([jnp.concatenate(a1, axis=-1)], pair[0])[0])
    call = functools.partial(
        local_call, core=core.reshape(1).astype(jnp.int32), acts=hidden_acts, grads=out_grads
    )
    unit = 512 * (HA + HG)
    ca, cg, tok = call(
        early_body, args=[block_gram] + [y for j in range(3) for y in (x[j], a1[j])],
        outs=[ACC, ACC, TOKEN], flops=512 * unit, width=C1, pinned=range(1, 7), mib=28,
    )
    last.append([hop(y, STEP6[j], 1) for j, y in enumerate(cut[1])])
    sums = [ca, cg]
    for which in range(2):
        got = last[which]
        if which:
            got = [gate([y], tok)[0] for y in got]
            swapped = [swap(y) for y in got]
        else:
            swapped = [swap(gate([jnp.concatenate(got, axis=-1)], tok, o1)[0])] * 3
        sums = call(
            functools.partial(late_own_body, which=which),
            args=[y for j in range(3) for y in (x[j], a1[j], got[j])] + list(sums),
            outs=[ACC, ACC, KERN, KERN] + [IDS] * which, flops=512 * unit * which, width=SETMAX,
            scratch=[
                pltpu.VMEM((3, 4, 2, 8, 8, SETMAX), jnp.bfloat16),
                pltpu.SemaphoreType.DMA((3, 4)),
                pltpu.SemaphoreType.DMA((4,)),
            ],
        )
        outs = [ACC, ACC, KERN, KERN, TOKEN]
        scratch = [pltpu.VMEM((3, 8, 8, 8, SETMAX), jnp.bfloat16)]
        if which:
            outs = [
                jax.ShapeDtypeStruct((NVAL, TOK), jnp.float32),
                jax.ShapeDtypeStruct((NVAL, 128), jnp.float32),
            ]
            scratch += [pltpu.VMEM(a.shape, a.dtype) for a in (ACC, ACC, KERN, KERN, IDS)]
        outs = call(
            functools.partial(late_other_body, which=which),
            args=[o0, o1] + swapped + list(sums), outs=outs, flops=768 * unit * which, width=SETMAX,
            scratch=scratch + [
                pltpu.SemaphoreType.DMA((3, 8)),
                pltpu.SemaphoreType.DMA((5,)),
            ],
        )
        sums, tok = outs[:4], outs[-1]
    raw, norm = outs
    norm = norm + swap(norm)
    token_scores = raw * lax.rsqrt(norm[:, :1] + 1e-06)
    return (token_scores, block_gram)


def solution(mesh):
    return jax.shard_map(
        shards,
        mesh=mesh,
        in_specs=(
            P(AXES, None),
            P(AXES, None),
            P(AXES, None),
            P(AXES, None),
            P(AXES),
        ),
        out_specs=(P(None, AXES), P(AXES, None)),
        check_vma=False,
    )
```

```python
import functools
import math

import jax
import jax.numpy as jnp
from jax import lax
from jax.experimental import pallas as pl
from jax.experimental.pallas import tpu as pltpu
from jax.sharding import PartitionSpec as P

D = 8192
FF = 14336
BLK = 128
NVAL = 4
TOK = 512
VAL = 512
AXES = ("dp", "seq")
HA = FF // 2
HG = D // 2
C1 = 3840
C2A = HA - C1
C2G = 512
C2 = C2A + C2G
C3G = HG - C2G
IDW = 128
C3 = C3G + IDW
MASKS = ((1, 3), (3, 1))


def coords(i):
    dp, seq = divmod(i, 8)
    c = dp % 2
    z = (dp // 2) % 4
    x = (seq // 4) * 2 + dp // 8
    return {"x": x, "y": seq % 4, "z": z, "c": c}


def index(p):
    dp = ((p["x"] % 2) * 4 + p["z"]) * 2 + p["c"]
    return dp * 8 + (p["x"] // 2) * 4 + p["y"]


def ring_pairs(axes, step):
    pairs = []
    for i in range(128):
        p = coords(i)
        for axis in axes:
            p[axis] ^= MASKS[p["c"]][step]
        pairs.append((i, index(p)))
    return pairs


def core_pairs():
    pairs = []
    for i in range(128):
        p = coords(i)
        p["c"] ^= 1
        pairs.append((i, index(p)))
    return pairs


def swap(x):
    return lax.ppermute(x, AXES, core_pairs())


def hop(x, axes, step):
    return lax.ppermute(x, AXES, ring_pairs(axes, step))


def double(x, axis, step):
    return jnp.stack([x, hop(x, axis, step)])


def pin(x):
    return pltpu.with_memory_space_constraint(x, pltpu.VMEM)


def gate(xs, *deps, space=pltpu.VMEM):
    n = len(xs)
    anyspec = pl.BlockSpec(memory_space=pl.ANY)
    return pl.pallas_call(
        lambda *refs: None,
        in_specs=[anyspec] * (n + len(deps)),
        out_specs=[anyspec] * n,
        out_shape=[jax.ShapeDtypeStruct(x.shape, x.dtype) for x in xs],
        input_output_aliases={i: i for i in range(n)},
        compiler_params=pltpu.CompilerParams(vmem_limit_bytes=1 << 20),
        cost_estimate=pl.CostEstimate(flops=0, bytes_accessed=0, transcendentals=0),
    )(*[pltpu.with_memory_space_constraint(x, space) for x in xs], *deps)


def nt(a, b):
    return lax.dot_general(a, b, (((1,), (1,)), ((), ())), preferred_element_type=jnp.float32)


def self_add(acc, ref):
    acc[0:256, :] += nt(ref[256:512, :], ref[0:256, :])
    acc[256:384, 0:128] += nt(ref[128:256, :], ref[0:128, :])
    acc[384:512, 0:128] += nt(ref[384:512, :], ref[256:384, :])


def self_first_body(x_ref, dep_ref, out_ref):
    @pl.when(pl.program_id(0) == 0)
    def _():
        out_ref[...] = jnp.zeros_like(out_ref)

    self_add(out_ref, x_ref)


def self_last_body(x_ref, first_ref, dep_ref, out_ref, acc, *, steps):
    i = pl.program_id(0)

    @pl.when(i == 0)
    def _():
        acc[...] = jnp.zeros_like(acc)

    self_add(acc, x_ref)

    @pl.when(i == steps - 1)
    def _():
        k = first_ref[...] * acc[...]
        rows = lax.broadcasted_iota(jnp.int32, (4, 4), 0)
        cols = lax.broadcasted_iota(jnp.int32, (4, 4), 1)
        out = jnp.zeros((4, 4), jnp.float32)
        spots = (
            (2, 0, 0, 0), (2, 1, 0, 128), (3, 0, 128, 0), (3, 1, 128, 128),
            (1, 0, 256, 0), (3, 2, 384, 0),
        )
        for b, c, r0, c0 in spots:
            s = jnp.sum(k[r0:r0 + 128, c0:c0 + 128])
            out = jnp.where((rows == b) & (cols == c), s, out)
        out_ref[...] = out / (float(BLK) * math.sqrt(float(FF) * float(D)))


KC = 2048


def self_call(x, dep, first=None):
    width = x.shape[1]
    half = pl.BlockSpec((512, 256), lambda i: (0, 0))
    anyspec = pl.BlockSpec(memory_space=pl.ANY)
    args = [x] + ([] if first is None else [first]) + [dep]
    body = self_first_body
    if first is not None:
        body = functools.partial(self_last_body, steps=width // KC)
    return pl.pallas_call(
        body,
        grid=(width // KC,),
        in_specs=[pl.BlockSpec((TOK, KC), lambda i: (0, i))]
        + ([] if first is None else [half]) + [anyspec],
        out_specs=half if first is None else pl.BlockSpec((4, 4), lambda i: (0, 0)),
        out_shape=jax.ShapeDtypeStruct((512, 256) if first is None else (4, 4), jnp.float32),
        scratch_shapes=[] if first is None else [pltpu.VMEM((512, 256), jnp.float32)],
        compiler_params=pltpu.CompilerParams(vmem_limit_bytes=16 << 20),
        cost_estimate=pl.CostEstimate(
            flops=2 * 512 * 256 * width, bytes_accessed=2 * TOK * width, transcendentals=0
        ),
    )(*args)


RUNS = ("y", "z", "x")
STEP5 = ("z", "x", "y")
STEP6 = ("x", "y", "z")
WEIGHT = {"x": 4, "y": 2, "z": 1}


def place(part, k, s4):
    n = s4 * WEIGHT[RUNS[part]]
    if k in (1, 3):
        n += WEIGHT[STEP5[part]]
    if k in (2, 3):
        n += WEIGHT[STEP6[part]]
    return n


WIDTHS = (C1, C2, C3)
STARTS = (0, C1, C1 + C2)
ALLW = C1 + C2 + C3
FULL = (
    (("a", 0, 0, C1),),
    (("a", C1, 0, C2A), ("g", 0, C2A, C2G)),
    (("g", C2G, 0, C3G),),
)
SETAT = ((0, 0, 0), (2048, 1792, 1792))
SETW = ((2048, 1792, 1792), (C1 - 2048, C2 - 1792, C3 - 1792))
SETS = (
    ((("a", 0, 0, 2048),), (("a", C1, 0, 1792),), (("g", C2G, 0, 1792),)),
    (
        (("a", 2048, 0, C1 - 2048),),
        (("a", C1 + 1792, 0, C2A - 1792), ("g", 0, C2A - 1792, C2G)),
        (("g", C2G + 1792, 0, C3G - 1792),),
    ),
)
SETMAX = 2048


class Train:
    def __init__(self, core_ref, acts, grads, half, parts, hbuf, sems):
        c = core_ref[0]
        o = c if half == 0 else 1 - c
        self.hbuf, self.todo = hbuf, []
        for part, segments in enumerate(parts):
            cps = []
            for i, (name, col, at, w) in enumerate(segments):
                src, step = (acts, HA) if name == "a" else (grads, HG)
                first = pl.multiple_of(o * step + col, 128)
                cps.append(pltpu.make_async_copy(
                    src.at[:, pl.ds(first, w)], hbuf.at[part, :, pl.ds(at, w)], sems.at[part, i]
                ))
            self.todo.append(cps)

    def go(self, part):
        for cp in self.todo[part]:
            cp.start()

    def wait(self, part):
        for cp in self.todo[part]:
            cp.wait()

    def get(self, part, at, w):
        return self.hbuf[part, :, at:at + w]


def cross_rows(part, segments, ks, pieces, train, ca, cg):
    train.wait(part)
    for name, _, at, w in segments:
        acc = ca if name == "a" else cg
        rows = [p[:, :, :, at:at + w].reshape(128, w) for p in pieces]
        x = nt(jnp.concatenate(rows, axis=0), train.get(part, at, w))
        for i, k in enumerate(ks):
            for s4 in range(2):
                r = i * 128 + s4 * 64
                acc[place(part, k, s4)] += x[r:r + 64].reshape(8, 8, TOK)


def once(cps):
    left = list(cps)

    def wait():
        while left:
            left.pop().wait()

    return wait


def val_rows(core_ref, blocks, ka, kg, name, seen, ready):
    even = jnp.concatenate([x[:32] for x in blocks], axis=0)
    late = jnp.concatenate(blocks[4:], axis=0)
    y = nt(jnp.where(core_ref[0] == 0, even, late), jnp.concatenate(blocks, axis=0))
    acc = ka if name == "a" else kg
    ready()
    if name in seen:
        acc[...] += y
    else:
        acc[...] = y
        seen.add(name)


def early_body(core_ref, acts, grads, dep_ref, *refs):
    own = [refs[p * 2:p * 2 + 2] for p in range(3)]
    ca, cg, tok, hbuf, sems = refs[6:]
    train = Train(core_ref, acts, grads, 0, FULL, hbuf, sems)
    for part in range(3):
        train.go(part)
    tok[...] = jnp.zeros_like(tok)
    ca[...] = jnp.zeros_like(ca)
    cg[...] = jnp.zeros_like(cg)
    for part in range(3):
        cross_rows(part, FULL[part], (0, 1), own[part], train, ca, cg)


def bring(moves, sems):
    cps = [pltpu.make_async_copy(x, y, sems.at[i]) for i, (x, y) in enumerate(moves)]
    for cp in cps:
        cp.start()
    return cps


def late_own_body(core_ref, acts, grads, *refs, which):
    pieces = [refs[p * 3:p * 3 + 3] for p in range(3)]
    n = 2 + 2 * which
    ins, refs = refs[9:9 + n], refs[9 + n:]
    ca, cg, ka, kg = refs[:4]
    if which:
        ids = refs[4]
    hbuf, sems, pbuf, psems, asems = refs[4 + which:]
    train = Train(core_ref, acts, grads, 0, SETS[which], hbuf, sems)
    todo = []
    for part in range(3):
        x, a1, last = pieces[part]
        w = SETW[which][part]
        cols = pl.ds(SETAT[which][part], w)
        srcs = (x.at[:, :, :, cols], a1.at[:, :, :, cols], last.at[0], last.at[1])
        todo.append(bring(
            [(src, pbuf.at[part, k, :, :, :, pl.ds(0, w)]) for k, src in enumerate(srcs)],
            psems.at[part],
        ))
        train.go(part)
        if part == 0:
            ready = once(bring(list(zip(ins, (ca, cg, ka, kg))), asems))
    seen = {"a", "g"} if which else set()
    for part in range(3):
        for cp in todo[part]:
            cp.wait()

        def blocks(at, w):
            out = [None] * 8
            for k in range(4):
                for s4 in range(2):
                    out[place(part, k, s4)] = pbuf[part, k, s4, :, :, at:at + w].reshape(64, w)
            return out

        for name, _, at, w in SETS[which][part]:
            val_rows(core_ref, blocks(at, w), ka, kg, name, seen, ready)
        if which and part == 2:
            for b, x in enumerate(blocks(SETW[1][2] - IDW, IDW)):
                ids[b * 64:b * 64 + 64, :] = x.astype(jnp.float32)
        cross_rows(
            part, SETS[which][part], (2, 3), [pbuf.at[part, 2], pbuf.at[part, 3]], train, ca, cg
        )


def late_other_body(core_ref, acts, grads, o0, o1, o2, o3, o4, ain, gin, k1, k2, *refs, which):
    c = core_ref[0]
    lasts = (o2, o3, o4)
    if which:
        idin, raw_ref, norm_ref, hbuf, sems, vbuf, acc_a, acc_g, ka, kg, ids, vsems, asems = refs
        extra = [(idin, ids)]
    else:
        acc_a, acc_g, ka, kg, tok, hbuf, sems, vbuf, vsems, asems = refs
        tok[...] = jnp.zeros_like(tok)
        extra = []
    train = Train(core_ref, acts, grads, 1, SETS[which], hbuf, sems)
    todo = []
    for part in range(3):
        w = SETW[which][part]
        cols = pl.ds(STARTS[part] + SETAT[which][part], w)
        first = 0 if which else sum(SETW[0][:part])
        todo.append(bring(
            [
                (
                    o.at[s4, :, :, cols] if k < 2 else o.at[s4, :, :, pl.ds(first, w)],
                    vbuf.at[part, :, place(part, k, s4), :, pl.ds(0, w)],
                )
                for k, o in enumerate((o0, o1, lasts[part].at[0], lasts[part].at[1]))
                for s4 in range(2)
            ],
            vsems.at[part],
        ))
        train.go(part)
        if part == 0:
            sums = [(ain, acc_a), (gin, acc_g), (k1, ka), (k2, kg)] + extra
            ready = once(bring(sums, asems))
    seen = {"a", "g"}
    for part in range(3):
        for cp in todo[part]:
            cp.wait()
        for name, _, at, w in SETS[which][part]:
            blocks = [vbuf[part, b, :, :, at:at + w].reshape(64, w) for b in range(8)]
            val_rows(core_ref, blocks, ka, kg, name, seen, ready)
        train.wait(part)
        for name, _, at, w in SETS[which][part]:
            acc = acc_a if name == "a" else acc_g
            rows = vbuf[part, :, :, :, at:at + w].reshape(VAL, w)
            acc[...] += nt(rows, train.get(part, at, w)).reshape(8, 8, 8, TOK)
    if not which:
        return

    cross = acc_a[...].reshape(VAL, TOK) * acc_g[...].reshape(VAL, TOK)
    kern = ka[...] * kg[...]
    all_ids = ids[...]
    row_ids = jnp.transpose(all_ids)[0:1, :]
    even = jnp.concatenate([all_ids[b * 64:b * 64 + 32] for b in range(8)], axis=0)
    half_ids = jnp.where(c == 0, even, all_ids[256:512])
    for v in range(NVAL):
        keep = jnp.where(all_ids == float(v), 1.0, 0.0)
        keep = jnp.concatenate([keep] * 4, axis=1)
        raw_ref[v:v + 1, :] = jnp.sum(cross * keep, axis=0, keepdims=True)
        keep = jnp.where(half_ids == float(v), 1.0, 0.0)
        keep = jnp.concatenate([keep] * 4, axis=1)
        part = jnp.sum(kern * keep, axis=0, keepdims=True)
        part = jnp.sum(jnp.where(row_ids == float(v), part, 0.0))
        norm_ref[v:v + 1, :] = jnp.full((1, 128), part, jnp.float32)


ACC = jax.ShapeDtypeStruct((8, 8, 8, TOK), jnp.float32)
KERN = jax.ShapeDtypeStruct((VAL // 2, VAL), jnp.float32)


TOKEN = jax.ShapeDtypeStruct((8, 128), jnp.float32)
IDS = jax.ShapeDtypeStruct((VAL, IDW), jnp.float32)


def local_call(body, core, acts, grads, args, outs, flops, width, scratch=(), pinned=(), mib=26):
    vmem = pl.BlockSpec(memory_space=pltpu.VMEM)
    anyspec = pl.BlockSpec(memory_space=pl.ANY)
    return pl.pallas_call(
        body,
        in_specs=[pl.BlockSpec(memory_space=pltpu.SMEM)] + [anyspec] * 2
        + [vmem if i in pinned else anyspec for i in range(len(args))],
        out_specs=[vmem] * len(outs),
        out_shape=outs,
        scratch_shapes=[
            pltpu.VMEM((3, TOK, width), jnp.bfloat16),
            pltpu.SemaphoreType.DMA((3, 2)),
        ] + list(scratch),
        compiler_params=pltpu.CompilerParams(vmem_limit_bytes=mib << 20),
        cost_estimate=pl.CostEstimate(
            flops=flops, bytes_accessed=TOK * (FF + D) if flops else 0, transcendentals=0
        ),
    )(core, acts, grads, *[pin(x) if i in pinned else x for i, x in enumerate(args)])


def prepare_body(core_ref, ids_ref, acts_ref, grads_ref, keep_ref, away_ref):
    first = core_ref[0] == 0
    for at, ref, w in ((0, acts_ref, HA), (HA, grads_ref, HG)):
        low, high = ref[:, 0:w], ref[:, w:2 * w]
        keep_ref[:, at:at + w] = jnp.where(first, low, high)
        away_ref[:, at:at + w] = jnp.where(first, high, low)
    row = lax.broadcasted_iota(jnp.int32, (4, IDW), 0)
    ids = jnp.zeros((4, IDW), jnp.float32)
    for r in range(4):
        ids = jnp.where(row == r, ids_ref[r].astype(jnp.float32), ids)
    keep_ref[:, HA + HG:] = ids.astype(jnp.bfloat16)
    away_ref[:, HA + HG:] = ids.astype(jnp.bfloat16)


def prepare(core, val_acts, val_grads, val_ids):
    vmem = pl.BlockSpec(memory_space=pltpu.VMEM)
    smem = pl.BlockSpec(memory_space=pltpu.SMEM)
    return pl.pallas_call(
        prepare_body,
        in_specs=[smem, smem, vmem, vmem],
        out_specs=[vmem, vmem],
        out_shape=[jax.ShapeDtypeStruct((4, ALLW), jnp.bfloat16)] * 2,
        compiler_params=pltpu.CompilerParams(vmem_limit_bytes=4 << 20),
        cost_estimate=pl.CostEstimate(flops=0, bytes_accessed=720896, transcendentals=0),
    )(core, val_ids, val_acts, val_grads)


def shards(hidden_acts, out_grads, val_acts, val_grads, val_ids):
    hidden_acts = pltpu.with_memory_space_constraint(hidden_acts, pltpu.HBM)
    out_grads = pltpu.with_memory_space_constraint(out_grads, pltpu.HBM)
    core = lax.axis_index("dp") % 2
    first = core == 0
    core = core.reshape(1).astype(jnp.int32)
    keep, away = prepare(core, val_acts, val_grads, val_ids)
    got = swap(away)
    rows = jnp.concatenate([jnp.where(first, keep, got), jnp.where(first, got, keep)], axis=0)

    def send(block, n):
        return hop(block, [a for a in "xyz" if n & WEIGHT[a]], 0)

    rows = jnp.stack([rows] + [send(rows, n) for n in (1, 2, 3)])
    sg = self_call(out_grads, rows)
    (rows,) = gate([jnp.concatenate([rows, send(rows, 4)], axis=0)], sg)
    x = [double(rows[..., s:s + w], RUNS[j], 1) for j, (s, w) in enumerate(zip(STARTS, WIDTHS))]
    block_gram = self_call(hidden_acts, x[1], sg)
    a1 = [hop(x[j], STEP5[j], 1) for j in range(3)]
    o0 = swap(jnp.concatenate(x, axis=-1))
    pair = gate([jnp.stack([x[j], a1[j]]) for j in range(3)], block_gram, o0)
    cut = [
        [pair[j][..., a:a + w] for j, (a, w) in enumerate(zip(at, width))]
        for at, width in zip(SETAT, SETW)
    ]
    last = [[hop(y, STEP6[j], 1) for j, y in enumerate(cut[0])]]
    o1 = swap(gate([jnp.concatenate(a1, axis=-1)], pair[0])[0])
    call = functools.partial(
        local_call, core=core, acts=hidden_acts, grads=out_grads
    )
    unit = 512 * (HA + HG)
    ca, cg, tok = call(
        early_body, args=[block_gram] + [y for j in range(3) for y in (x[j], a1[j])],
        outs=[ACC, ACC, TOKEN], flops=512 * unit, width=C1, pinned=range(1, 7), mib=28,
    )
    last.append([hop(y, STEP6[j], 1) for j, y in enumerate(cut[1])])
    sums = [ca, cg]
    for which in range(2):
        got = last[which]
        if which:
            got = [gate([y], tok)[0] for y in got]
            swapped = [swap(y) for y in got]
        else:
            swapped = [swap(gate([jnp.concatenate(got, axis=-1)], tok, o1)[0])] * 3
        sums = call(
            functools.partial(late_own_body, which=which),
            args=[y for j in range(3) for y in (x[j], a1[j], got[j])] + list(sums),
            outs=[ACC, ACC, KERN, KERN] + [IDS] * which, flops=512 * unit * which, width=SETMAX,
            scratch=[
                pltpu.VMEM((3, 4, 2, 8, 8, SETMAX), jnp.bfloat16),
                pltpu.SemaphoreType.DMA((3, 4)),
                pltpu.SemaphoreType.DMA((4,)),
            ],
        )
        outs = [ACC, ACC, KERN, KERN, TOKEN]
        scratch = [pltpu.VMEM((3, 8, 8, 8, SETMAX), jnp.bfloat16)]
        if which:
            outs = [
                jax.ShapeDtypeStruct((NVAL, TOK), jnp.float32),
                jax.ShapeDtypeStruct((NVAL, 128), jnp.float32),
            ]
            scratch += [pltpu.VMEM(a.shape, a.dtype) for a in (ACC, ACC, KERN, KERN, IDS)]
        outs = call(
            functools.partial(late_other_body, which=which),
            args=[o0, o1] + swapped + list(sums), outs=outs, flops=768 * unit * which, width=SETMAX,
            scratch=scratch + [
                pltpu.SemaphoreType.DMA((3, 8)),
                pltpu.SemaphoreType.DMA((5,)),
            ],
        )
        sums, tok = outs[:4], outs[-1]
    raw, norm = outs
    norm = norm + swap(norm)
    token_scores = raw * lax.rsqrt(norm[:, :1] + 1e-06)
    return (token_scores, block_gram)


def solution(mesh):
    return jax.shard_map(
        shards,
        mesh=mesh,
        in_specs=(
            P(AXES, None),
            P(AXES, None),
            P(AXES, None),
            P(AXES, None),
            P(AXES),
        ),
        out_specs=(P(None, AXES), P(AXES, None)),
        check_vma=False,
    )
```

```python
import functools
import math

import jax
import jax.numpy as jnp
from jax import lax
from jax.experimental import pallas as pl
from jax.experimental.pallas import tpu as pltpu
from jax.sharding import PartitionSpec as P

D = 8192
FF = 14336
BLK = 128
NVAL = 4
TOK = 512
VAL = 512
AXES = ("dp", "seq")
HA = FF // 2
HG = D // 2
C1 = 3840
C2A = HA - C1
C2G = 512
C2 = C2A + C2G
C3G = HG - C2G
IDW = 128
C3 = C3G + IDW
MASKS = ((1, 3), (3, 1))


def coords(i):
    dp, seq = divmod(i, 8)
    c = dp % 2
    z = (dp // 2) % 4
    x = (seq // 4) * 2 + dp // 8
    return {"x": x, "y": seq % 4, "z": z, "c": c}


def index(p):
    dp = ((p["x"] % 2) * 4 + p["z"]) * 2 + p["c"]
    return dp * 8 + (p["x"] // 2) * 4 + p["y"]


def ring_pairs(axes, step):
    pairs = []
    for i in range(128):
        p = coords(i)
        for axis in axes:
            p[axis] ^= MASKS[p["c"]][step]
        pairs.append((i, index(p)))
    return pairs


def core_pairs():
    pairs = []
    for i in range(128):
        p = coords(i)
        p["c"] ^= 1
        pairs.append((i, index(p)))
    return pairs


def swap(x):
    return lax.ppermute(x, AXES, core_pairs())


def hop(x, axes, step):
    return lax.ppermute(x, AXES, ring_pairs(axes, step))


def double(x, axis, step):
    return jnp.stack([x, hop(x, axis, step)])


def pin(x):
    return pltpu.with_memory_space_constraint(x, pltpu.VMEM)


def gate(xs, *deps, space=pltpu.VMEM):
    n = len(xs)
    anyspec = pl.BlockSpec(memory_space=pl.ANY)
    return pl.pallas_call(
        lambda *refs: None,
        in_specs=[anyspec] * (n + len(deps)),
        out_specs=[anyspec] * n,
        out_shape=[jax.ShapeDtypeStruct(x.shape, x.dtype) for x in xs],
        input_output_aliases={i: i for i in range(n)},
        compiler_params=pltpu.CompilerParams(vmem_limit_bytes=1 << 20),
        cost_estimate=pl.CostEstimate(flops=0, bytes_accessed=0, transcendentals=0),
    )(*[pltpu.with_memory_space_constraint(x, space) for x in xs], *deps)


def nt(a, b):
    return lax.dot_general(a, b, (((1,), (1,)), ((), ())), preferred_element_type=jnp.float32)


def self_add(acc, ref):
    acc[0:256, :] += nt(ref[256:512, :], ref[0:256, :])
    acc[256:384, 0:128] += nt(ref[128:256, :], ref[0:128, :])
    acc[384:512, 0:128] += nt(ref[384:512, :], ref[256:384, :])


def self_first_body(x_ref, dep_ref, out_ref):
    @pl.when(pl.program_id(0) == 0)
    def _():
        out_ref[...] = jnp.zeros_like(out_ref)

    self_add(out_ref, x_ref)


def self_last_body(x_ref, first_ref, dep_ref, out_ref, acc, *, steps):
    i = pl.program_id(0)

    @pl.when(i == 0)
    def _():
        acc[...] = jnp.zeros_like(acc)

    self_add(acc, x_ref)

    @pl.when(i == steps - 1)
    def _():
        k = first_ref[...] * acc[...]
        rows = lax.broadcasted_iota(jnp.int32, (4, 4), 0)
        cols = lax.broadcasted_iota(jnp.int32, (4, 4), 1)
        out = jnp.zeros((4, 4), jnp.float32)
        spots = (
            (2, 0, 0, 0), (2, 1, 0, 128), (3, 0, 128, 0), (3, 1, 128, 128),
            (1, 0, 256, 0), (3, 2, 384, 0),
        )
        for b, c, r0, c0 in spots:
            s = jnp.sum(k[r0:r0 + 128, c0:c0 + 128])
            out = jnp.where((rows == b) & (cols == c), s, out)
        out_ref[...] = out / (float(BLK) * math.sqrt(float(FF) * float(D)))


KC = 2048


def self_call(x, dep, first=None):
    width = x.shape[1]
    half = pl.BlockSpec((512, 256), lambda i: (0, 0))
    anyspec = pl.BlockSpec(memory_space=pl.ANY)
    args = [x] + ([] if first is None else [first]) + [dep]
    body = self_first_body
    if first is not None:
        body = functools.partial(self_last_body, steps=width // KC)
    return pl.pallas_call(
        body,
        grid=(width // KC,),
        in_specs=[pl.BlockSpec((TOK, KC), lambda i: (0, i))]
        + ([] if first is None else [half]) + [anyspec],
        out_specs=half if first is None else pl.BlockSpec((4, 4), lambda i: (0, 0)),
        out_shape=jax.ShapeDtypeStruct((512, 256) if first is None else (4, 4), jnp.float32),
        scratch_shapes=[] if first is None else [pltpu.VMEM((512, 256), jnp.float32)],
        compiler_params=pltpu.CompilerParams(vmem_limit_bytes=16 << 20),
        cost_estimate=pl.CostEstimate(
            flops=2 * 512 * 256 * width, bytes_accessed=2 * TOK * width, transcendentals=0
        ),
    )(*args)


RUNS = ("y", "z", "x")
STEP5 = ("z", "x", "y")
STEP6 = ("x", "y", "z")
WEIGHT = {"x": 4, "y": 2, "z": 1}


def place(part, k, s4):
    n = s4 * WEIGHT[RUNS[part]]
    if k in (1, 3):
        n += WEIGHT[STEP5[part]]
    if k in (2, 3):
        n += WEIGHT[STEP6[part]]
    return n


WIDTHS = (C1, C2, C3)
STARTS = (0, C1, C1 + C2)
ALLW = C1 + C2 + C3
FULL = (
    (("a", 0, 0, C1),),
    (("a", C1, 0, C2A), ("g", 0, C2A, C2G)),
    (("g", C2G, 0, C3G),),
)
SETAT = ((0, 0, 0), (2048, 1792, 1792))
SETW = ((2048, 1792, 1792), (C1 - 2048, C2 - 1792, C3 - 1792))
SETS = (
    ((("a", 0, 0, 2048),), (("a", C1, 0, 1792),), (("g", C2G, 0, 1792),)),
    (
        (("a", 2048, 0, C1 - 2048),),
        (("a", C1 + 1792, 0, C2A - 1792), ("g", 0, C2A - 1792, C2G)),
        (("g", C2G + 1792, 0, C3G - 1792),),
    ),
)
SETMAX = 2048


class Train:
    def __init__(self, core_ref, acts, grads, half, parts, hbuf, sems):
        c = core_ref[0]
        o = c if half == 0 else 1 - c
        self.hbuf, self.todo = hbuf, []
        for part, segments in enumerate(parts):
            cps = []
            for i, (name, col, at, w) in enumerate(segments):
                src, step = (acts, HA) if name == "a" else (grads, HG)
                first = pl.multiple_of(o * step + col, 128)
                cps.append(pltpu.make_async_copy(
                    src.at[:, pl.ds(first, w)], hbuf.at[part, :, pl.ds(at, w)], sems.at[part, i]
                ))
            self.todo.append(cps)

    def go(self, part):
        for cp in self.todo[part]:
            cp.start()

    def wait(self, part):
        for cp in self.todo[part]:
            cp.wait()

    def get(self, part, at, w):
        return self.hbuf[part, :, at:at + w]


def cross_rows(part, segments, ks, pieces, train, ca, cg):
    train.wait(part)
    for name, _, at, w in segments:
        acc = ca if name == "a" else cg
        rows = [p[:, :, :, at:at + w].reshape(128, w) for p in pieces]
        x = nt(jnp.concatenate(rows, axis=0), train.get(part, at, w))
        for i, k in enumerate(ks):
            for s4 in range(2):
                r = i * 128 + s4 * 64
                acc[place(part, k, s4)] += x[r:r + 64].reshape(8, 8, TOK)


def once(cps):
    left = list(cps)

    def wait():
        while left:
            left.pop().wait()

    return wait


def val_rows(core_ref, blocks, ka, kg, name, seen, ready):
    even = jnp.concatenate([x[:32] for x in blocks], axis=0)
    late = jnp.concatenate(blocks[4:], axis=0)
    y = nt(jnp.where(core_ref[0] == 0, even, late), jnp.concatenate(blocks, axis=0))
    acc = ka if name == "a" else kg
    ready()
    if name in seen:
        acc[...] += y
    else:
        acc[...] = y
        seen.add(name)


def early_body(core_ref, acts, grads, dep_ref, *refs):
    own = [refs[p * 2:p * 2 + 2] for p in range(3)]
    ca, cg, tok, hbuf, sems = refs[6:]
    train = Train(core_ref, acts, grads, 0, FULL, hbuf, sems)
    for part in range(3):
        train.go(part)
    tok[...] = jnp.zeros_like(tok)
    ca[...] = jnp.zeros_like(ca)
    cg[...] = jnp.zeros_like(cg)
    for part in range(3):
        cross_rows(part, FULL[part], (0, 1), own[part], train, ca, cg)


def bring(moves, sems):
    cps = [pltpu.make_async_copy(x, y, sems.at[i]) for i, (x, y) in enumerate(moves)]
    for cp in cps:
        cp.start()
    return cps


def late_own_body(core_ref, acts, grads, *refs, which):
    pieces = [refs[p * 3:p * 3 + 3] for p in range(3)]
    n = 2 + 2 * which
    ins, refs = refs[9:9 + n], refs[9 + n:]
    ca, cg, ka, kg = refs[:4]
    if which:
        ids = refs[4]
    hbuf, sems, pbuf, psems, asems = refs[4 + which:]
    train = Train(core_ref, acts, grads, 0, SETS[which], hbuf, sems)
    todo = []
    for part in range(3):
        x, a1, last = pieces[part]
        w = SETW[which][part]
        cols = pl.ds(SETAT[which][part], w)
        srcs = (x.at[:, :, :, cols], a1.at[:, :, :, cols], last.at[0], last.at[1])
        todo.append(bring(
            [(src, pbuf.at[part, k, :, :, :, pl.ds(0, w)]) for k, src in enumerate(srcs)],
            psems.at[part],
        ))
        train.go(part)
        if part == 0:
            ready = once(bring(list(zip(ins, (ca, cg, ka, kg))), asems))
    seen = {"a", "g"} if which else set()
    for part in range(3):
        for cp in todo[part]:
            cp.wait()

        def blocks(at, w):
            out = [None] * 8
            for k in range(4):
                for s4 in range(2):
                    out[place(part, k, s4)] = pbuf[part, k, s4, :, :, at:at + w].reshape(64, w)
            return out

        for name, _, at, w in SETS[which][part]:
            val_rows(core_ref, blocks(at, w), ka, kg, name, seen, ready)
        if which and part == 2:
            for b, x in enumerate(blocks(SETW[1][2] - IDW, IDW)):
                ids[b * 64:b * 64 + 64, :] = x.astype(jnp.float32)
        cross_rows(
            part, SETS[which][part], (2, 3), [pbuf.at[part, 2], pbuf.at[part, 3]], train, ca, cg
        )


def late_other_body(core_ref, acts, grads, o0, o1, o2, o3, o4, ain, gin, k1, k2, *refs, which):
    c = core_ref[0]
    lasts = (o2, o3, o4)
    if which:
        idin, raw_ref, norm_ref, hbuf, sems, vbuf, acc_a, acc_g, ka, kg, ids, vsems, asems = refs
        extra = [(idin, ids)]
    else:
        acc_a, acc_g, ka, kg, tok, hbuf, sems, vbuf, vsems, asems = refs
        tok[...] = jnp.zeros_like(tok)
        extra = []
    train = Train(core_ref, acts, grads, 1, SETS[which], hbuf, sems)
    todo = []
    for part in range(3):
        w = SETW[which][part]
        cols = pl.ds(STARTS[part] + SETAT[which][part], w)
        first = 0 if which else sum(SETW[0][:part])
        todo.append(bring(
            [
                (
                    o.at[s4, :, :, cols] if k < 2 else o.at[s4, :, :, pl.ds(first, w)],
                    vbuf.at[part, :, place(part, k, s4), :, pl.ds(0, w)],
                )
                for k, o in enumerate((o0, o1, lasts[part].at[0], lasts[part].at[1]))
                for s4 in range(2)
            ],
            vsems.at[part],
        ))
        train.go(part)
        if part == 0:
            sums = [(ain, acc_a), (gin, acc_g), (k1, ka), (k2, kg)] + extra
            ready = once(bring(sums, asems))
    seen = {"a", "g"}
    for part in range(3):
        for cp in todo[part]:
            cp.wait()
        for name, _, at, w in SETS[which][part]:
            blocks = [vbuf[part, b, :, :, at:at + w].reshape(64, w) for b in range(8)]
            val_rows(core_ref, blocks, ka, kg, name, seen, ready)
        train.wait(part)
        for name, _, at, w in SETS[which][part]:
            acc = acc_a if name == "a" else acc_g
            rows = vbuf[part, :, :, :, at:at + w].reshape(VAL, w)
            acc[...] += nt(rows, train.get(part, at, w)).reshape(8, 8, 8, TOK)
    if not which:
        return

    cross = acc_a[...].reshape(VAL, TOK) * acc_g[...].reshape(VAL, TOK)
    kern = ka[...] * kg[...]
    all_ids = ids[...]
    row_ids = jnp.transpose(all_ids)[0:1, :]
    even = jnp.concatenate([all_ids[b * 64:b * 64 + 32] for b in range(8)], axis=0)
    half_ids = jnp.where(c == 0, even, all_ids[256:512])
    for v in range(NVAL):
        keep = jnp.where(all_ids == float(v), 1.0, 0.0)
        keep = jnp.concatenate([keep] * 4, axis=1)
        raw_ref[v:v + 1, :] = jnp.sum(cross * keep, axis=0, keepdims=True)
        keep = jnp.where(half_ids == float(v), 1.0, 0.0)
        keep = jnp.concatenate([keep] * 4, axis=1)
        part = jnp.sum(kern * keep, axis=0, keepdims=True)
        part = jnp.sum(jnp.where(row_ids == float(v), part, 0.0))
        norm_ref[v:v + 1, :] = jnp.full((1, 128), part, jnp.float32)


ACC = jax.ShapeDtypeStruct((8, 8, 8, TOK), jnp.float32)
KERN = jax.ShapeDtypeStruct((VAL // 2, VAL), jnp.float32)


TOKEN = jax.ShapeDtypeStruct((8, 128), jnp.float32)
IDS = jax.ShapeDtypeStruct((VAL, IDW), jnp.float32)


def local_call(body, core, acts, grads, args, outs, flops, width, scratch=(), pinned=(), mib=26):
    vmem = pl.BlockSpec(memory_space=pltpu.VMEM)
    anyspec = pl.BlockSpec(memory_space=pl.ANY)
    return pl.pallas_call(
        body,
        in_specs=[pl.BlockSpec(memory_space=pltpu.SMEM)] + [anyspec] * 2
        + [vmem if i in pinned else anyspec for i in range(len(args))],
        out_specs=[vmem] * len(outs),
        out_shape=outs,
        scratch_shapes=[
            pltpu.VMEM((3, TOK, width), jnp.bfloat16),
            pltpu.SemaphoreType.DMA((3, 2)),
        ] + list(scratch),
        compiler_params=pltpu.CompilerParams(vmem_limit_bytes=mib << 20),
        cost_estimate=pl.CostEstimate(
            flops=flops, bytes_accessed=TOK * (FF + D) if flops else 0, transcendentals=0
        ),
    )(core, acts, grads, *[pin(x) if i in pinned else x for i, x in enumerate(args)])


def prepare_body(core_ref, ids_in, acts_in, grads_in, keep_ref, away_ref, ids_ref, acts_ref, grads_ref, sems):
    moves = bring([(acts_in, acts_ref), (grads_in, grads_ref), (ids_in, ids_ref)], sems)
    for cp in moves:
        cp.wait()
    first = core_ref[0] == 0
    for at, ref, w in ((0, acts_ref, HA), (HA, grads_ref, HG)):
        low, high = ref[:, 0:w], ref[:, w:2 * w]
        keep_ref[:, at:at + w] = jnp.where(first, low, high)
        away_ref[:, at:at + w] = jnp.where(first, high, low)
    row = lax.broadcasted_iota(jnp.int32, (4, IDW), 0)
    ids = jnp.zeros((4, IDW), jnp.float32)
    for r in range(4):
        ids = jnp.where(row == r, ids_ref[r].astype(jnp.float32), ids)
    keep_ref[:, HA + HG:] = ids.astype(jnp.bfloat16)
    away_ref[:, HA + HG:] = ids.astype(jnp.bfloat16)


def prepare(core, val_acts, val_grads, val_ids):
    vmem = pl.BlockSpec(memory_space=pltpu.VMEM)
    smem = pl.BlockSpec(memory_space=pltpu.SMEM)
    return pl.pallas_call(
        prepare_body,
        in_specs=[smem] + [pl.BlockSpec(memory_space=pl.ANY)] * 3,
        out_specs=[vmem, vmem],
        out_shape=[jax.ShapeDtypeStruct((4, ALLW), jnp.bfloat16)] * 2,
        scratch_shapes=[
            pltpu.SMEM((4,), jnp.int32),
            pltpu.VMEM((4, FF), jnp.bfloat16),
            pltpu.VMEM((4, D), jnp.bfloat16),
            pltpu.SemaphoreType.DMA((3,)),
        ],
        compiler_params=pltpu.CompilerParams(vmem_limit_bytes=4 << 20),
        cost_estimate=pl.CostEstimate(flops=0, bytes_accessed=720896, transcendentals=0),
    )(core, *[
        pltpu.with_memory_space_constraint(x, pltpu.HBM) for x in (val_ids, val_acts, val_grads)
    ])


def shards(hidden_acts, out_grads, val_acts, val_grads, val_ids):
    hidden_acts = pltpu.with_memory_space_constraint(hidden_acts, pltpu.HBM)
    out_grads = pltpu.with_memory_space_constraint(out_grads, pltpu.HBM)
    core = lax.axis_index("dp") % 2
    first = core == 0
    core = core.reshape(1).astype(jnp.int32)
    keep, away = prepare(core, val_acts, val_grads, val_ids)
    got = swap(away)
    rows = jnp.concatenate([jnp.where(first, keep, got), jnp.where(first, got, keep)], axis=0)

    def send(block, n):
        return hop(block, [a for a in "xyz" if n & WEIGHT[a]], 0)

    rows = jnp.stack([rows] + [send(rows, n) for n in (1, 2, 3)])
    sg = self_call(out_grads, rows)
    (rows,) = gate([jnp.concatenate([rows, send(rows, 4)], axis=0)], sg)
    x = [double(rows[..., s:s + w], RUNS[j], 1) for j, (s, w) in enumerate(zip(STARTS, WIDTHS))]
    block_gram = self_call(hidden_acts, x[1], sg)
    a1 = [hop(x[j], STEP5[j], 1) for j in range(3)]
    o0 = swap(jnp.concatenate(x, axis=-1))
    pair = gate([jnp.stack([x[j], a1[j]]) for j in range(3)], block_gram, o0)
    cut = [
        [pair[j][..., a:a + w] for j, (a, w) in enumerate(zip(at, width))]
        for at, width in zip(SETAT, SETW)
    ]
    last = [[hop(y, STEP6[j], 1) for j, y in enumerate(cut[0])]]
    o1 = swap(gate([jnp.concatenate(a1, axis=-1)], pair[0])[0])
    call = functools.partial(
        local_call, core=core, acts=hidden_acts, grads=out_grads
    )
    unit = 512 * (HA + HG)
    ca, cg, tok = call(
        early_body, args=[block_gram] + [y for j in range(3) for y in (x[j], a1[j])],
        outs=[ACC, ACC, TOKEN], flops=512 * unit, width=C1, pinned=range(1, 7), mib=28,
    )
    last.append([hop(y, STEP6[j], 1) for j, y in enumerate(cut[1])])
    sums = [ca, cg]
    for which in range(2):
        got = last[which]
        if which:
            got = [gate([y], tok)[0] for y in got]
            swapped = [swap(y) for y in got]
        else:
            swapped = [swap(gate([jnp.concatenate(got, axis=-1)], tok, o1)[0])] * 3
        sums = call(
            functools.partial(late_own_body, which=which),
            args=[y for j in range(3) for y in (x[j], a1[j], got[j])] + list(sums),
            outs=[ACC, ACC, KERN, KERN] + [IDS] * which, flops=512 * unit * which, width=SETMAX,
            scratch=[
                pltpu.VMEM((3, 4, 2, 8, 8, SETMAX), jnp.bfloat16),
                pltpu.SemaphoreType.DMA((3, 4)),
                pltpu.SemaphoreType.DMA((4,)),
            ],
        )
        outs = [ACC, ACC, KERN, KERN, TOKEN]
        scratch = [pltpu.VMEM((3, 8, 8, 8, SETMAX), jnp.bfloat16)]
        if which:
            outs = [
                jax.ShapeDtypeStruct((NVAL, TOK), jnp.float32),
                jax.ShapeDtypeStruct((NVAL, 128), jnp.float32),
            ]
            scratch += [pltpu.VMEM(a.shape, a.dtype) for a in (ACC, ACC, KERN, KERN, IDS)]
        outs = call(
            functools.partial(late_other_body, which=which),
            args=[o0, o1] + swapped + list(sums), outs=outs, flops=768 * unit * which, width=SETMAX,
            scratch=scratch + [
                pltpu.SemaphoreType.DMA((3, 8)),
                pltpu.SemaphoreType.DMA((5,)),
            ],
        )
        sums, tok = outs[:4], outs[-1]
    raw, norm = outs
    norm = norm + swap(norm)
    token_scores = raw * lax.rsqrt(norm[:, :1] + 1e-06)
    return (token_scores, block_gram)


def solution(mesh):
    return jax.shard_map(
        shards,
        mesh=mesh,
        in_specs=(
            P(AXES, None),
            P(AXES, None),
            P(AXES, None),
            P(AXES, None),
            P(AXES),
        ),
        out_specs=(P(None, AXES), P(AXES, None)),
        check_vma=False,
    )
```

```python
import functools
import math

import jax
import jax.numpy as jnp
from jax import lax
from jax.experimental import pallas as pl
from jax.experimental.pallas import tpu as pltpu
from jax.sharding import PartitionSpec as P

D = 8192
FF = 14336
BLK = 128
NVAL = 4
TOK = 512
VAL = 512
AXES = ("dp", "seq")
HA = FF // 2
HG = D // 2
C1 = 3840
C2A = HA - C1
C2G = 512
C2 = C2A + C2G
C3G = HG - C2G
IDW = 128
C3 = C3G + IDW
MASKS = ((1, 3), (3, 1))


def coords(i):
    dp, seq = divmod(i, 8)
    c = dp % 2
    z = (dp // 2) % 4
    x = (seq // 4) * 2 + dp // 8
    return {"x": x, "y": seq % 4, "z": z, "c": c}


def index(p):
    dp = ((p["x"] % 2) * 4 + p["z"]) * 2 + p["c"]
    return dp * 8 + (p["x"] // 2) * 4 + p["y"]


def ring_pairs(axes, step):
    pairs = []
    for i in range(128):
        p = coords(i)
        for axis in axes:
            p[axis] ^= MASKS[p["c"]][step]
        pairs.append((i, index(p)))
    return pairs


def core_pairs():
    pairs = []
    for i in range(128):
        p = coords(i)
        p["c"] ^= 1
        pairs.append((i, index(p)))
    return pairs


def swap(x):
    return lax.ppermute(x, AXES, core_pairs())


def hop(x, axes, step):
    return lax.ppermute(x, AXES, ring_pairs(axes, step))


def double(x, axis, step):
    return jnp.stack([x, hop(x, axis, step)])


def pin(x):
    return pltpu.with_memory_space_constraint(x, pltpu.VMEM)


def gate(xs, *deps, space=pltpu.VMEM):
    n = len(xs)
    anyspec = pl.BlockSpec(memory_space=pl.ANY)
    return pl.pallas_call(
        lambda *refs: None,
        in_specs=[anyspec] * (n + len(deps)),
        out_specs=[anyspec] * n,
        out_shape=[jax.ShapeDtypeStruct(x.shape, x.dtype) for x in xs],
        input_output_aliases={i: i for i in range(n)},
        compiler_params=pltpu.CompilerParams(vmem_limit_bytes=1 << 20),
        cost_estimate=pl.CostEstimate(flops=0, bytes_accessed=0, transcendentals=0),
    )(*[pltpu.with_memory_space_constraint(x, space) for x in xs], *deps)


def nt(a, b):
    return lax.dot_general(a, b, (((1,), (1,)), ((), ())), preferred_element_type=jnp.float32)


def self_add(acc, ref):
    acc[0:256, :] += nt(ref[256:512, :], ref[0:256, :])
    acc[256:384, 0:128] += nt(ref[128:256, :], ref[0:128, :])
    acc[384:512, 0:128] += nt(ref[384:512, :], ref[256:384, :])


def self_first_body(x_ref, dep_ref, out_ref):
    @pl.when(pl.program_id(0) == 0)
    def _():
        out_ref[...] = jnp.zeros_like(out_ref)

    self_add(out_ref, x_ref)


def self_last_body(x_ref, first_ref, dep_ref, out_ref, acc, *, steps):
    i = pl.program_id(0)

    @pl.when(i == 0)
    def _():
        acc[...] = jnp.zeros_like(acc)

    self_add(acc, x_ref)

    @pl.when(i == steps - 1)
    def _():
        k = first_ref[...] * acc[...]
        rows = lax.broadcasted_iota(jnp.int32, (4, 4), 0)
        cols = lax.broadcasted_iota(jnp.int32, (4, 4), 1)
        out = jnp.zeros((4, 4), jnp.float32)
        spots = (
            (2, 0, 0, 0), (2, 1, 0, 128), (3, 0, 128, 0), (3, 1, 128, 128),
            (1, 0, 256, 0), (3, 2, 384, 0),
        )
        for b, c, r0, c0 in spots:
            s = jnp.sum(k[r0:r0 + 128, c0:c0 + 128])
            out = jnp.where((rows == b) & (cols == c), s, out)
        out_ref[...] = out / (float(BLK) * math.sqrt(float(FF) * float(D)))


KC = 2048


def self_call(x, dep, first=None):
    width = x.shape[1]
    half = pl.BlockSpec((512, 256), lambda i: (0, 0))
    anyspec = pl.BlockSpec(memory_space=pl.ANY)
    args = [x] + ([] if first is None else [first]) + [dep]
    body = self_first_body
    if first is not None:
        body = functools.partial(self_last_body, steps=width // KC)
    return pl.pallas_call(
        body,
        grid=(width // KC,),
        in_specs=[pl.BlockSpec((TOK, KC), lambda i: (0, i))]
        + ([] if first is None else [half]) + [anyspec],
        out_specs=half if first is None else pl.BlockSpec((4, 4), lambda i: (0, 0)),
        out_shape=jax.ShapeDtypeStruct((512, 256) if first is None else (4, 4), jnp.float32),
        scratch_shapes=[] if first is None else [pltpu.VMEM((512, 256), jnp.float32)],
        compiler_params=pltpu.CompilerParams(vmem_limit_bytes=16 << 20),
        cost_estimate=pl.CostEstimate(
            flops=2 * 512 * 256 * width, bytes_accessed=2 * TOK * width, transcendentals=0
        ),
    )(*args)


RUNS = ("y", "z", "x")
STEP5 = ("z", "x", "y")
STEP6 = ("x", "y", "z")
WEIGHT = {"x": 4, "y": 2, "z": 1}


def place(part, k, s4):
    n = s4 * WEIGHT[RUNS[part]]
    if k in (1, 3):
        n += WEIGHT[STEP5[part]]
    if k in (2, 3):
        n += WEIGHT[STEP6[part]]
    return n


WIDTHS = (C1, C2, C3)
STARTS = (0, C1, C1 + C2)
ALLW = C1 + C2 + C3
FULL = (
    (("a", 0, 0, C1),),
    (("a", C1, 0, C2A), ("g", 0, C2A, C2G)),
    (("g", C2G, 0, C3G),),
)
SETAT = ((0, 0, 0), (1792, 1792, 1792))
SETW = ((1792, 1792, 1792), (C1 - 1792, C2 - 1792, C3 - 1792))
SETS = (
    ((("a", 0, 0, 1792),), (("a", C1, 0, 1792),), (("g", C2G, 0, 1792),)),
    (
        (("a", 1792, 0, C1 - 1792),),
        (("a", C1 + 1792, 0, C2A - 1792), ("g", 0, C2A - 1792, C2G)),
        (("g", C2G + 1792, 0, C3G - 1792),),
    ),
)
SETMAX = 2048


class Train:
    def __init__(self, core_ref, acts, grads, half, parts, hbuf, sems):
        c = core_ref[0]
        o = c if half == 0 else 1 - c
        self.hbuf, self.todo = hbuf, []
        for part, segments in enumerate(parts):
            cps = []
            for i, (name, col, at, w) in enumerate(segments):
                src, step = (acts, HA) if name == "a" else (grads, HG)
                first = pl.multiple_of(o * step + col, 128)
                cps.append(pltpu.make_async_copy(
                    src.at[:, pl.ds(first, w)], hbuf.at[part, :, pl.ds(at, w)], sems.at[part, i]
                ))
            self.todo.append(cps)

    def go(self, part):
        for cp in self.todo[part]:
            cp.start()

    def wait(self, part):
        for cp in self.todo[part]:
            cp.wait()

    def get(self, part, at, w):
        return self.hbuf[part, :, at:at + w]


def cross_rows(part, segments, ks, pieces, train, ca, cg):
    train.wait(part)
    for name, _, at, w in segments:
        acc = ca if name == "a" else cg
        rows = [p[:, :, :, at:at + w].reshape(128, w) for p in pieces]
        x = nt(jnp.concatenate(rows, axis=0), train.get(part, at, w))
        for i, k in enumerate(ks):
            for s4 in range(2):
                r = i * 128 + s4 * 64
                acc[place(part, k, s4)] += x[r:r + 64].reshape(8, 8, TOK)


def once(cps):
    left = list(cps)

    def wait():
        while left:
            left.pop().wait()

    return wait


def val_rows(core_ref, blocks, ka, kg, name, seen, ready):
    even = jnp.concatenate([x[:32] for x in blocks], axis=0)
    late = jnp.concatenate(blocks[4:], axis=0)
    y = nt(jnp.where(core_ref[0] == 0, even, late), jnp.concatenate(blocks, axis=0))
    acc = ka if name == "a" else kg
    ready()
    if name in seen:
        acc[...] += y
    else:
        acc[...] = y
        seen.add(name)


def early_body(core_ref, acts, grads, dep_ref, *refs):
    own = [refs[p * 2:p * 2 + 2] for p in range(3)]
    ca, cg, tok, hbuf, sems = refs[6:]
    train = Train(core_ref, acts, grads, 0, FULL, hbuf, sems)
    for part in range(3):
        train.go(part)
    tok[...] = jnp.zeros_like(tok)
    ca[...] = jnp.zeros_like(ca)
    cg[...] = jnp.zeros_like(cg)
    for part in range(3):
        cross_rows(part, FULL[part], (0, 1), own[part], train, ca, cg)


def bring(moves, sems):
    cps = [pltpu.make_async_copy(x, y, sems.at[i]) for i, (x, y) in enumerate(moves)]
    for cp in cps:
        cp.start()
    return cps


def late_own_body(core_ref, acts, grads, *refs, which):
    pieces = [refs[p * 3:p * 3 + 3] for p in range(3)]
    n = 2 + 2 * which
    ins, refs = refs[9:9 + n], refs[9 + n:]
    ca, cg, ka, kg = refs[:4]
    if which:
        ids = refs[4]
    hbuf, sems, pbuf, psems, asems = refs[4 + which:]
    train = Train(core_ref, acts, grads, 0, SETS[which], hbuf, sems)
    todo = []
    for part in range(3):
        x, a1, last = pieces[part]
        w = SETW[which][part]
        cols = pl.ds(SETAT[which][part], w)
        srcs = (x.at[:, :, :, cols], a1.at[:, :, :, cols], last.at[0], last.at[1])
        todo.append(bring(
            [(src, pbuf.at[part, k, :, :, :, pl.ds(0, w)]) for k, src in enumerate(srcs)],
            psems.at[part],
        ))
        train.go(part)
        if part == 0:
            ready = once(bring(list(zip(ins, (ca, cg, ka, kg))), asems))
    seen = {"a", "g"} if which else set()
    for part in range(3):
        for cp in todo[part]:
            cp.wait()

        def blocks(at, w):
            out = [None] * 8
            for k in range(4):
                for s4 in range(2):
                    out[place(part, k, s4)] = pbuf[part, k, s4, :, :, at:at + w].reshape(64, w)
            return out

        for name, _, at, w in SETS[which][part]:
            val_rows(core_ref, blocks(at, w), ka, kg, name, seen, ready)
        if which and part == 2:
            for b, x in enumerate(blocks(SETW[1][2] - IDW, IDW)):
                ids[b * 64:b * 64 + 64, :] = x.astype(jnp.float32)
        cross_rows(
            part, SETS[which][part], (2, 3), [pbuf.at[part, 2], pbuf.at[part, 3]], train, ca, cg
        )


def late_other_body(core_ref, acts, grads, o0, o1, o2, o3, o4, ain, gin, k1, k2, *refs, which):
    c = core_ref[0]
    lasts = (o2, o3, o4)
    if which:
        idin, raw_ref, norm_ref, hbuf, sems, vbuf, acc_a, acc_g, ka, kg, ids, vsems, asems = refs
        extra = [(idin, ids)]
    else:
        acc_a, acc_g, ka, kg, tok, hbuf, sems, vbuf, vsems, asems = refs
        tok[...] = jnp.zeros_like(tok)
        extra = []
    train = Train(core_ref, acts, grads, 1, SETS[which], hbuf, sems)
    todo = []
    for part in range(3):
        w = SETW[which][part]
        cols = pl.ds(STARTS[part] + SETAT[which][part], w)
        first = 0 if which else sum(SETW[0][:part])
        todo.append(bring(
            [
                (
                    o.at[s4, :, :, cols] if k < 2 else o.at[s4, :, :, pl.ds(first, w)],
                    vbuf.at[part, :, place(part, k, s4), :, pl.ds(0, w)],
                )
                for k, o in enumerate((o0, o1, lasts[part].at[0], lasts[part].at[1]))
                for s4 in range(2)
            ],
            vsems.at[part],
        ))
        train.go(part)
        if part == 0:
            sums = [(ain, acc_a), (gin, acc_g), (k1, ka), (k2, kg)] + extra
            ready = once(bring(sums, asems))
    seen = {"a", "g"}
    for part in range(3):
        for cp in todo[part]:
            cp.wait()
        for name, _, at, w in SETS[which][part]:
            blocks = [vbuf[part, b, :, :, at:at + w].reshape(64, w) for b in range(8)]
            val_rows(core_ref, blocks, ka, kg, name, seen, ready)
        train.wait(part)
        for name, _, at, w in SETS[which][part]:
            acc = acc_a if name == "a" else acc_g
            rows = vbuf[part, :, :, :, at:at + w].reshape(VAL, w)
            acc[...] += nt(rows, train.get(part, at, w)).reshape(8, 8, 8, TOK)
    if not which:
        return

    cross = acc_a[...].reshape(VAL, TOK) * acc_g[...].reshape(VAL, TOK)
    kern = ka[...] * kg[...]
    all_ids = ids[...]
    row_ids = jnp.transpose(all_ids)[0:1, :]
    even = jnp.concatenate([all_ids[b * 64:b * 64 + 32] for b in range(8)], axis=0)
    half_ids = jnp.where(c == 0, even, all_ids[256:512])
    for v in range(NVAL):
        keep = jnp.where(all_ids == float(v), 1.0, 0.0)
        keep = jnp.concatenate([keep] * 4, axis=1)
        raw_ref[v:v + 1, :] = jnp.sum(cross * keep, axis=0, keepdims=True)
        keep = jnp.where(half_ids == float(v), 1.0, 0.0)
        keep = jnp.concatenate([keep] * 4, axis=1)
        part = jnp.sum(kern * keep, axis=0, keepdims=True)
        part = jnp.sum(jnp.where(row_ids == float(v), part, 0.0))
        norm_ref[v:v + 1, :] = jnp.full((1, 128), part, jnp.float32)


ACC = jax.ShapeDtypeStruct((8, 8, 8, TOK), jnp.float32)
KERN = jax.ShapeDtypeStruct((VAL // 2, VAL), jnp.float32)


TOKEN = jax.ShapeDtypeStruct((8, 128), jnp.float32)
IDS = jax.ShapeDtypeStruct((VAL, IDW), jnp.float32)


def local_call(body, core, acts, grads, args, outs, flops, width, scratch=(), pinned=(), mib=26):
    vmem = pl.BlockSpec(memory_space=pltpu.VMEM)
    anyspec = pl.BlockSpec(memory_space=pl.ANY)
    return pl.pallas_call(
        body,
        in_specs=[pl.BlockSpec(memory_space=pltpu.SMEM)] + [anyspec] * 2
        + [vmem if i in pinned else anyspec for i in range(len(args))],
        out_specs=[vmem] * len(outs),
        out_shape=outs,
        scratch_shapes=[
            pltpu.VMEM((3, TOK, width), jnp.bfloat16),
            pltpu.SemaphoreType.DMA((3, 2)),
        ] + list(scratch),
        compiler_params=pltpu.CompilerParams(vmem_limit_bytes=mib << 20),
        cost_estimate=pl.CostEstimate(
            flops=flops, bytes_accessed=TOK * (FF + D) if flops else 0, transcendentals=0
        ),
    )(core, acts, grads, *[pin(x) if i in pinned else x for i, x in enumerate(args)])


def prepare_body(core_ref, ids_in, acts_in, grads_in, keep_ref, away_ref, ids_ref, acts_ref, grads_ref, sems):
    moves = bring([(acts_in, acts_ref), (grads_in, grads_ref), (ids_in, ids_ref)], sems)
    for cp in moves:
        cp.wait()
    first = core_ref[0] == 0
    for at, ref, w in ((0, acts_ref, HA), (HA, grads_ref, HG)):
        low, high = ref[:, 0:w], ref[:, w:2 * w]
        keep_ref[:, at:at + w] = jnp.where(first, low, high)
        away_ref[:, at:at + w] = jnp.where(first, high, low)
    row = lax.broadcasted_iota(jnp.int32, (4, IDW), 0)
    ids = jnp.zeros((4, IDW), jnp.float32)
    for r in range(4):
        ids = jnp.where(row == r, ids_ref[r].astype(jnp.float32), ids)
    keep_ref[:, HA + HG:] = ids.astype(jnp.bfloat16)
    away_ref[:, HA + HG:] = ids.astype(jnp.bfloat16)


def prepare(core, val_acts, val_grads, val_ids):
    vmem = pl.BlockSpec(memory_space=pltpu.VMEM)
    smem = pl.BlockSpec(memory_space=pltpu.SMEM)
    return pl.pallas_call(
        prepare_body,
        in_specs=[smem] + [pl.BlockSpec(memory_space=pl.ANY)] * 3,
        out_specs=[vmem, vmem],
        out_shape=[jax.ShapeDtypeStruct((4, ALLW), jnp.bfloat16)] * 2,
        scratch_shapes=[
            pltpu.SMEM((4,), jnp.int32),
            pltpu.VMEM((4, FF), jnp.bfloat16),
            pltpu.VMEM((4, D), jnp.bfloat16),
            pltpu.SemaphoreType.DMA((3,)),
        ],
        compiler_params=pltpu.CompilerParams(vmem_limit_bytes=4 << 20),
        cost_estimate=pl.CostEstimate(flops=0, bytes_accessed=720896, transcendentals=0),
    )(core, *[
        pltpu.with_memory_space_constraint(x, pltpu.HBM) for x in (val_ids, val_acts, val_grads)
    ])


def shards(hidden_acts, out_grads, val_acts, val_grads, val_ids):
    hidden_acts = pltpu.with_memory_space_constraint(hidden_acts, pltpu.HBM)
    out_grads = pltpu.with_memory_space_constraint(out_grads, pltpu.HBM)
    core = lax.axis_index("dp") % 2
    first = core == 0
    core = core.reshape(1).astype(jnp.int32)
    keep, away = prepare(core, val_acts, val_grads, val_ids)
    got = swap(away)
    rows = jnp.concatenate([jnp.where(first, keep, got), jnp.where(first, got, keep)], axis=0)

    def send(block, n):
        return hop(block, [a for a in "xyz" if n & WEIGHT[a]], 0)

    rows = jnp.stack([rows] + [send(rows, n) for n in (1, 2, 3)])
    sg = self_call(out_grads, rows)
    (rows,) = gate([jnp.concatenate([rows, send(rows, 4)], axis=0)], sg)
    x = [double(rows[..., s:s + w], RUNS[j], 1) for j, (s, w) in enumerate(zip(STARTS, WIDTHS))]
    block_gram = self_call(hidden_acts, x[1], sg)
    a1 = [hop(x[j], STEP5[j], 1) for j in range(3)]
    o0 = swap(jnp.concatenate(x, axis=-1))
    pair = gate([jnp.stack([x[j], a1[j]]) for j in range(3)], block_gram, o0)
    cut = [
        [pair[j][..., a:a + w] for j, (a, w) in enumerate(zip(at, width))]
        for at, width in zip(SETAT, SETW)
    ]
    last = [[hop(y, STEP6[j], 1) for j, y in enumerate(cut[0])]]
    o1 = swap(gate([jnp.concatenate(a1, axis=-1)], pair[0])[0])
    call = functools.partial(
        local_call, core=core, acts=hidden_acts, grads=out_grads
    )
    unit = 512 * (HA + HG)
    ca, cg, tok = call(
        early_body, args=[block_gram] + [y for j in range(3) for y in (x[j], a1[j])],
        outs=[ACC, ACC, TOKEN], flops=512 * unit, width=C1, pinned=range(1, 7), mib=28,
    )
    last.append([hop(y, STEP6[j], 1) for j, y in enumerate(cut[1])])
    sums = [ca, cg]
    for which in range(2):
        got = last[which]
        if which:
            got = [gate([y], tok)[0] for y in got]
            swapped = [swap(y) for y in got]
        else:
            swapped = [swap(gate([jnp.concatenate(got, axis=-1)], tok, o1)[0])] * 3
        sums = call(
            functools.partial(late_own_body, which=which),
            args=[y for j in range(3) for y in (x[j], a1[j], got[j])] + list(sums),
            outs=[ACC, ACC, KERN, KERN] + [IDS] * which, flops=512 * unit * which, width=SETMAX,
            scratch=[
                pltpu.VMEM((3, 4, 2, 8, 8, SETMAX), jnp.bfloat16),
                pltpu.SemaphoreType.DMA((3, 4)),
                pltpu.SemaphoreType.DMA((4,)),
            ],
        )
        outs = [ACC, ACC, KERN, KERN, TOKEN]
        scratch = [pltpu.VMEM((3, 8, 8, 8, SETMAX), jnp.bfloat16)]
        if which:
            outs = [
                jax.ShapeDtypeStruct((NVAL, TOK), jnp.float32),
                jax.ShapeDtypeStruct((NVAL, 128), jnp.float32),
            ]
            scratch += [pltpu.VMEM(a.shape, a.dtype) for a in (ACC, ACC, KERN, KERN, IDS)]
        outs = call(
            functools.partial(late_other_body, which=which),
            args=[o0, o1] + swapped + list(sums), outs=outs, flops=768 * unit * which, width=SETMAX,
            scratch=scratch + [
                pltpu.SemaphoreType.DMA((3, 8)),
                pltpu.SemaphoreType.DMA((5,)),
            ],
        )
        sums, tok = outs[:4], outs[-1]
    raw, norm = outs
    norm = norm + swap(norm)
    token_scores = raw * lax.rsqrt(norm[:, :1] + 1e-06)
    return (token_scores, block_gram)


def solution(mesh):
    return jax.shard_map(
        shards,
        mesh=mesh,
        in_specs=(
            P(AXES, None),
            P(AXES, None),
            P(AXES, None),
            P(AXES, None),
            P(AXES),
        ),
        out_specs=(P(None, AXES), P(AXES, None)),
        check_vma=False,
    )
```
